256 devices in a mesh: section: 8 (over y, x_lo), replica: 32 (over z, x_hi, core).
Axes of the slice: x: 4 (x_hi: 2, x_lo: 2; x = x_hi * 2 + x_lo), y: 4, z: 8, core: 2. Of those that a mesh axis runs over, the one named last changes fastest.
Arguments:
- master_old: float32 [16, 2048, 2048], P('section', 'replica'), may hold values from -0.125 to 0.125
- first_moment_old: float32 [16, 2048, 2048], P('section', 'replica'), may hold values from -180 to 180
- second_moment_old: float32 [16, 2048, 2048], P('section', 'replica'), may hold values from 100 to 10000
- layer_vectors: bfloat16 [16, 3, 2048], P('section'), may hold values from -1.5 to 1.5, as said below
- new_section: int32 [16], P('section'), may hold values from -1 to 7, as said below
- frozen: int32 [8], replicated, may hold values 0 or 1
- window_input: bfloat16 [8192, 2048], P('replica'), may hold values from -6 to 6
- cotangent: bfloat16 [8192, 2048], P('replica'), may hold values from -6 to 6
Outputs:
- master_new: float32 [8, 2048, 2048], P('section', 'replica')
- first_moment_new: float32 [8, 2048, 2048], P('section', 'replica')
- second_moment_new: float32 [8, 2048, 2048], P('section', 'replica')
The draws below stay inside these ranges and needn't reach their ends.
Inputs may be any that keep to these rules, and one draw needn't show every extreme that they name: `new_section`: every section holds exactly one layer, in one of its 2 slots; the other slots hold -1. Every new section 0 to 7 is named once. A layer's new section differs from its old section by at most 1; in every draw the layer of section 0 moves to section 1 and the layer of section 7 moves to section 6. `layer_vectors`: row 0 of a slot is the projection's bias, row 1 the norm's gain (0.5 to 1.5), row 2 the norm's shift.
All inputs are finite; a program needn't handle non-finite values.
Results may differ from the reference program's by a relative error of at most 0.0044.
Values may be sent and summed in bfloat16 or wider, within the bound.
No kernel may reach another device: no remote copies, remote signals or barrier semaphores. Data moves between devices by JAX's collectives and lax.ppermute only.
A program may use at most 128 MiB of HBM per device.

```python
import math
import jax
import jax.numpy as jnp
from jax import lax

D = 2048
SLOTS = 2
TOK_DEV = 256
TOKENS = 8192
OLD_SLOTS = 16
N_SECTION = 8
N_REPLICA = 32


def draw_layer_vectors(key, part):
    key = jax.random.fold_in(key, 23)
    bias_key = jax.random.fold_in(key, 1)
    gain_key = jax.random.fold_in(key, 2)
    shift_key = jax.random.fold_in(key, 3)
    bias_rows = 0.5 * jax.random.truncated_normal(bias_key, -3.0, 3.0, (OLD_SLOTS, 1, D), jnp.float32)
    shift_rows = 0.5 * jax.random.truncated_normal(shift_key, -3.0, 3.0, (OLD_SLOTS, 1, D), jnp.float32)
    gain_rows = jax.random.uniform(gain_key, (OLD_SLOTS, 1, D), jnp.float32, 0.5, 1.5)
    return jnp.concatenate([bias_rows, gain_rows, shift_rows], axis=1).astype(jnp.bfloat16)


def draw_new_section(key, part):
    key = jax.random.fold_in(key, 7)
    pair_count = N_SECTION // 2
    pair_ids = jnp.arange(pair_count, dtype=jnp.int32)
    swap_flags = jax.random.randint(jax.random.fold_in(key, 1), (pair_count,), 0, 2, dtype=jnp.int32)
    swap_flags = jnp.where((pair_ids == 0) | (pair_ids == pair_count - 1), 1, swap_flags).astype(jnp.int32)
    section_ids = jnp.arange(N_SECTION, dtype=jnp.int32)
    section_swap = jnp.repeat(swap_flags, 2)
    partner = jnp.where(section_ids % 2 == 0, section_ids + 1, section_ids - 1)
    target = jnp.where(section_swap == 1, partner, section_ids).astype(jnp.int32)
    held_slot = jax.random.randint(jax.random.fold_in(key, 2), (N_SECTION,), 0, SLOTS, dtype=jnp.int32)
    slot_ids = jnp.arange(SLOTS, dtype=jnp.int32)
    table = jnp.where(slot_ids[None, :] == held_slot[:, None], target[:, None], -1)
    return table.reshape(-1).astype(jnp.int32)


def touch_ends(entries, stream_key, least, top_value):
    longest = entries.shape.index(max(entries.shape))
    spots = []
    for shift in (0, 1):
        where = [jax.random.randint(jax.random.fold_in(stream_key, axis), (), 0, length) for axis, length in enumerate(entries.shape)]
        where[longest] = (where[longest] + shift) % entries.shape[longest]
        spots.append(tuple(where))
    return entries.at[spots[0]].set(least).at[spots[1]].set(top_value)


def steps_of(rng, dims, split, least, top_value):
    factor_of = 1.0
    for axis_at, blocks in split:
        steps = jax.random.uniform(jax.random.fold_in(jax.random.fold_in(rng, 6), axis_at), (blocks,), jnp.float32, least / len(split), top_value / len(split))
        factor_of = factor_of * jnp.repeat(jnp.exp(steps), dims[axis_at] // blocks).reshape((-1,) + (1,) * (len(dims) - 1 - axis_at))
    return factor_of


def normal_values(stream_key, extent, scale, bound, pieces=(), kind=jnp.bfloat16):
    result = jax.random.normal(stream_key, extent, jnp.float32) * scale
    if len(pieces) > 0:
        result = steps_of(stream_key, extent, pieces, -0.22, 0.18) * result
    return jnp.clip(result, min=-bound, max=bound).astype(kind)


def setup_inputs(seed: int = 0) -> dict:
    streams_of = jax.random.split(jax.random.key(seed), 9)
    return {
        "master_old": normal_values(streams_of[0], (OLD_SLOTS, D, D), D ** -0.5, 0.125, ((0, 8), (1, 32)), jnp.float32),
        "first_moment_old": normal_values(streams_of[1], (OLD_SLOTS, D, D), 30.0, 180.0, ((0, 8), (1, 32)), jnp.float32),
        "second_moment_old": jnp.clip(jnp.exp(math.log(10000.0) - 4.6051702 * jax.random.uniform(streams_of[2], (OLD_SLOTS, D, D), jnp.float32) ** steps_of(streams_of[2], (OLD_SLOTS, D, D), ((0, 8), (1, 32)), -0.2, 0.2)), 100.0, 10000.0),
        "layer_vectors": draw_layer_vectors(jax.random.fold_in(streams_of[8], 71), 0),
        "new_section": draw_new_section(jax.random.fold_in(streams_of[8], 71), 0),
        "frozen": touch_ends((jax.random.randint(streams_of[5], (N_SECTION,), 0, 2) < 1).astype(jnp.int32), jax.random.fold_in(streams_of[5], 1), 0, 1),
        "window_input": normal_values(streams_of[6], (TOKENS, D), 1.0, 6.0, ((0, 32),)),
        "cotangent": normal_values(streams_of[7], (TOKENS, D), 1.0, 6.0, ((0, 32),)),
    }


FIRST_DECAY = 0.9
SECOND_DECAY = 0.999
STEP_SIZE = 0.01
EPSILON = 1e-08
FIRST_CORRECTION = 1.0 - 0.9 ** 10
SECOND_CORRECTION = 1.0 - 0.999 ** 10

def layer_norm(summed, norm_gain, norm_shift):
    center = summed - lax.optimization_barrier(jnp.mean(summed, axis=-1, keepdims=True))
    spread = lax.optimization_barrier(jnp.mean(center * center, axis=-1, keepdims=True))
    return center * lax.rsqrt(spread + 1e-05) * norm_gain + norm_shift

def smooth_gate(values):
    return jax.nn.gelu(values, approximate=True)

def layer_forward(layer_in, weight, vectors):
    linear = jnp.dot(layer_in, weight, preferred_element_type=jnp.float32) + vectors[0]
    summed = layer_in.astype(jnp.float32) + smooth_gate(linear)
    return (linear, layer_norm(summed, vectors[1], vectors[2]))

def layer_backward(layer_in, linear, upstream, weight, vectors):
    summed = layer_in.astype(jnp.float32) + smooth_gate(linear)
    _, pull_norm = jax.vjp(lambda values: layer_norm(values, vectors[1], vectors[2]), summed)
    grad_summed, = pull_norm(upstream.astype(jnp.float32))
    _, pull_gate = jax.vjp(smooth_gate, linear)
    grad_linear, = pull_gate(grad_summed)
    grad_linear = grad_linear.astype(jnp.bfloat16)
    input_grads = grad_summed + lax.dot_general(grad_linear, weight, (((1,), (1,)), ((), ())), preferred_element_type=jnp.float32)
    return (input_grads.astype(jnp.bfloat16), grad_linear)

def replica_sum(layer_in, grad_linear):
    inputs_split = layer_in.reshape(N_REPLICA, TOK_DEV, D)
    grads_split = grad_linear.reshape(N_REPLICA, TOK_DEV, D)

    def accumulate(running, operands):
        partial_value = lax.dot_general(operands[0], operands[1], (((0,), (0,)), ((), ())), preferred_element_type=jnp.float32)
        rounded = lax.optimization_barrier(partial_value.astype(jnp.bfloat16))
        return (running + rounded.astype(jnp.float32), None)
    running, _ = lax.scan(accumulate, jnp.zeros((D, D), jnp.float32), (inputs_split, grads_split))
    return running

def reference(master_old, first_moment_old, second_moment_old, layer_vectors, new_section, frozen, window_input, cotangent):
    layer_ids = jnp.arange(N_SECTION, dtype=jnp.int32)
    slot_ids = jnp.arange(OLD_SLOTS, dtype=jnp.int32)
    matches = new_section[None, :] == layer_ids[:, None]
    source = lax.optimization_barrier(jnp.sum(jnp.where(matches, slot_ids[None, :], 0), axis=1)).astype(jnp.int32)
    master = jnp.take(master_old, source, axis=0)
    first_state = jnp.take(first_moment_old, source, axis=0)
    second_state = jnp.take(second_moment_old, source, axis=0)
    vectors = jnp.take(layer_vectors, source, axis=0).astype(jnp.float32)
    current = window_input
    saved_inputs = []
    saved_linear = []
    weights = []
    for layer_index in range(N_SECTION):
        weight = master[layer_index].astype(jnp.bfloat16)
        linear, output = layer_forward(current, weight, vectors[layer_index])
        saved_inputs.append(current)
        saved_linear.append(linear)
        weights.append(weight)
        current = output.astype(jnp.bfloat16)
    upstream = cotangent
    grad_list = [None] * N_SECTION
    for layer_index in reversed(range(N_SECTION)):
        input_grads, grad_linear = layer_backward(saved_inputs[layer_index], saved_linear[layer_index], upstream, weights[layer_index], vectors[layer_index])
        grad_list[layer_index] = replica_sum(saved_inputs[layer_index], grad_linear)
        upstream = input_grads
    grad_stack = jnp.stack(grad_list)
    learning = (frozen == 0)[:, None, None]
    first_next = FIRST_DECAY * first_state + (1.0 - FIRST_DECAY) * grad_stack
    second_next = SECOND_DECAY * second_state + (1.0 - SECOND_DECAY) * grad_stack * grad_stack
    stepped = master - STEP_SIZE * (first_next / FIRST_CORRECTION) / (jnp.sqrt(second_next / SECOND_CORRECTION) + EPSILON)
    master_new = jnp.where(learning, stepped, master)
    first_moment_new = jnp.where(learning, first_next, first_state)
    second_moment_new = jnp.where(learning, second_next, second_state)
    return (master_new, first_moment_new, second_moment_new)
```

```python
import functools
import jax
import jax.numpy as jnp
from jax import lax
from jax.experimental import pallas as pl
from jax.experimental.pallas import tpu as pltpu
from jax.sharding import PartitionSpec as P

BF16 = jnp.bfloat16
F32 = jnp.float32
D = 2048
NZ = 8
VMEM_LIMIT = 48 * 1024 * 1024
GELU_K = 0.7978845608028654


def weight_copies(near, far, w_scr, sems, z_me, x_me, core):
    groups = {}
    for side, msgs in ((0, near), (1, far)):
        owner = core if side == 0 else 1 - core
        for piece, dx, dz, half in msgs:
            x = lax.rem(x_me + dx + 4, 4)
            z = lax.rem(z_me + dz + 8, 8)
            row = pl.multiple_of(((z * 2 + x // 2) * 2 + owner) * 64 + half * 32, 32)
            slot = dx % 2
            k = dz % 8
            groups.setdefault((slot, k), []).append(
                pltpu.make_async_copy(piece, w_scr.at[slot, pl.ds(row, 32), :], sems.at[slot, k])
            )
    return groups


def message_pieces(refs):
    pieces = []
    z_steps = (0, -1, 1, -2, 2, -3, 3)
    x_order = (0, -1, 1, 2)
    head, tail = refs[:9], refs[9:]
    for ref, dz in zip(head[:7], z_steps):
        for at, dx in enumerate(x_order):
            pieces.append((ref.at[at], dx, dz, 0))
    for at, dx in enumerate(x_order):
        ref = head[7] if at < 2 else head[8]
        pieces.append((ref.at[at % 2], dx, 4, 0))
    order = (0, -1, 1, -2, 2, -3, 3, 4)
    for ref, dx in zip(tail[:3], (0, -1, 1)):
        for at, dz in enumerate(order):
            pieces.append((ref.at[at], dx, dz, 1))
    for at, dz in enumerate(order):
        ref = tail[3] if at < 4 else tail[4]
        pieces.append((ref.at[at % 4], 2, dz, 1))
    return pieces


def gelu(u):
    return 0.5 * u * (1.0 + jnp.tanh(GELU_K * (u + 0.044715 * (u * u * u))))


def gelu_slope(u):
    t = jnp.tanh(GELU_K * (u + 0.044715 * (u * u * u)))
    return 0.5 * (1.0 + t) + 0.5 * u * (1.0 - t * t) * (GELU_K * (1.0 + 3 * 0.044715 * (u * u)))


def norm_parts(z):
    center = z - jnp.mean(z, axis=-1, keepdims=True)
    spread = jnp.mean(center * center, axis=-1, keepdims=True)
    return center, lax.rsqrt(spread + 1e-5)


def issue(groups, first):
    def start(slot):
        for k in range(NZ):
            for copy in groups[slot, k]:
                copy.start()

    @pl.when(first == 0)
    def _():
        start(0)
        start(1)

    @pl.when(first == 1)
    def _():
        start(1)
        start(0)


def wait_block(w_scr, sems, slot, k, z):
    rows = w_scr.at[slot, pl.ds(pl.multiple_of(z * 256, 256), 256), :]
    pltpu.make_async_copy(rows, rows, sems.at[slot, k]).wait()


def forward_kernel(n_msgs, rows, ctl, *refs):
    near, far = refs[:n_msgs], refs[n_msgs:2 * n_msgs]
    window, recv, vec, xs_in, ls_in, act, xs, ls, w_scr, x_scr, lin_scr, sems, sem_x, sem_o = refs[2 * n_msgs:]
    del xs_in, ls_in
    active, stage, batch, x_me, z_me, core, first, xl = (ctl[i] for i in range(8))

    @pl.when(active == 1)
    def _():
        groups = weight_copies(message_pieces(near), message_pieces(far), w_scr, sems, z_me, x_me, core)
        per_half = window.shape[0] // 2
        at = pl.multiple_of(batch * rows, rows)

        @pl.when(stage == 0)
        def _():
            src = window.at[pl.ds(pl.multiple_of(xl * per_half + batch * rows, rows), rows), :]
            pltpu.make_async_copy(src, x_scr.at[0], sem_x).start()

        @pl.when(stage != 0)
        def _():
            pltpu.make_async_copy(recv, x_scr.at[0], sem_x).start()

        issue(groups, first)
        pltpu.make_async_copy(recv, x_scr.at[0], sem_x).wait()
        outs = []
        for layer in range(2):
            slot = first ^ layer
            lin_scr[layer] = jnp.broadcast_to(vec[layer, 0:1, :], (rows, D))
            for k in range(NZ):
                z = lax.rem(z_me + k, NZ)
                wait_block(w_scr, sems, slot, k, z)
                cols = pl.ds(pl.multiple_of(z * 256, 256), 256)
                lin_scr[layer] += jnp.dot(
                    x_scr[layer, :, cols], w_scr[slot, cols, :], preferred_element_type=F32
                )
            lin = lin_scr[layer]
            center, scale = norm_parts(x_scr[layer].astype(F32) + gelu(lin))
            y = (center * scale * vec[layer, 1:2, :] + vec[layer, 2:3, :]).astype(BF16)
            if layer == 0:
                x_scr[1] = y
            else:
                act[...] = y
            for src, dst, n in ((x_scr, xs, 0), (lin_scr, ls, 1)):
                copy = pltpu.make_async_copy(src.at[layer], dst.at[layer, pl.ds(at, rows), :], sem_o.at[layer, n])
                copy.start()
                outs.append(copy)
        for copy in outs:
            copy.wait()


def backward_kernel(n_msgs, rows, ctl, *refs):
    near, far = refs[:n_msgs], refs[n_msgs:2 * n_msgs]
    cot, recv, vec, xs, ls, ds_in, back, ds, w_scr, g_scr, x_scr, lin_scr, dz_scr, dl_scr, sems, sem_x, sem_o = refs[2 * n_msgs:]
    del ds_in
    active, stage, batch, x_me, z_me, core, first, xl = (ctl[i] for i in range(8))

    @pl.when(active == 1)
    def _():
        groups = weight_copies(message_pieces(near), message_pieces(far), w_scr, sems, z_me, x_me, core)
        per_half = cot.shape[0] // 2
        at = pl.multiple_of(batch * rows, rows)

        @pl.when(stage == 3)
        def _():
            src = cot.at[pl.ds(pl.multiple_of(xl * per_half + batch * rows, rows), rows), :]
            pltpu.make_async_copy(src, g_scr, sem_x.at[2, 0]).start()

        @pl.when(stage != 3)
        def _():
            pltpu.make_async_copy(recv, g_scr, sem_x.at[2, 0]).start()

        loads = {}
        for layer in (1, 0):
            loads[layer] = (
                pltpu.make_async_copy(xs.at[layer, pl.ds(at, rows), :], x_scr.at[layer], sem_x.at[layer, 0]),
                pltpu.make_async_copy(ls.at[layer, pl.ds(at, rows), :], lin_scr.at[layer], sem_x.at[layer, 1]),
            )
            for copy in loads[layer]:
                copy.start()
        issue(groups, 1 - first)
        pltpu.make_async_copy(recv, g_scr, sem_x.at[2, 0]).wait()
        outs = []
        for layer in (1, 0):
            slot = first ^ layer
            for copy in loads[layer]:
                copy.wait()
            lin = lin_scr[layer]
            center, scale = norm_parts(x_scr[layer].astype(F32) + gelu(lin))
            unit = center * scale
            g = g_scr[...].astype(F32) * vec[layer, 1:2, :]
            dz = scale * (g - jnp.mean(g, axis=-1, keepdims=True) - unit * jnp.mean(g * unit, axis=-1, keepdims=True))
            dz_scr[...] = dz
            dl_scr[layer] = (dz * gelu_slope(lin)).astype(BF16)
            copy = pltpu.make_async_copy(dl_scr.at[layer], ds.at[layer, pl.ds(at, rows), :], sem_o.at[layer])
            copy.start()
            outs.append(copy)
            for k in range(NZ):
                z = lax.rem(z_me + k, NZ)
                wait_block(w_scr, sems, slot, k, z)
                cols = pl.ds(pl.multiple_of(z * 256, 256), 256)

                def step():
                    down = lax.dot_general(
                        dl_scr[layer], w_scr[slot, cols, :], (((1,), (1,)), ((), ())), preferred_element_type=F32
                    )
                    y = (dz_scr[:, cols] + down).astype(BF16)
                    if layer == 1:
                        g_scr[:, cols] = y
                    else:
                        back[:, cols] = y

                if layer == 1:
                    step()
                else:
                    pl.when(stage != 0)(step)
        for copy in outs:
            copy.wait()


def forward_call(ctl, near, far, window, recv, vec, xs, ls):
    rows = recv.shape[0]
    n = len(near)
    any_spec = pl.BlockSpec(memory_space=pl.ANY)
    vm = pl.BlockSpec(memory_space=pltpu.VMEM)
    return pl.pallas_call(
        functools.partial(forward_kernel, n, rows),
        out_shape=(
            jax.ShapeDtypeStruct((rows, D), BF16),
            jax.ShapeDtypeStruct(xs.shape, xs.dtype),
            jax.ShapeDtypeStruct(ls.shape, ls.dtype),
        ),
        in_specs=[pl.BlockSpec(memory_space=pltpu.SMEM)] + [any_spec] * (2 * n + 2) + [vm] + [any_spec] * 2,
        out_specs=(vm, any_spec, any_spec),
        scratch_shapes=[
            pltpu.VMEM((2, D, D), BF16),
            pltpu.VMEM((2, rows, D), BF16),
            pltpu.VMEM((2, rows, D), F32),
            pltpu.SemaphoreType.DMA((2, NZ)),
            pltpu.SemaphoreType.DMA,
            pltpu.SemaphoreType.DMA((2, 2)),
        ],
        input_output_aliases={2 * n + 4: 1, 2 * n + 5: 2},
        compiler_params=pltpu.CompilerParams(vmem_limit_bytes=VMEM_LIMIT),
        cost_estimate=pl.CostEstimate(flops=4 * rows * D * D, bytes_accessed=4 * D * D, transcendentals=2 * rows * D),
        name="forward_tick",
    )(ctl, *near, *far, window, recv, vec, xs, ls)


def backward_call(ctl, near, far, cot, recv, vec, xs, ls, ds):
    rows = recv.shape[0]
    n = len(near)
    any_spec = pl.BlockSpec(memory_space=pl.ANY)
    vm = pl.BlockSpec(memory_space=pltpu.VMEM)
    return pl.pallas_call(
        functools.partial(backward_kernel, n, rows),
        out_shape=(jax.ShapeDtypeStruct((rows, D), BF16), jax.ShapeDtypeStruct(ds.shape, ds.dtype)),
        in_specs=[pl.BlockSpec(memory_space=pltpu.SMEM)] + [any_spec] * (2 * n + 2) + [vm] + [any_spec] * 3,
        out_specs=(vm, any_spec),
        scratch_shapes=[
            pltpu.VMEM((2, D, D), BF16),
            pltpu.VMEM((rows, D), BF16),
            pltpu.VMEM((2, rows, D), BF16),
            pltpu.VMEM((2, rows, D), F32),
            pltpu.VMEM((rows, D), F32),
            pltpu.VMEM((2, rows, D), BF16),
            pltpu.SemaphoreType.DMA((2, NZ)),
            pltpu.SemaphoreType.DMA((3, 2)),
            pltpu.SemaphoreType.DMA((2,)),
        ],
        input_output_aliases={2 * n + 6: 1},
        compiler_params=pltpu.CompilerParams(vmem_limit_bytes=VMEM_LIMIT),
        cost_estimate=pl.CostEstimate(flops=4 * rows * D * D, bytes_accessed=4 * D * D, transcendentals=2 * rows * D),
        name="backward_tick",
    )(ctl, *near, *far, cot, recv, vec, xs, ls, ds)

AXES = ("y", "xl", "z", "xh", "c")
MICRO = 2
STAGES = 4

FIRST_DECAY = 0.9
SECOND_DECAY = 0.999
STEP_SIZE = 0.01
EPSILON = 1e-08
FIRST_CORRECTION = 1.0 - 0.9**10
SECOND_CORRECTION = 1.0 - 0.999**10


def shift_x(v, by):
    place = lambda x: (x & 1) * 2 + (x >> 1)
    return lax.ppermute(v, ("xl", "xh"), [(place(x), place((x + by) % 4)) for x in range(4)])


def shift_z(v, by):
    return lax.ppermute(v, "z", [(z, (z + by) % 8) for z in range(8)])


def swap_core(v):
    return lax.ppermute(v, "c", [(0, 1), (1, 0)])


def swap_pair(v):
    return lax.ppermute(v, "xl", [(0, 1), (1, 0)])


def swap_cross(v):
    return lax.ppermute(v, ("y", "xl"), [(3, 4), (4, 3)])


def ring_gather(v, shift, steps):
    right = left = v
    out = []
    for _ in range(1, steps):
        right, left = shift(right, 1), shift(left, -1)
        out += [right, left]
    half = v.shape[0] // 2
    return out + [shift(right[:half], 1), shift(left[half:], -1)]


def gather_plane(rows):
    a = rows[:32][None]
    b = rows[32:].reshape(2, 16, D)
    near_x = [a, shift_x(a, 1), shift_x(a, -1), shift_x(a, 2)]
    along_z = jnp.concatenate([b] + ring_gather(b, shift_z, 4), axis=0).reshape(8, 32, D)
    heads = jnp.concatenate(near_x, axis=0)
    return [heads] + ring_gather(heads, shift_z, 4) + [along_z] + ring_gather(along_z, shift_x, 2)


def add_rounded(a, b):
    return (a.astype(F32) + b.astype(F32)).astype(BF16)


def ring_reduce(chunks, shift, steps):
    half = chunks.shape[1] // 2
    far = chunks[steps]
    right, left = shift(far[:half], 1), shift(far[half:], -1)
    for k in range(steps - 1, 0, -1):
        up, down = chunks[k], chunks[2 * steps - k]
        if k == steps - 1:
            right = jnp.concatenate([add_rounded(up[:half], right), up[half:]], axis=0)
            left = jnp.concatenate([down[:half], add_rounded(down[half:], left)], axis=0)
        else:
            right, left = add_rounded(up, right), add_rounded(down, left)
        right, left = shift(right, 1), shift(left, -1)
    return chunks[0].astype(F32) + right.astype(F32) + left.astype(F32)


def grad_kernel(at, ds, g1, g2):
    for parity in range(2):
        block = at[:, parity].reshape(2 * 2 * 64, at.shape[-1])
        for n in range(4):
            cols = pl.ds(n * 512, 512)
            part = jnp.dot(block, ds[parity, :, cols], preferred_element_type=F32).astype(BF16)
            part = part.reshape(2, 2, 2, 32, 512)
            for z in range(2):
                for i in range(2):
                    g1[z, 2 * i + parity, :, cols] = part[z, i, 0]
                    g2[2 * i + parity, z, :, cols] = part[z, i, 1]


def grad_call(at, ds):
    tokens = at.shape[-1]
    return pl.pallas_call(
        grad_kernel,
        grid=(4,),
        out_shape=(jax.ShapeDtypeStruct((8, 4, 32, D), BF16), jax.ShapeDtypeStruct((4, 8, 32, D), BF16)),
        in_specs=[
            pl.BlockSpec((2, 2, 2, 64, tokens), lambda i: (i, 0, 0, 0, 0)),
            pl.BlockSpec((2, tokens, D), lambda i: (0, 0, 0)),
        ],
        out_specs=(
            pl.BlockSpec((2, 4, 32, D), lambda i: (i, 0, 0, 0)),
            pl.BlockSpec((4, 2, 32, D), lambda i: (0, i, 0, 0)),
        ),
        compiler_params=pltpu.CompilerParams(vmem_limit_bytes=VMEM_LIMIT),
        cost_estimate=pl.CostEstimate(flops=4 * tokens * D * 1024, bytes_accessed=12 << 20, transcendentals=0),
        name="weight_grads",
    )(at, ds)


def rolled(v, axis, by, order=None):
    size = v.shape[axis]
    return lax.dynamic_slice_in_dim(jnp.concatenate([v, v], axis=axis), by, size, axis=axis)


def scatter_grads(xs, ds, x_me, z_me, core, xl):
    x_all = jnp.concatenate([xs, swap_core(xs)], axis=1)
    d_all = jnp.concatenate([ds, swap_core(ds)], axis=1)
    tokens = x_all.shape[1]
    at = jnp.swapaxes(x_all, 1, 2).reshape(2, 8, 2, 2, 64, tokens)
    at = lax.dynamic_index_in_dim(at, core, 3, keepdims=False)
    at = at.transpose(1, 2, 0, 3, 4).reshape(8, 4, 64, tokens)
    at = rolled(rolled(at, 0, z_me), 1, x_me)
    at = at.reshape(8, 2, 2, 64, tokens).swapaxes(1, 2)
    d_all = rolled(d_all, 0, xl)
    g1, g2 = grad_call(at, d_all)
    first = ring_reduce(g1, shift_z, 4).astype(BF16)
    second = ring_reduce(g2, shift_x, 2).astype(BF16)
    first = (
        first[0].astype(F32)
        + shift_x(first[1], 1).astype(F32)
        + shift_x(first[3], -1).astype(F32)
        + shift_x(first[2], 2).astype(F32)
    )
    second = ring_reduce(second.reshape(8, 2, 16, D), shift_z, 4).reshape(32, D)
    return jnp.concatenate([first, second], axis=0)


def pick(stacked, mask):
    shaped = mask.reshape((-1,) + (1,) * (stacked.ndim - 1))
    return jnp.sum(jnp.where(shaped, stacked, jnp.zeros_like(stacked)), axis=0)


def shards(master_old, first_old, second_old, layer_vectors, new_section, frozen, window_input, cotangent):
    y, xl, z_me, xh, core = (lax.axis_index(name) for name in AXES)
    section = y * 2 + xl
    x_me = xl + 2 * xh
    stay = new_section == section
    pair = new_section == jnp.bitwise_xor(section, 1)
    cross = jnp.where(section == 3, new_section == 4, (section == 4) & (new_section == 3))
    plane = stay | pair
    label = jnp.where(jnp.any(plane), jnp.sum(jnp.where(plane, new_section, 0)) & 1, xl)

    held = pick(master_old, plane).astype(BF16) + swap_cross(pick(master_old, cross).astype(BF16))
    near = gather_plane(held)
    far = [swap_core(m) for m in near]
    own_vec = pick(layer_vectors, plane) + swap_cross(pick(layer_vectors, cross))
    other_vec = swap_pair(own_vec)
    vec = jnp.where(label == 0, jnp.stack([own_vec, other_vec]), jnp.stack([other_vec, own_vec])).astype(F32)

    tokens = window_input.shape[0] // 2
    rows = tokens // MICRO
    xs = jnp.zeros((2, tokens, D), BF16)
    ls = jnp.zeros((2, tokens, D), F32)
    ds = jnp.zeros((2, tokens, D), BF16)
    ahead = behind = jnp.zeros((rows, D), BF16)

    def control(batch):
        active = (batch >= 0) & (batch < MICRO)
        slot = jnp.clip(batch, 0, MICRO - 1)
        parts = [active, y, slot, x_me, z_me, core, label, xl]
        return jnp.stack([jnp.asarray(p, jnp.int32) for p in parts])

    for tick in range(MICRO + 2 * STAGES - 2):
        f_stages = [s for s in range(STAGES) if 0 <= tick - s < MICRO]
        b_stages = [s for s in range(STAGES) if 0 <= tick - 2 * (STAGES - 1) + s < MICRO]
        if f_stages:
            act, xs, ls = forward_call(control(tick - y), near, far, window_input, ahead, vec, xs, ls)
            pairs = [(s, s + 1) for s in f_stages if s + 1 < STAGES]
            if pairs:
                ahead = lax.ppermute(act, "y", pairs)
        if b_stages:
            back, ds = backward_call(
                control(tick - 2 * (STAGES - 1) + y), near, far, cotangent, behind, vec, xs, ls, ds
            )
            pairs = [(s, s - 1) for s in b_stages if s > 0]
            if pairs:
                behind = lax.ppermute(back, "y", pairs)

    zero = (near[-1][0, 0, 0].astype(F32) * 0.0).astype(jnp.int32)
    late = new_section + zero
    states = (master_old, first_old, second_old)
    send = lambda mask: jnp.stack([pick(s, mask) for s in states])
    late_pair = late == jnp.bitwise_xor(section, 1)
    late_cross = jnp.where(section == 3, late == 4, (section == 4) & (late == 3))
    moved = swap_pair(send(late_pair)) + swap_cross(send(late_cross))
    master, first_state, second_state = (pick(s, stay) + moved[i] for i, s in enumerate(states))

    grad_rows = scatter_grads(xs, ds, x_me, z_me, core, xl)
    learning = lax.dynamic_index_in_dim(frozen, section, 0, keepdims=False) == 0
    first_next = FIRST_DECAY * first_state + (1.0 - FIRST_DECAY) * grad_rows
    second_next = SECOND_DECAY * second_state + (1.0 - SECOND_DECAY) * grad_rows * grad_rows
    stepped = master - STEP_SIZE * (first_next / FIRST_CORRECTION) / (
        jnp.sqrt(second_next / SECOND_CORRECTION) + EPSILON
    )
    master_new = jnp.where(learning, stepped, master)
    first_new = jnp.where(learning, first_next, first_state)
    second_new = jnp.where(learning, second_next, second_state)
    return (master_new[None], first_new[None], second_new[None])


def solution(mesh):
    fine = jax.sharding.Mesh(mesh.devices.reshape(4, 2, 8, 2, 2), AXES)
    sec, rep = ("y", "xl"), ("z", "xh", "c")
    rows = P(sec, rep, None)
    in_specs = (rows, rows, rows, P(sec, None, None), P(sec), P(), P(rep, None), P(rep, None))
    return jax.shard_map(shards, mesh=fine, in_specs=in_specs, out_specs=(rows, rows, rows), check_vma=False)
```

```python
import functools
import jax
import jax.numpy as jnp
from jax import lax
from jax.experimental import pallas as pl
from jax.experimental.pallas import tpu as pltpu
from jax.sharding import PartitionSpec as P

BF16 = jnp.bfloat16
F32 = jnp.float32
D = 2048
NZ = 8
VMEM_LIMIT = 60 * 1024 * 1024
GELU_K = 0.7978845608028654


def weight_copies(near, far, w_scr, sems, z_me, x_me, core):
    copies = ([], [])
    for msgs, owner in ((near, core), (far, 1 - core)):
        head, tail = msgs[:9], msgs[9:]
        for dx, ref, zs in ((0, 0, 0), (-1, 1, 0), (1, 2, 0), (2, 3, 0), (2, 4, 4)):
            xh = lax.rem(x_me + dx + 4, 4) // 2
            count = 8 if ref < 3 else 4
            dst = w_scr.at[dx % 2, pl.ds(zs, count), xh, owner, pl.ds(32, 32), :]
            copies[dx % 2].append(pltpu.make_async_copy(tail[ref], dst, sems.at[dx % 2, NZ]))
    for slot in range(2):
        for at, dz in enumerate((0, -1, 1, -2, 2, -3, 3, 4)):
            z = lax.rem(z_me + dz + 8, 8)
            for msgs, owner in ((near, core), (far, 1 - core)):
                src = msgs[at].at[slot] if at < 7 else msgs[7 + slot].at[0]
                dst = w_scr.at[slot, z, :, owner, pl.ds(0, 32), :]
                copies[slot].append(pltpu.make_async_copy(src, dst, sems.at[slot, dz % 8]))
    return copies


def gelu_parts(u):
    square = u * u
    t = jnp.tanh(GELU_K * u * (1.0 + 0.044715 * square))
    return 0.5 * u * (1.0 + t), t, square


def gelu_slope(u, t, square):
    return 0.5 * (1.0 + t) + 0.5 * u * (1.0 - t * t) * (GELU_K * (1.0 + 3 * 0.044715 * square))


def norm_parts(z):
    center = z - jnp.mean(z, axis=-1, keepdims=True)
    spread = jnp.mean(center * center, axis=-1, keepdims=True)
    return center, lax.rsqrt(spread + 1e-5)


def issue(groups, first):
    def start(slot):
        for copy in groups[slot]:
            copy.start()

    @pl.when(first == 0)
    def _():
        start(0)
        start(1)

    @pl.when(first == 1)
    def _():
        start(1)
        start(0)


def wait_tails(w_scr, sems, slot):
    rows = w_scr.at[slot, :, :, :, pl.ds(32, 32), :]
    pltpu.make_async_copy(rows, rows, sems.at[slot, NZ]).wait()


def wait_heads(w_scr, sems, slot, k, z):
    rows = w_scr.at[slot, z, :, :, pl.ds(0, 32), :]
    pltpu.make_async_copy(rows, rows, sems.at[slot, k]).wait()


def forward_kernel(n_msgs, rows, ctl, *refs):
    near, far = refs[:n_msgs], refs[n_msgs:2 * n_msgs]
    window, recv, vec_in, xs_in, ls_in, act, xs, ls, w_scr, x_scr, lin_scr, vec, act_scr, sems, sem_x, sem_v, sem_o = refs[2 * n_msgs:]
    del xs_in, ls_in
    active, stage, batch, x_me, z_me, core, first, xl = (ctl[i] for i in range(8))

    @pl.when(active == 1)
    def _():
        groups = weight_copies(near, far, w_scr, sems, z_me, x_me, core)
        per_half = window.shape[0] // 2
        at = pl.multiple_of(batch * rows, rows)

        @pl.when(stage == 0)
        def _():
            src = window.at[pl.ds(pl.multiple_of(xl * per_half + batch * rows, rows), rows), :]
            pltpu.make_async_copy(src, x_scr.at[0], sem_x).start()

        @pl.when(stage != 0)
        def _():
            pltpu.make_async_copy(recv, x_scr.at[0], sem_x).start()

        vec_copy = pltpu.make_async_copy(vec_in, vec, sem_v)
        vec_copy.start()
        issue(groups, first)
        vec_copy.wait()
        pltpu.make_async_copy(recv, x_scr.at[0], sem_x).wait()
        outs = []
        for layer in range(2):
            slot = first ^ layer
            lin_scr[layer] = jnp.broadcast_to(vec[layer, 0:1, :], (rows, D))
            wait_tails(w_scr, sems, slot)

            @pl.loop(0, NZ)
            def _(k):
                z = lax.rem(z_me + k, NZ)
                wait_heads(w_scr, sems, slot, k, z)
                cols = pl.ds(pl.multiple_of(z * 256, 256), 256)
                lin_scr[layer] += jnp.dot(
                    x_scr[layer, :, cols], w_scr[slot, z].reshape(256, D), preferred_element_type=F32
                )

            lin = lin_scr[layer]
            center, scale = norm_parts(x_scr[layer].astype(F32) + gelu_parts(lin)[0])
            y = (center * scale * vec[layer, 1:2, :] + vec[layer, 2:3, :]).astype(BF16)
            if layer == 0:
                x_scr[1] = y
            else:
                act_scr[...] = y
                outs.append(pltpu.make_async_copy(act_scr, act, sem_v))
                outs[-1].start()
            for src, dst, n in ((x_scr, xs, 0), (lin_scr, ls, 1)):
                copy = pltpu.make_async_copy(src.at[layer], dst.at[layer, pl.ds(at, rows), :], sem_o.at[layer, n])
                copy.start()
                outs.append(copy)
        for copy in outs:
            copy.wait()


def backward_kernel(n_msgs, rows, n_early, ctl, *refs):
    near, far = refs[:n_msgs], refs[n_msgs:2 * n_msgs]
    cot, recv, vec_in, xs, ls, ds_in = refs[2 * n_msgs:2 * n_msgs + 6]
    back, ds, w_scr, g_scr, x_scr, lin_scr, dz_scr, dl_scr, vec, back_scr, sems, sem_x, sem_v, sem_o = refs[2 * n_msgs + 6 + n_early:]
    del ds_in
    active, stage, batch, x_me, z_me, core, first, xl = (ctl[i] for i in range(8))

    @pl.when(active == 1)
    def _():
        groups = weight_copies(near, far, w_scr, sems, z_me, x_me, core)
        per_half = cot.shape[0] // 2
        at = pl.multiple_of(batch * rows, rows)

        @pl.when(stage == 3)
        def _():
            src = cot.at[pl.ds(pl.multiple_of(xl * per_half + batch * rows, rows), rows), :]
            pltpu.make_async_copy(src, g_scr, sem_x.at[2, 0]).start()

        @pl.when(stage != 3)
        def _():
            pltpu.make_async_copy(recv, g_scr, sem_x.at[2, 0]).start()

        loads = {}
        for layer in (1, 0):
            loads[layer] = (
                pltpu.make_async_copy(xs.at[layer, pl.ds(at, rows), :], x_scr.at[layer], sem_x.at[layer, 0]),
                pltpu.make_async_copy(ls.at[layer, pl.ds(at, rows), :], lin_scr.at[layer], sem_x.at[layer, 1]),
            )
            for copy in loads[layer]:
                copy.start()
        vec_copy = pltpu.make_async_copy(vec_in, vec, sem_v)
        vec_copy.start()
        issue(groups, 1 - first)
        vec_copy.wait()
        pltpu.make_async_copy(recv, g_scr, sem_x.at[2, 0]).wait()
        outs = []
        for layer in (1, 0):
            slot = first ^ layer
            for copy in loads[layer]:
                copy.wait()
            lin = lin_scr[layer]
            gated, t, square = gelu_parts(lin)
            center, scale = norm_parts(x_scr[layer].astype(F32) + gated)
            unit = center * scale
            g = g_scr[...].astype(F32) * vec[layer, 1:2, :]
            dz = scale * (g - jnp.mean(g, axis=-1, keepdims=True) - unit * jnp.mean(g * unit, axis=-1, keepdims=True))
            dz_scr[...] = dz
            dl_scr[layer] = (dz * gelu_slope(lin, t, square)).astype(BF16)
            copy = pltpu.make_async_copy(dl_scr.at[layer], ds.at[layer, pl.ds(at, rows), :], sem_o.at[layer])
            copy.start()
            outs.append(copy)
            wait_tails(w_scr, sems, slot)

            @pl.loop(0, NZ)
            def _(k):
                z = lax.rem(z_me + k, NZ)
                wait_heads(w_scr, sems, slot, k, z)
                cols = pl.ds(pl.multiple_of(z * 256, 256), 256)

                def step():
                    down = lax.dot_general(
                        dl_scr[layer], w_scr[slot, z].reshape(256, D), (((1,), (1,)), ((), ())), preferred_element_type=F32
                    )
                    y = (dz_scr[:, cols] + down).astype(BF16)
                    if layer == 1:
                        g_scr[:, cols] = y
                    else:
                        back_scr[:, cols] = y

                if layer == 1:
                    step()
                else:
                    pl.when(stage != 0)(step)
        outs.append(pltpu.make_async_copy(back_scr, back, sem_v))
        outs[-1].start()
        for copy in outs:
            copy.wait()


def forward_call(ctl, near, far, window, recv, vec, xs, ls):
    rows = recv.shape[0]
    n = len(near)
    any_spec = pl.BlockSpec(memory_space=pl.ANY)
    return pl.pallas_call(
        functools.partial(forward_kernel, n, rows),
        out_shape=(
            jax.ShapeDtypeStruct((rows, D), BF16),
            jax.ShapeDtypeStruct(xs.shape, xs.dtype),
            jax.ShapeDtypeStruct(ls.shape, ls.dtype),
        ),
        in_specs=[pl.BlockSpec(memory_space=pltpu.SMEM)] + [any_spec] * (2 * n + 5),
        out_specs=(any_spec, any_spec, any_spec),
        scratch_shapes=[
            pltpu.VMEM((2, 8, 2, 2, 64, D), BF16),
            pltpu.VMEM((2, rows, D), BF16),
            pltpu.VMEM((2, rows, D), F32),
            pltpu.VMEM(vec.shape, F32),
            pltpu.VMEM((rows, D), BF16),
            pltpu.SemaphoreType.DMA((2, NZ + 1)),
            pltpu.SemaphoreType.DMA,
            pltpu.SemaphoreType.DMA,
            pltpu.SemaphoreType.DMA((2, 2)),
        ],
        input_output_aliases={2 * n + 4: 1, 2 * n + 5: 2},
        compiler_params=pltpu.CompilerParams(vmem_limit_bytes=VMEM_LIMIT),
        cost_estimate=pl.CostEstimate(flops=4 * rows * D * D, bytes_accessed=4 * D * D, transcendentals=2 * rows * D),
        name="forward_tick",
    )(ctl, *near, *far, window, recv, vec, xs, ls)


def backward_call(ctl, near, far, cot, recv, vec, xs, ls, ds, early=()):
    rows = recv.shape[0]
    n = len(near)
    any_spec = pl.BlockSpec(memory_space=pl.ANY)
    return pl.pallas_call(
        functools.partial(backward_kernel, n, rows, len(early)),
        out_shape=(jax.ShapeDtypeStruct((rows, D), BF16), jax.ShapeDtypeStruct(ds.shape, ds.dtype)),
        in_specs=[pl.BlockSpec(memory_space=pltpu.SMEM)] + [any_spec] * (2 * n + 6 + len(early)),
        out_specs=(any_spec, any_spec),
        scratch_shapes=[
            pltpu.VMEM((2, 8, 2, 2, 64, D), BF16),
            pltpu.VMEM((rows, D), BF16),
            pltpu.VMEM((2, rows, D), BF16),
            pltpu.VMEM((2, rows, D), F32),
            pltpu.VMEM((rows, D), F32),
            pltpu.VMEM((2, rows, D), BF16),
            pltpu.VMEM(vec.shape, F32),
            pltpu.VMEM((rows, D), BF16),
            pltpu.SemaphoreType.DMA((2, NZ + 1)),
            pltpu.SemaphoreType.DMA((3, 2)),
            pltpu.SemaphoreType.DMA,
            pltpu.SemaphoreType.DMA((2,)),
        ],
        input_output_aliases={2 * n + 6: 1},
        compiler_params=pltpu.CompilerParams(vmem_limit_bytes=VMEM_LIMIT),
        cost_estimate=pl.CostEstimate(flops=4 * rows * D * D, bytes_accessed=4 * D * D, transcendentals=2 * rows * D),
        name="backward_tick",
    )(ctl, *near, *far, cot, recv, vec, xs, ls, ds, *early)

AXES = ("y", "xl", "z", "xh", "c")
MICRO = 2
STAGES = 4

FIRST_DECAY = 0.9
SECOND_DECAY = 0.999
STEP_SIZE = 0.01
EPSILON = 1e-08
FIRST_CORRECTION = 1.0 - 0.9**10
SECOND_CORRECTION = 1.0 - 0.999**10


def shift_x(v, by):
    place = lambda x: (x & 1) * 2 + (x >> 1)
    return lax.ppermute(v, ("xl", "xh"), [(place(x), place((x + by) % 4)) for x in range(4)])


def shift_z(v, by):
    return lax.ppermute(v, "z", [(z, (z + by) % 8) for z in range(8)])


def swap_core(v):
    return lax.ppermute(v, "c", [(0, 1), (1, 0)])


def swap_pair(v):
    return lax.ppermute(v, "xl", [(0, 1), (1, 0)])


def swap_cross(v):
    return lax.ppermute(v, ("y", "xl"), [(3, 4), (4, 3)])


def ring_gather(v, shift, steps):
    right = left = v
    out = []
    for _ in range(1, steps):
        right, left = shift(right, 1), shift(left, -1)
        out += [right, left]
    half = v.shape[0] // 2
    return out + [shift(right[:half], 1), shift(left[half:], -1)]


def gather_plane(rows, x_me, xh):
    a, b = rows[:32], rows[32:]
    before, after, across = shift_x(a, 1), shift_x(a, -1), shift_x(a, 2)
    along_z = lax.all_gather(b, "z", axis=0)
    own_first, before_first = xh == 0, lax.rem(x_me + 3, 4) < 2
    heads = jnp.stack(
        [
            jnp.stack([jnp.where(own_first, a, across), jnp.where(own_first, across, a)]),
            jnp.stack([jnp.where(before_first, before, after), jnp.where(before_first, after, before)]),
        ]
    )
    return [heads] + ring_gather(heads, shift_z, 4) + [along_z] + ring_gather(along_z, shift_x, 2)


def add_rounded(a, b):
    return (a.astype(F32) + b.astype(F32)).astype(BF16)


def ring_reduce(chunks, shift, steps):
    half = chunks.shape[1] // 2
    far = chunks[steps]
    right, left = shift(far[:half], 1), shift(far[half:], -1)
    for k in range(steps - 1, 0, -1):
        up, down = chunks[k], chunks[2 * steps - k]
        if k == steps - 1:
            right = jnp.concatenate([add_rounded(up[:half], right), up[half:]], axis=0)
            left = jnp.concatenate([down[:half], add_rounded(down[half:], left)], axis=0)
        else:
            right, left = add_rounded(up, right), add_rounded(down, left)
        right, left = shift(right, 1), shift(left, -1)
    return chunks[0].astype(F32) + right.astype(F32) + left.astype(F32)


def grad_kernel(n_parts, xt, *refs):
    parts, g, d_scr, sem = refs[:n_parts], refs[n_parts], refs[n_parts + 1], refs[n_parts + 2]
    size = parts[0].shape[0]
    for i, part in enumerate(parts):
        pltpu.make_async_copy(part, d_scr.at[pl.ds(i * size, size), :], sem).start()
    pltpu.make_async_copy(d_scr, d_scr, sem).wait()

    @pl.loop(0, D // 256)
    def _(n):
        cols = pl.ds(pl.multiple_of(n * 256, 256), 256)
        part = jnp.dot(xt[...], d_scr[:, cols], preferred_element_type=F32).astype(BF16)
        g[:, :, cols] = part.reshape(8, 64, 256)


def grad_call(xt, parts):
    tokens = xt.shape[1]
    return pl.pallas_call(
        functools.partial(grad_kernel, len(parts)),
        out_shape=jax.ShapeDtypeStruct((8, 64, D), BF16),
        in_specs=[pl.BlockSpec(memory_space=pltpu.VMEM)] + [pl.BlockSpec(memory_space=pl.ANY)] * len(parts),
        out_specs=pl.BlockSpec(memory_space=pltpu.VMEM),
        scratch_shapes=[pltpu.VMEM((tokens, D), BF16), pltpu.SemaphoreType.DMA],
        compiler_params=pltpu.CompilerParams(vmem_limit_bytes=VMEM_LIMIT),
        cost_estimate=pl.CostEstimate(flops=2 * tokens * D * 512, bytes_accessed=7 << 20, transcendentals=0),
        name="weight_grads",
    )(xt, *parts)


def rolled(v, axis, by):
    return lax.dynamic_slice_in_dim(jnp.concatenate([v, v], axis=axis), by, v.shape[axis], axis=axis)


def trade_inputs(xs, x_me, z_me, core):
    tokens = xs.shape[1]
    xt = jnp.swapaxes(xs, 1, 2).reshape(2, 8, 2, 2, 64, tokens)
    mine = lax.dynamic_index_in_dim(xt, core, 3, keepdims=False)
    theirs = lax.dynamic_index_in_dim(xt, 1 - core, 3, keepdims=False)
    both = jnp.concatenate([mine, swap_core(theirs)], axis=-1)

    def meant_for(step):
        x = lax.rem(x_me + step, 4)
        block = lax.dynamic_index_in_dim(both, x % 2, 0, keepdims=False)
        return lax.dynamic_index_in_dim(block, x // 2, 1, keepdims=False)

    blocks = [meant_for(0), shift_x(meant_for(1), 1), shift_x(meant_for(3), -1), shift_x(meant_for(2), 2)]
    return rolled(jnp.concatenate(blocks, axis=-1), 0, z_me).reshape(512, 8 * tokens)


def trade_slopes(ds, xl):
    own = lax.dynamic_index_in_dim(ds, xl, 0, keepdims=False)
    other = lax.dynamic_index_in_dim(ds, 1 - xl, 0, keepdims=False)
    parts = []
    for part in (own, shift_x(other, 1), shift_x(other, -1), shift_x(own, 2)):
        parts += [part, swap_core(part)]
    return parts


def plus_nothing(index, v):
    return index + (v[(0,) * v.ndim].astype(F32) * 0.0).astype(jnp.int32)


def pick(stacked, mask):
    shaped = mask.reshape((-1,) + (1,) * (stacked.ndim - 1))
    return jnp.sum(jnp.where(shaped, stacked, jnp.zeros_like(stacked)), axis=0)


def shards(master_old, first_old, second_old, layer_vectors, new_section, frozen, window_input, cotangent):
    y, xl, z_me, xh, core = (lax.axis_index(name) for name in AXES)
    section = y * 2 + xl
    x_me = xl + 2 * xh
    stay = new_section == section
    pair = new_section == jnp.bitwise_xor(section, 1)
    cross = jnp.where(section == 3, new_section == 4, (section == 4) & (new_section == 3))
    plane = stay | pair
    label = jnp.where(jnp.any(plane), jnp.sum(jnp.where(plane, new_section, 0)) & 1, xl)

    vec_pad = lambda mask: jnp.pad(pick(layer_vectors, mask), ((0, 13), (0, 0)))
    traded = swap_cross(jnp.concatenate([pick(master_old, cross).astype(BF16), vec_pad(cross)], axis=0))
    held = pick(master_old, plane).astype(BF16) + traded[:64]
    near = gather_plane(held, x_me, xh)
    far = [swap_core(m) for m in near]
    own_vec = pick(layer_vectors, plane) + traded[64:67]
    other_vec = swap_pair(own_vec)
    vec = jnp.where(label == 0, jnp.stack([own_vec, other_vec]), jnp.stack([other_vec, own_vec])).astype(F32)

    states = (master_old, first_old, second_old)
    send = lambda mask: jnp.stack([pick(s, mask) for s in states])
    soon, late = plus_nothing(new_section, near[0]), plus_nothing(new_section, near[-1])
    late_pair = late == jnp.bitwise_xor(section, 1)
    soon_cross = jnp.where(section == 3, soon == 4, (section == 4) & (soon == 3))
    moved = swap_pair(send(late_pair)) + swap_cross(send(soon_cross))

    tokens = window_input.shape[0] // 2
    rows = tokens // MICRO
    xs = jnp.zeros((2, tokens, D), BF16)
    ls = jnp.zeros((2, tokens, D), F32)
    ds = jnp.zeros((2, tokens, D), BF16)
    slopes = []
    ahead = behind = jnp.zeros((rows, D), BF16)

    def control(batch):
        active = (batch >= 0) & (batch < MICRO)
        slot = jnp.clip(batch, 0, MICRO - 1)
        parts = [active, y, slot, x_me, z_me, core, label, xl]
        return jnp.stack([jnp.asarray(p, jnp.int32) for p in parts])

    for tick in range(MICRO + 2 * STAGES - 2):
        f_stages = [s for s in range(STAGES) if 0 <= tick - s < MICRO]
        b_stages = [s for s in range(STAGES) if 0 <= tick - 2 * (STAGES - 1) + s < MICRO]
        if f_stages:
            act, xs, ls = forward_call(control(tick - y), near, far, window_input, ahead, vec, xs, ls)
            pairs = [(s, s + 1) for s in f_stages if s + 1 < STAGES]
            if pairs:
                ahead = lax.ppermute(act, "y", pairs)
        if b_stages:
            early = ()
            if tick == MICRO + 2 * STAGES - 3:
                xt = trade_inputs(xs, x_me, z_me, core)
                early = (xt, moved)
            back, ds = backward_call(
                control(tick - 2 * (STAGES - 1) + y), near, far, cotangent, behind, vec, xs, ls, ds, early
            )
            pairs = [(s, s - 1) for s in b_stages if s > 0]
            if pairs:
                behind = lax.ppermute(back, "y", pairs)
            done = tick - 2 * (STAGES - 1)
            if done >= 0:
                slopes.append(trade_slopes(ds[:, done * rows:(done + 1) * rows], xl))

    master, first_state, second_state = (pick(s, stay) + moved[i] for i, s in enumerate(states))

    parts = [slopes[m][i] for i in range(8) for m in range(MICRO)]
    grad_rows = ring_reduce(grad_call(xt, parts), shift_z, 4)
    learning = lax.dynamic_index_in_dim(frozen, section, 0, keepdims=False) == 0
    first_next = FIRST_DECAY * first_state + (1.0 - FIRST_DECAY) * grad_rows
    second_next = SECOND_DECAY * second_state + (1.0 - SECOND_DECAY) * grad_rows * grad_rows
    stepped = master - STEP_SIZE * (first_next / FIRST_CORRECTION) / (
        jnp.sqrt(second_next / SECOND_CORRECTION) + EPSILON
    )
    master_new = jnp.where(learning, stepped, master)
    first_new = jnp.where(learning, first_next, first_state)
    second_new = jnp.where(learning, second_next, second_state)
    return (master_new[None], first_new[None], second_new[None])


def solution(mesh):
    fine = jax.sharding.Mesh(mesh.devices.reshape(4, 2, 8, 2, 2), AXES)
    sec, rep = ("y", "xl"), ("z", "xh", "c")
    rows = P(sec, rep, None)
    in_specs = (rows, rows, rows, P(sec, None, None), P(sec), P(), P(rep, None), P(rep, None))
    return jax.shard_map(shards, mesh=fine, in_specs=in_specs, out_specs=(rows, rows, rows), check_vma=False)
```

```python
import functools
import jax
import jax.numpy as jnp
from jax import lax
from jax.experimental import pallas as pl
from jax.experimental.pallas import tpu as pltpu
from jax.sharding import PartitionSpec as P

BF16 = jnp.bfloat16
F32 = jnp.float32
D = 2048
NZ = 8
VMEM_LIMIT = 60 * 1024 * 1024
GELU_K = 0.7978845608028654


def weight_copies(near, far, w_scr, sems, z_me, x_me, core):
    copies = ([], [])
    for msgs, owner in ((near, core), (far, 1 - core)):
        head, tail = msgs[:9], msgs[9:]
        for dx, ref, zs in ((0, 0, 0), (-1, 1, 0), (1, 2, 0), (2, 3, 0), (2, 4, 4)):
            xh = lax.rem(x_me + dx + 4, 4) // 2
            count = 8 if ref < 3 else 4
            dst = w_scr.at[dx % 2, pl.ds(zs, count), xh, owner, pl.ds(32, 32), :]
            copies[dx % 2].append(pltpu.make_async_copy(tail[ref], dst, sems.at[dx % 2, NZ]))
    for slot in range(2):
        for at, dz in enumerate((0, -1, 1, -2, 2, -3, 3, 4)):
            z = lax.rem(z_me + dz + 8, 8)
            for msgs, owner in ((near, core), (far, 1 - core)):
                src = msgs[at].at[slot] if at < 7 else msgs[7 + slot].at[0]
                dst = w_scr.at[slot, z, :, owner, pl.ds(0, 32), :]
                copies[slot].append(pltpu.make_async_copy(src, dst, sems.at[slot, dz % 8]))
    return copies


def gelu_parts(u):
    square = u * u
    t = jnp.tanh(GELU_K * u * (1.0 + 0.044715 * square))
    return 0.5 * u * (1.0 + t), t, square


def gelu_slope(u, t, square):
    return 0.5 * (1.0 + t) + 0.5 * u * (1.0 - t * t) * (GELU_K * (1.0 + 3 * 0.044715 * square))


def norm_parts(z):
    center = z - jnp.mean(z, axis=-1, keepdims=True)
    spread = jnp.mean(center * center, axis=-1, keepdims=True)
    return center, lax.rsqrt(spread + 1e-5)


def issue(groups, first):
    def start(slot):
        for copy in groups[slot]:
            copy.start()

    @pl.when(first == 0)
    def _():
        start(0)
        start(1)

    @pl.when(first == 1)
    def _():
        start(1)
        start(0)


def wait_tails(w_scr, sems, slot):
    rows = w_scr.at[slot, :, :, :, pl.ds(32, 32), :]
    pltpu.make_async_copy(rows, rows, sems.at[slot, NZ]).wait()


def wait_heads(w_scr, sems, slot, k, z):
    rows = w_scr.at[slot, z, :, :, pl.ds(0, 32), :]
    pltpu.make_async_copy(rows, rows, sems.at[slot, k]).wait()


def forward_kernel(n_msgs, rows, ctl, *refs):
    near, far = refs[:n_msgs], refs[n_msgs:2 * n_msgs]
    window, recv, vec_in = refs[2 * n_msgs:2 * n_msgs + 3]
    act, xs, ls, w_scr, x_scr, lin_scr, vec, act_scr, sems, sem_x, sem_v, sem_o = refs[-12:]
    active, stage, batch, x_me, z_me, core, first, xl = (ctl[i] for i in range(8))

    @pl.when(active == 1)
    def _():
        groups = weight_copies(near, far, w_scr, sems, z_me, x_me, core)
        per_half = window.shape[0] // 2
        at = pl.multiple_of(batch * rows, rows)

        @pl.when(stage == 0)
        def _():
            src = window.at[pl.ds(pl.multiple_of(xl * per_half + batch * rows, rows), rows), :]
            pltpu.make_async_copy(src, x_scr.at[0], sem_x).start()

        @pl.when(stage != 0)
        def _():
            pltpu.make_async_copy(recv, x_scr.at[0], sem_x).start()

        vec_copy = pltpu.make_async_copy(vec_in, vec, sem_v)
        vec_copy.start()
        issue(groups, first)
        vec_copy.wait()
        pltpu.make_async_copy(recv, x_scr.at[0], sem_x).wait()
        outs = []
        for layer in range(2):
            slot = first ^ layer
            lin_scr[layer] = jnp.broadcast_to(vec[layer, 0:1, :], (rows, D))
            wait_tails(w_scr, sems, slot)

            @pl.loop(0, NZ)
            def _(k):
                z = lax.rem(z_me + k, NZ)
                wait_heads(w_scr, sems, slot, k, z)
                cols = pl.ds(pl.multiple_of(z * 256, 256), 256)
                lin_scr[layer] += jnp.dot(
                    x_scr[layer, :, cols], w_scr[slot, z].reshape(256, D), preferred_element_type=F32
                )

            lin = lin_scr[layer]
            center, scale = norm_parts(x_scr[layer].astype(F32) + gelu_parts(lin)[0])
            y = (center * scale * vec[layer, 1:2, :] + vec[layer, 2:3, :]).astype(BF16)
            if layer == 0:
                x_scr[1] = y
            else:
                act_scr[...] = y
                outs.append(pltpu.make_async_copy(act_scr, act, sem_v))
                outs[-1].start()
            for src, dst, n in ((x_scr, xs, 0), (lin_scr, ls, 1)):
                copy = pltpu.make_async_copy(src.at[layer], dst.at[layer, pl.ds(at, rows), :], sem_o.at[layer, n])
                copy.start()
                outs.append(copy)
        for copy in outs:
            copy.wait()


def backward_kernel(n_msgs, rows, ctl, *refs):
    near, far = refs[:n_msgs], refs[n_msgs:2 * n_msgs]
    cot, recv, vec_in, xs, ls = refs[2 * n_msgs:2 * n_msgs + 5]
    back, ds, w_scr, g_scr, x_scr, lin_scr, dz_scr, dl_scr, vec, back_scr, sems, sem_x, sem_v, sem_o = refs[-14:]
    active, stage, batch, x_me, z_me, core, first, xl = (ctl[i] for i in range(8))

    @pl.when(active == 1)
    def _():
        groups = weight_copies(near, far, w_scr, sems, z_me, x_me, core)
        per_half = cot.shape[0] // 2
        at = pl.multiple_of(batch * rows, rows)

        @pl.when(stage == 3)
        def _():
            src = cot.at[pl.ds(pl.multiple_of(xl * per_half + batch * rows, rows), rows), :]
            pltpu.make_async_copy(src, g_scr, sem_x.at[2, 0]).start()

        @pl.when(stage != 3)
        def _():
            pltpu.make_async_copy(recv, g_scr, sem_x.at[2, 0]).start()

        loads = {}
        for layer in (1, 0):
            loads[layer] = (
                pltpu.make_async_copy(xs.at[layer, pl.ds(at, rows), :], x_scr.at[layer], sem_x.at[layer, 0]),
                pltpu.make_async_copy(ls.at[layer, pl.ds(at, rows), :], lin_scr.at[layer], sem_x.at[layer, 1]),
            )
            for copy in loads[layer]:
                copy.start()
        vec_copy = pltpu.make_async_copy(vec_in, vec, sem_v)
        vec_copy.start()
        issue(groups, 1 - first)
        vec_copy.wait()
        pltpu.make_async_copy(recv, g_scr, sem_x.at[2, 0]).wait()
        outs = []
        for layer in (1, 0):
            slot = first ^ layer
            for copy in loads[layer]:
                copy.wait()
            lin = lin_scr[layer]
            gated, t, square = gelu_parts(lin)
            center, scale = norm_parts(x_scr[layer].astype(F32) + gated)
            unit = center * scale
            g = g_scr[...].astype(F32) * vec[layer, 1:2, :]
            dz = scale * (g - jnp.mean(g, axis=-1, keepdims=True) - unit * jnp.mean(g * unit, axis=-1, keepdims=True))
            dz_scr[...] = dz
            dl_scr[layer] = (dz * gelu_slope(lin, t, square)).astype(BF16)
            copy = pltpu.make_async_copy(dl_scr.at[layer], ds.at[layer, pl.ds(at, rows), :], sem_o.at[layer])
            copy.start()
            outs.append(copy)
            wait_tails(w_scr, sems, slot)

            @pl.loop(0, NZ)
            def _(k):
                z = lax.rem(z_me + k, NZ)
                wait_heads(w_scr, sems, slot, k, z)
                cols = pl.ds(pl.multiple_of(z * 256, 256), 256)

                def step():
                    down = lax.dot_general(
                        dl_scr[layer], w_scr[slot, z].reshape(256, D), (((1,), (1,)), ((), ())), preferred_element_type=F32
                    )
                    y = (dz_scr[:, cols] + down).astype(BF16)
                    if layer == 1:
                        g_scr[:, cols] = y
                    else:
                        back_scr[:, cols] = y

                if layer == 1:
                    step()
                else:
                    pl.when(stage != 0)(step)
        outs.append(pltpu.make_async_copy(back_scr, back, sem_v))
        outs[-1].start()
        for copy in outs:
            copy.wait()


def forward_call(ctl, near, far, window, recv, vec, stash):
    rows = recv.shape[0]
    tokens = window.shape[0] // 2
    n = len(near)
    any_spec = pl.BlockSpec(memory_space=pl.ANY)
    return pl.pallas_call(
        functools.partial(forward_kernel, n, rows),
        out_shape=(
            jax.ShapeDtypeStruct((rows, D), BF16),
            jax.ShapeDtypeStruct((2, tokens, D), BF16),
            jax.ShapeDtypeStruct((2, tokens, D), F32),
        ),
        in_specs=[pl.BlockSpec(memory_space=pltpu.SMEM)] + [any_spec] * (2 * n + 3 + len(stash)),
        out_specs=(any_spec, any_spec, any_spec),
        scratch_shapes=[
            pltpu.VMEM((2, 8, 2, 2, 64, D), BF16),
            pltpu.VMEM((2, rows, D), BF16),
            pltpu.VMEM((2, rows, D), F32),
            pltpu.VMEM(vec.shape, F32),
            pltpu.VMEM((rows, D), BF16),
            pltpu.SemaphoreType.DMA((2, NZ + 1)),
            pltpu.SemaphoreType.DMA,
            pltpu.SemaphoreType.DMA,
            pltpu.SemaphoreType.DMA((2, 2)),
        ],
        input_output_aliases={2 * n + 4 + i: 1 + i for i in range(len(stash))},
        compiler_params=pltpu.CompilerParams(vmem_limit_bytes=VMEM_LIMIT),
        cost_estimate=pl.CostEstimate(flops=4 * rows * D * D, bytes_accessed=4 * D * D, transcendentals=2 * rows * D),
        name="forward_tick",
    )(ctl, *near, *far, window, recv, vec, *stash)


def backward_call(ctl, near, far, cot, recv, vec, xs, ls, stash, early=()):
    rows = recv.shape[0]
    n = len(near)
    any_spec = pl.BlockSpec(memory_space=pl.ANY)
    return pl.pallas_call(
        functools.partial(backward_kernel, n, rows),
        out_shape=(jax.ShapeDtypeStruct((rows, D), BF16), jax.ShapeDtypeStruct(xs.shape, BF16)),
        in_specs=[pl.BlockSpec(memory_space=pltpu.SMEM)] + [any_spec] * (2 * n + 5 + len(stash) + len(early)),
        out_specs=(any_spec, any_spec),
        scratch_shapes=[
            pltpu.VMEM((2, 8, 2, 2, 64, D), BF16),
            pltpu.VMEM((rows, D), BF16),
            pltpu.VMEM((2, rows, D), BF16),
            pltpu.VMEM((2, rows, D), F32),
            pltpu.VMEM((rows, D), F32),
            pltpu.VMEM((2, rows, D), BF16),
            pltpu.VMEM(vec.shape, F32),
            pltpu.VMEM((rows, D), BF16),
            pltpu.SemaphoreType.DMA((2, NZ + 1)),
            pltpu.SemaphoreType.DMA((3, 2)),
            pltpu.SemaphoreType.DMA,
            pltpu.SemaphoreType.DMA((2,)),
        ],
        input_output_aliases={2 * n + 6: 1} if stash else {},
        compiler_params=pltpu.CompilerParams(vmem_limit_bytes=VMEM_LIMIT),
        cost_estimate=pl.CostEstimate(flops=4 * rows * D * D, bytes_accessed=4 * D * D, transcendentals=2 * rows * D),
        name="backward_tick",
    )(ctl, *near, *far, cot, recv, vec, xs, ls, *stash, *early)

AXES = ("y", "xl", "z", "xh", "c")
MICRO = 2
STAGES = 4

FIRST_DECAY = 0.9
SECOND_DECAY = 0.999
STEP_SIZE = 0.01
EPSILON = 1e-08
FIRST_CORRECTION = 1.0 - 0.9**10
SECOND_CORRECTION = 1.0 - 0.999**10


def shift_x(v, by):
    place = lambda x: (x & 1) * 2 + (x >> 1)
    return lax.ppermute(v, ("xl", "xh"), [(place(x), place((x + by) % 4)) for x in range(4)])


def shift_z(v, by):
    return lax.ppermute(v, "z", [(z, (z + by) % 8) for z in range(8)])


def swap_core(v):
    return lax.ppermute(v, "c", [(0, 1), (1, 0)])


def swap_pair(v):
    return lax.ppermute(v, "xl", [(0, 1), (1, 0)])


def swap_cross(v):
    return lax.ppermute(v, ("y", "xl"), [(3, 4), (4, 3)])


def ring_gather(v, shift, steps):
    right = left = v
    out = []
    for _ in range(1, steps):
        right, left = shift(right, 1), shift(left, -1)
        out += [right, left]
    half = v.shape[0] // 2
    return out + [shift(right[:half], 1), shift(left[half:], -1)]


def place_kernel(n, at, *refs):
    blocks, out, sem = refs[:n], refs[n], refs[n + 1]
    for i, block in enumerate(blocks):
        pltpu.make_async_copy(block, out.at[at[i]], sem).start()
    pltpu.make_async_copy(out, out, sem).wait()


def place(blocks, at):
    n = len(blocks)
    return pl.pallas_call(
        functools.partial(place_kernel, n),
        out_shape=jax.ShapeDtypeStruct((n,) + blocks[0].shape, blocks[0].dtype),
        in_specs=[pl.BlockSpec(memory_space=pltpu.SMEM)] + [pl.BlockSpec(memory_space=pl.ANY)] * n,
        out_specs=pl.BlockSpec(memory_space=pl.ANY),
        scratch_shapes=[pltpu.SemaphoreType.DMA],
        compiler_params=pltpu.CompilerParams(vmem_limit_bytes=VMEM_LIMIT),
        cost_estimate=pl.CostEstimate(flops=0, bytes_accessed=2 * n * blocks[0].size * 2, transcendentals=0),
        name="place_blocks",
    )(at, *blocks)


def gather_plane(rows, x_me, z_me):
    a, b = rows[:32], rows[32:]
    x_steps, z_steps = (0, 1, -1, 2), (0, 1, -1, 2, -2, 3, -3, 4)
    along_x = [a] + [shift_x(a, k) for k in x_steps[1:]]
    along_z = [b] + [shift_z(b, k) for k in z_steps[1:]]
    x_from = lax.rem(x_me + 4 - jnp.array(x_steps, jnp.int32), 4)
    parity = jnp.array([k % 2 for k in x_steps], jnp.int32)
    heads = place(along_x, parity * 2 + x_from // 2).reshape(2, 2, 32, D)
    z_from = lax.rem(z_me + 8 - jnp.array(z_steps, jnp.int32), 8)
    tails = place(along_z, z_from)
    return [heads] + ring_gather(heads, shift_z, 4) + [tails] + ring_gather(tails, shift_x, 2)


def add_rounded(a, b):
    return (a.astype(F32) + b.astype(F32)).astype(BF16)


def ring_reduce(chunks, shift, steps):
    half = chunks.shape[1] // 2
    far = chunks[steps]
    right, left = shift(far[:half], 1), shift(far[half:], -1)
    for k in range(steps - 1, 0, -1):
        up, down = chunks[k], chunks[2 * steps - k]
        if k == steps - 1:
            right = jnp.concatenate([add_rounded(up[:half], right), up[half:]], axis=0)
            left = jnp.concatenate([down[:half], add_rounded(down[half:], left)], axis=0)
        else:
            right, left = add_rounded(up, right), add_rounded(down, left)
        right, left = shift(right, 1), shift(left, -1)
    return chunks[0].astype(F32) + right.astype(F32) + left.astype(F32)


def grad_kernel(n_parts, xt, *refs):
    parts, g, d_scr, sem = refs[:n_parts], refs[n_parts], refs[n_parts + 1], refs[n_parts + 2]
    size = parts[0].shape[0]
    for i, part in enumerate(parts):
        pltpu.make_async_copy(part, d_scr.at[pl.ds(i * size, size), :], sem).start()
    pltpu.make_async_copy(d_scr, d_scr, sem).wait()

    @pl.loop(0, D // 256)
    def _(n):
        cols = pl.ds(pl.multiple_of(n * 256, 256), 256)
        part = jnp.dot(xt[...], d_scr[:, cols], preferred_element_type=F32).astype(BF16)
        g[:, :, cols] = part.reshape(8, 64, 256)


def grad_call(xt, parts):
    tokens = xt.shape[1]
    return pl.pallas_call(
        functools.partial(grad_kernel, len(parts)),
        out_shape=jax.ShapeDtypeStruct((8, 64, D), BF16),
        in_specs=[pl.BlockSpec(memory_space=pltpu.VMEM)] + [pl.BlockSpec(memory_space=pl.ANY)] * len(parts),
        out_specs=pl.BlockSpec(memory_space=pltpu.VMEM),
        scratch_shapes=[pltpu.VMEM((tokens, D), BF16), pltpu.SemaphoreType.DMA],
        compiler_params=pltpu.CompilerParams(vmem_limit_bytes=VMEM_LIMIT),
        cost_estimate=pl.CostEstimate(flops=2 * tokens * D * 512, bytes_accessed=7 << 20, transcendentals=0),
        name="weight_grads",
    )(xt, *parts)


def rolled(v, axis, by):
    return lax.dynamic_slice_in_dim(jnp.concatenate([v, v], axis=axis), by, v.shape[axis], axis=axis)


def trade_inputs(xs, x_me, z_me, core):
    tokens = xs.shape[1]
    xt = jnp.swapaxes(xs, 1, 2).reshape(2, 8, 2, 2, 64, tokens)
    mine = lax.dynamic_index_in_dim(xt, core, 3, keepdims=False)
    theirs = lax.dynamic_index_in_dim(xt, 1 - core, 3, keepdims=False)
    both = jnp.concatenate([mine, swap_core(theirs)], axis=-1)

    def meant_for(step):
        x = lax.rem(x_me + step, 4)
        block = lax.dynamic_index_in_dim(both, x % 2, 0, keepdims=False)
        return lax.dynamic_index_in_dim(block, x // 2, 1, keepdims=False)

    blocks = [meant_for(0), shift_x(meant_for(1), 1), shift_x(meant_for(3), -1), shift_x(meant_for(2), 2)]
    return rolled(jnp.concatenate(blocks, axis=-1), 0, z_me).reshape(512, 8 * tokens)


def trade_slopes(ds, xl):
    own = lax.dynamic_index_in_dim(ds, xl, 0, keepdims=False)
    other = lax.dynamic_index_in_dim(ds, 1 - xl, 0, keepdims=False)
    parts = []
    for part in (own, shift_x(other, 1), shift_x(other, -1), shift_x(own, 2)):
        parts += [part, swap_core(part)]
    return parts


def plus_nothing(index, v):
    return index + (v[(0,) * v.ndim].astype(F32) * 0.0).astype(jnp.int32)


def shards(master_old, first_old, second_old, layer_vectors, new_section, frozen, window_input, cotangent):
    y, xl, z_me, xh, core = (lax.axis_index(name) for name in AXES)
    section = y * 2 + xl
    x_me = xl + 2 * xh
    slot = (new_section[1] >= 0).astype(jnp.int32)
    goal = lax.dynamic_index_in_dim(new_section, slot, 0, keepdims=False)
    in_plane = goal // 2 == y
    label = jnp.where(in_plane, goal & 1, xl)

    held_of = lambda v: lax.dynamic_index_in_dim(v, slot, 0, keepdims=False)
    own_rows, own_vec = held_of(master_old).astype(BF16), held_of(layer_vectors)
    traded = swap_cross(jnp.concatenate([own_rows, jnp.pad(own_vec, ((0, 13), (0, 0)))], axis=0))
    near = gather_plane(jnp.where(in_plane, own_rows, traded[:64]), x_me, z_me)
    far = [swap_core(m) for m in near]
    own_vec = jnp.where(in_plane, own_vec, traded[64:67])
    other_vec = swap_pair(own_vec)
    vec = jnp.where(label == 0, jnp.stack([own_vec, other_vec]), jnp.stack([other_vec, own_vec])).astype(F32)

    tokens = window_input.shape[0] // 2
    rows = tokens // MICRO
    stash = slope_stash = ()
    states = (master_old, first_old, second_old)
    slopes = []
    ahead = behind = jnp.zeros((rows, D), BF16)

    def control(batch):
        active = (batch >= 0) & (batch < MICRO)
        slot = jnp.clip(batch, 0, MICRO - 1)
        parts = [active, y, slot, x_me, z_me, core, label, xl]
        return jnp.stack([jnp.asarray(p, jnp.int32) for p in parts])

    for tick in range(MICRO + 2 * STAGES - 2):
        f_stages = [s for s in range(STAGES) if 0 <= tick - s < MICRO]
        b_stages = [s for s in range(STAGES) if 0 <= tick - 2 * (STAGES - 1) + s < MICRO]
        if f_stages:
            act, xs, ls = forward_call(control(tick - y), near, far, window_input, ahead, vec, stash)
            stash = (xs, ls)
            pairs = [(s, s + 1) for s in f_stages if s + 1 < STAGES]
            if pairs:
                ahead = lax.ppermute(act, "y", pairs)
                if tick == 0:
                    held = jnp.stack([lax.dynamic_index_in_dim(s, plus_nothing(slot, ahead), 0, keepdims=False) for s in states])
                    from_pair, from_cross = swap_pair(held), swap_cross(held)
        if b_stages:
            early = ()
            if tick == MICRO + 2 * STAGES - 4:
                xt = trade_inputs(xs, x_me, z_me, core)
                early = (xt,)
            back, ds = backward_call(
                control(tick - 2 * (STAGES - 1) + y), near, far, cotangent, behind, vec, xs, ls, slope_stash, early
            )
            slope_stash = (ds,)
            pairs = [(s, s - 1) for s in b_stages if s > 0]
            if pairs:
                behind = lax.ppermute(back, "y", pairs)
            done = tick - 2 * (STAGES - 1)
            if done >= 0:
                slopes.append(trade_slopes(ds[:, done * rows:(done + 1) * rows], xl))

    kept = jnp.where(goal == section, held, jnp.where(in_plane, from_pair, from_cross))
    master, first_state, second_state = kept[0], kept[1], kept[2]

    parts = [slopes[m][i] for i in range(8) for m in range(MICRO)]
    grad_rows = ring_reduce(grad_call(xt, parts), shift_z, 4)
    learning = lax.dynamic_index_in_dim(frozen, section, 0, keepdims=False) == 0
    first_next = FIRST_DECAY * first_state + (1.0 - FIRST_DECAY) * grad_rows
    second_next = SECOND_DECAY * second_state + (1.0 - SECOND_DECAY) * grad_rows * grad_rows
    stepped = master - STEP_SIZE * (first_next / FIRST_CORRECTION) / (
        jnp.sqrt(second_next / SECOND_CORRECTION) + EPSILON
    )
    master_new = jnp.where(learning, stepped, master)
    first_new = jnp.where(learning, first_next, first_state)
    second_new = jnp.where(learning, second_next, second_state)
    return (master_new[None], first_new[None], second_new[None])


def solution(mesh):
    fine = jax.sharding.Mesh(mesh.devices.reshape(4, 2, 8, 2, 2), AXES)
    sec, rep = ("y", "xl"), ("z", "xh", "c")
    rows = P(sec, rep, None)
    in_specs = (rows, rows, rows, P(sec, None, None), P(sec), P(), P(rep, None), P(rep, None))
    return jax.shard_map(shards, mesh=fine, in_specs=in_specs, out_specs=(rows, rows, rows), check_vma=False)
```

```python
import functools
import jax
import jax.numpy as jnp
from jax import lax
from jax.experimental import pallas as pl
from jax.experimental.pallas import tpu as pltpu
from jax.sharding import PartitionSpec as P

BF16 = jnp.bfloat16
F32 = jnp.float32
D = 2048
NQ = 4
VMEM_LIMIT = 60 * 1024 * 1024
GELU_K = 0.7978845608028654


def weight_copies(near, far, w_scr, sems, x_me, core):
    copies = ([], [])
    for msgs, owner in ((near, core), (far, 1 - core)):
        for dx, ref, zs in ((0, 1, 0), (-1, 2, 0), (1, 3, 0), (2, 4, 0), (2, 5, 4)):
            xh = lax.rem(x_me + dx + 4, 4) // 2
            count = 8 if ref < 4 else 4
            dst = w_scr.at[dx % 2, pl.ds(zs, count), xh, owner, pl.ds(32, 32), :]
            copies[dx % 2].append(pltpu.make_async_copy(msgs[ref], dst, sems.at[dx % 2, NQ]))
    for slot in range(2):
        for q in range(NQ):
            for msgs, owner in ((near, core), (far, 1 - core)):
                src = msgs[0].at[pl.ds(2 * q, 2), slot]
                dst = w_scr.at[slot, pl.ds(2 * q, 2), :, owner, pl.ds(0, 32), :]
                copies[slot].append(pltpu.make_async_copy(src, dst, sems.at[slot, q]))
    return copies


def gelu_parts(u):
    square = u * u
    t = jnp.tanh(GELU_K * u * (1.0 + 0.044715 * square))
    return 0.5 * u * (1.0 + t), t, square


def gelu_slope(u, t, square):
    return 0.5 * (1.0 + t) + 0.5 * u * (1.0 - t * t) * (GELU_K * (1.0 + 3 * 0.044715 * square))


def norm_parts(z):
    center = z - jnp.mean(z, axis=-1, keepdims=True)
    spread = jnp.mean(center * center, axis=-1, keepdims=True)
    return center, lax.rsqrt(spread + 1e-5)


def issue(groups, first):
    def start(slot):
        for copy in groups[slot]:
            copy.start()

    @pl.when(first == 0)
    def _():
        start(0)
        start(1)

    @pl.when(first == 1)
    def _():
        start(1)
        start(0)


def wait_tails(w_scr, sems, slot):
    rows = w_scr.at[slot, :, :, :, pl.ds(32, 32), :]
    pltpu.make_async_copy(rows, rows, sems.at[slot, NQ]).wait()


def wait_heads(w_scr, sems, slot, q):
    rows = w_scr.at[slot, pl.ds(2 * q, 2), :, :, pl.ds(0, 32), :]
    pltpu.make_async_copy(rows, rows, sems.at[slot, q]).wait()


def forward_kernel(n_msgs, rows, ctl, *refs):
    near, far = refs[:n_msgs], refs[n_msgs:2 * n_msgs]
    window, recv, vec_in = refs[2 * n_msgs:2 * n_msgs + 3]
    act, xs, ls, w_scr, x_scr, lin_scr, vec, act_scr, sems, sem_x, sem_v, sem_o = refs[-12:]
    active, stage, batch, x_me, core, first, xl = (ctl[i] for i in range(7))

    @pl.when(active == 1)
    def _():
        groups = weight_copies(near, far, w_scr, sems, x_me, core)
        per_half = window.shape[0] // 2
        at = pl.multiple_of(batch * rows, rows)

        @pl.when(stage == 0)
        def _():
            src = window.at[pl.ds(pl.multiple_of(xl * per_half + batch * rows, rows), rows), :]
            pltpu.make_async_copy(src, x_scr.at[0], sem_x).start()

        @pl.when(stage != 0)
        def _():
            pltpu.make_async_copy(recv, x_scr.at[0], sem_x).start()

        vec_copy = pltpu.make_async_copy(vec_in, vec, sem_v)
        vec_copy.start()
        issue(groups, first)
        vec_copy.wait()
        pltpu.make_async_copy(recv, x_scr.at[0], sem_x).wait()
        outs = []
        for layer in range(2):
            slot = first ^ layer
            lin_scr[layer] = jnp.broadcast_to(vec[layer, 0:1, :], (rows, D))
            wait_tails(w_scr, sems, slot)

            @pl.loop(0, NQ)
            def _(q):
                wait_heads(w_scr, sems, slot, q)
                cols = pl.ds(pl.multiple_of(q * 512, 512), 512)
                lin_scr[layer] += jnp.dot(
                    x_scr[layer, :, cols], w_scr[slot, pl.ds(2 * q, 2)].reshape(512, D), preferred_element_type=F32
                )

            lin = lin_scr[layer]
            center, scale = norm_parts(x_scr[layer].astype(F32) + gelu_parts(lin)[0])
            y = (center * scale * vec[layer, 1:2, :] + vec[layer, 2:3, :]).astype(BF16)
            if layer == 0:
                x_scr[1] = y
            else:
                act_scr[...] = y
                outs.append(pltpu.make_async_copy(act_scr, act, sem_v))
                outs[-1].start()
            for src, dst, n in ((x_scr, xs, 0), (lin_scr, ls, 1)):
                copy = pltpu.make_async_copy(src.at[layer], dst.at[layer, pl.ds(at, rows), :], sem_o.at[layer, n])
                copy.start()
                outs.append(copy)
        for copy in outs:
            copy.wait()


def backward_kernel(n_msgs, rows, ctl, *refs):
    near, far = refs[:n_msgs], refs[n_msgs:2 * n_msgs]
    cot, recv, vec_in, xs, ls = refs[2 * n_msgs:2 * n_msgs + 5]
    back, own_0, own_1, other_0, other_1 = refs[-17:-12]
    w_scr, g_scr, x_scr, lin_scr, dz_scr, dl_scr, vec, back_scr, sems, sem_x, sem_v, sem_o = refs[-12:]
    active, stage, batch, x_me, core, first, xl = (ctl[i] for i in range(7))

    @pl.when(active == 1)
    def _():
        groups = weight_copies(near, far, w_scr, sems, x_me, core)
        per_half = cot.shape[0] // 2
        at = pl.multiple_of(batch * rows, rows)

        @pl.when(stage == 3)
        def _():
            src = cot.at[pl.ds(pl.multiple_of(xl * per_half + batch * rows, rows), rows), :]
            pltpu.make_async_copy(src, g_scr, sem_x.at[2, 0]).start()

        @pl.when(stage != 3)
        def _():
            pltpu.make_async_copy(recv, g_scr, sem_x.at[2, 0]).start()

        loads = {}
        for layer in (1, 0):
            loads[layer] = (
                pltpu.make_async_copy(xs.at[layer, pl.ds(at, rows), :], x_scr.at[layer], sem_x.at[layer, 0]),
                pltpu.make_async_copy(ls.at[layer, pl.ds(at, rows), :], lin_scr.at[layer], sem_x.at[layer, 1]),
            )
            for copy in loads[layer]:
                copy.start()
        vec_copy = pltpu.make_async_copy(vec_in, vec, sem_v)
        vec_copy.start()
        issue(groups, 1 - first)
        vec_copy.wait()
        pltpu.make_async_copy(recv, g_scr, sem_x.at[2, 0]).wait()
        outs = []
        for layer in (1, 0):
            slot = first ^ layer
            for copy in loads[layer]:
                copy.wait()
            lin = lin_scr[layer]
            gated, t, square = gelu_parts(lin)
            center, scale = norm_parts(x_scr[layer].astype(F32) + gated)
            unit = center * scale
            g = g_scr[...].astype(F32) * vec[layer, 1:2, :]
            dz = scale * (g - jnp.mean(g, axis=-1, keepdims=True) - unit * jnp.mean(g * unit, axis=-1, keepdims=True))
            dz_scr[...] = dz
            dl_scr[layer] = (dz * gelu_slope(lin, t, square)).astype(BF16)
            for is_own, pair in ((1, (own_0, own_1)), (0, (other_0, other_1))):
                for m, dst in enumerate(pair):

                    @pl.when((batch == m) & ((xl == layer) == (is_own == 1)))
                    def _():
                        pltpu.make_async_copy(dl_scr.at[layer], dst, sem_o.at[layer]).start()

            outs.append(pltpu.make_async_copy(dl_scr.at[layer], own_0, sem_o.at[layer]))
            wait_tails(w_scr, sems, slot)

            @pl.loop(0, NQ)
            def _(q):
                wait_heads(w_scr, sems, slot, q)
                cols = pl.ds(pl.multiple_of(q * 512, 512), 512)

                def step():
                    down = lax.dot_general(
                        dl_scr[layer], w_scr[slot, pl.ds(2 * q, 2)].reshape(512, D), (((1,), (1,)), ((), ())), preferred_element_type=F32
                    )
                    y = (dz_scr[:, cols] + down).astype(BF16)
                    if layer == 1:
                        g_scr[:, cols] = y
                    else:
                        back_scr[:, cols] = y

                if layer == 1:
                    step()
                else:
                    pl.when(stage != 0)(step)
        outs.append(pltpu.make_async_copy(back_scr, back, sem_v))
        outs[-1].start()
        for copy in outs:
            copy.wait()


def forward_call(ctl, near, far, window, recv, vec, stash):
    rows = recv.shape[0]
    tokens = window.shape[0] // 2
    n = len(near)
    any_spec = pl.BlockSpec(memory_space=pl.ANY)
    return pl.pallas_call(
        functools.partial(forward_kernel, n, rows),
        out_shape=(
            jax.ShapeDtypeStruct((rows, D), BF16),
            jax.ShapeDtypeStruct((2, tokens, D), BF16),
            jax.ShapeDtypeStruct((2, tokens, D), F32),
        ),
        in_specs=[pl.BlockSpec(memory_space=pltpu.SMEM)] + [any_spec] * (2 * n + 3 + len(stash)),
        out_specs=(any_spec, any_spec, any_spec),
        scratch_shapes=[
            pltpu.VMEM((2, 8, 2, 2, 64, D), BF16),
            pltpu.VMEM((2, rows, D), BF16),
            pltpu.VMEM((2, rows, D), F32),
            pltpu.VMEM(vec.shape, F32),
            pltpu.VMEM((rows, D), BF16),
            pltpu.SemaphoreType.DMA((2, NQ + 1)),
            pltpu.SemaphoreType.DMA,
            pltpu.SemaphoreType.DMA,
            pltpu.SemaphoreType.DMA((2, 2)),
        ],
        input_output_aliases={2 * n + 4 + i: 1 + i for i in range(len(stash))},
        compiler_params=pltpu.CompilerParams(vmem_limit_bytes=VMEM_LIMIT),
        cost_estimate=pl.CostEstimate(flops=4 * rows * D * D, bytes_accessed=4 * D * D, transcendentals=2 * rows * D),
        name="forward_tick",
    )(ctl, *near, *far, window, recv, vec, *stash)


def backward_call(ctl, near, far, cot, recv, vec, xs, ls, stash, early=()):
    rows = recv.shape[0]
    n = len(near)
    any_spec = pl.BlockSpec(memory_space=pl.ANY)
    return pl.pallas_call(
        functools.partial(backward_kernel, n, rows),
        out_shape=(jax.ShapeDtypeStruct((rows, D), BF16),) * 5,
        in_specs=[pl.BlockSpec(memory_space=pltpu.SMEM)] + [any_spec] * (2 * n + 5 + len(stash) + len(early)),
        out_specs=(any_spec,) * 5,
        scratch_shapes=[
            pltpu.VMEM((2, 8, 2, 2, 64, D), BF16),
            pltpu.VMEM((rows, D), BF16),
            pltpu.VMEM((2, rows, D), BF16),
            pltpu.VMEM((2, rows, D), F32),
            pltpu.VMEM((rows, D), F32),
            pltpu.VMEM((2, rows, D), BF16),
            pltpu.VMEM(vec.shape, F32),
            pltpu.VMEM((rows, D), BF16),
            pltpu.SemaphoreType.DMA((2, NQ + 1)),
            pltpu.SemaphoreType.DMA((3, 2)),
            pltpu.SemaphoreType.DMA,
            pltpu.SemaphoreType.DMA((2,)),
        ],
        input_output_aliases={2 * n + 6 + i: 1 + i for i in range(len(stash))},
        compiler_params=pltpu.CompilerParams(vmem_limit_bytes=VMEM_LIMIT),
        cost_estimate=pl.CostEstimate(flops=4 * rows * D * D, bytes_accessed=4 * D * D, transcendentals=2 * rows * D),
        name="backward_tick",
    )(ctl, *near, *far, cot, recv, vec, xs, ls, *stash, *early)

AXES = ("y", "xl", "z", "xh", "c")
MICRO = 2
STAGES = 4

FIRST_DECAY = 0.9
SECOND_DECAY = 0.999
STEP_SIZE = 0.01
EPSILON = 1e-08
FIRST_CORRECTION = 1.0 - 0.9**10
SECOND_CORRECTION = 1.0 - 0.999**10


def shift_x(v, by):
    place = lambda x: (x & 1) * 2 + (x >> 1)
    return lax.ppermute(v, ("xl", "xh"), [(place(x), place((x + by) % 4)) for x in range(4)])


def shift_z(v, by):
    return lax.ppermute(v, "z", [(z, (z + by) % 8) for z in range(8)])


def swap_core(v):
    return lax.ppermute(v, "c", [(0, 1), (1, 0)])


def swap_pair(v):
    return lax.ppermute(v, "xl", [(0, 1), (1, 0)])


def swap_cross(v):
    return lax.ppermute(v, ("y", "xl"), [(3, 4), (4, 3)])


def ring_gather(v, shift, steps):
    right = left = v
    out = []
    for _ in range(1, steps):
        right, left = shift(right, 1), shift(left, -1)
        out += [right, left]
    half = v.shape[0] // 2
    return out + [shift(right[:half], 1), shift(left[half:], -1)]


def place_kernel(at, *refs):
    blocks, out, sem = refs[:9], refs[9], refs[10]
    for i, block in enumerate(blocks[:7]):
        pltpu.make_async_copy(block, out.at[at[i]], sem).start()
    for i, block in enumerate(blocks[7:]):
        pltpu.make_async_copy(block, out.at[at[7], pl.ds(16 * i, 16), :], sem).start()
    pltpu.make_async_copy(out, out, sem).wait()


def place(blocks, at):
    return pl.pallas_call(
        place_kernel,
        out_shape=jax.ShapeDtypeStruct((8, 32, D), BF16),
        in_specs=[pl.BlockSpec(memory_space=pltpu.SMEM)] + [pl.BlockSpec(memory_space=pl.ANY)] * 9,
        out_specs=pl.BlockSpec(memory_space=pltpu.VMEM),
        scratch_shapes=[pltpu.SemaphoreType.DMA],
        compiler_params=pltpu.CompilerParams(vmem_limit_bytes=VMEM_LIMIT),
        cost_estimate=pl.CostEstimate(flops=0, bytes_accessed=2 << 20, transcendentals=0),
        name="place_blocks",
    )(at, *blocks)


def gather_plane(rows, x_me, xh, z_me):
    a, b = rows[:32], rows[32:]
    before, after, across = shift_x(a, 1), shift_x(a, -1), shift_x(a, 2)
    own_first, before_first = xh == 0, lax.rem(x_me + 3, 4) < 2
    heads = jnp.stack(
        [
            jnp.stack([jnp.where(own_first, a, across), jnp.where(own_first, across, a)]),
            jnp.stack([jnp.where(before_first, before, after), jnp.where(before_first, after, before)]),
        ]
    )
    heads = lax.all_gather(heads, "z", axis=0)
    z_from = lax.rem(z_me + 8 + jnp.array((0, -1, 1, -2, 2, -3, 3, 4), jnp.int32), 8)
    tails = place([b] + ring_gather(b, shift_z, 4), z_from)
    return [heads, tails] + ring_gather(tails, shift_x, 2)


def add_rounded(a, b):
    return (a.astype(F32) + b.astype(F32)).astype(BF16)


def ring_reduce(chunks, shift, steps):
    half = chunks.shape[1] // 2
    far = chunks[steps]
    right, left = shift(far[:half], 1), shift(far[half:], -1)
    for k in range(steps - 1, 0, -1):
        up, down = chunks[k], chunks[2 * steps - k]
        if k == steps - 1:
            right = jnp.concatenate([add_rounded(up[:half], right), up[half:]], axis=0)
            left = jnp.concatenate([down[:half], add_rounded(down[half:], left)], axis=0)
        else:
            right, left = add_rounded(up, right), add_rounded(down, left)
        right, left = shift(right, 1), shift(left, -1)
    return chunks[0].astype(F32) + right.astype(F32) + left.astype(F32)


def grad_kernel(n_parts, xt, *refs):
    parts, g, d_scr, sem = refs[:n_parts], refs[n_parts], refs[n_parts + 1], refs[n_parts + 2]
    size = parts[0].shape[0]
    for i, part in enumerate(parts):
        pltpu.make_async_copy(part, d_scr.at[pl.ds(i * size, size), :], sem).start()
    pltpu.make_async_copy(d_scr, d_scr, sem).wait()

    @pl.loop(0, D // 256)
    def _(n):
        cols = pl.ds(pl.multiple_of(n * 256, 256), 256)
        part = jnp.dot(xt[...], d_scr[:, cols], preferred_element_type=F32).astype(BF16)
        g[:, :, cols] = part.reshape(8, 64, 256)


def grad_call(xt, parts):
    tokens = xt.shape[1]
    return pl.pallas_call(
        functools.partial(grad_kernel, len(parts)),
        out_shape=jax.ShapeDtypeStruct((8, 64, D), BF16),
        in_specs=[pl.BlockSpec(memory_space=pltpu.VMEM)] + [pl.BlockSpec(memory_space=pl.ANY)] * len(parts),
        out_specs=pl.BlockSpec(memory_space=pltpu.VMEM),
        scratch_shapes=[pltpu.VMEM((tokens, D), BF16), pltpu.SemaphoreType.DMA],
        compiler_params=pltpu.CompilerParams(vmem_limit_bytes=VMEM_LIMIT),
        cost_estimate=pl.CostEstimate(flops=2 * tokens * D * 512, bytes_accessed=7 << 20, transcendentals=0),
        name="weight_grads",
    )(xt, *parts)


def rolled(v, axis, by):
    return lax.dynamic_slice_in_dim(jnp.concatenate([v, v], axis=axis), by, v.shape[axis], axis=axis)


def trade_inputs(xs, x_me, z_me, core):
    tokens = xs.shape[1]
    xt = jnp.swapaxes(xs, 1, 2).reshape(2, 8, 2, 2, 64, tokens)
    mine = lax.dynamic_index_in_dim(xt, core, 3, keepdims=False)
    theirs = lax.dynamic_index_in_dim(xt, 1 - core, 3, keepdims=False)
    both = jnp.concatenate([mine, swap_core(theirs)], axis=-1)

    def meant_for(step):
        x = lax.rem(x_me + step, 4)
        block = lax.dynamic_index_in_dim(both, x % 2, 0, keepdims=False)
        return lax.dynamic_index_in_dim(block, x // 2, 1, keepdims=False)

    blocks = [meant_for(0), shift_x(meant_for(1), 1), shift_x(meant_for(3), -1), shift_x(meant_for(2), 2)]
    return rolled(jnp.concatenate(blocks, axis=-1), 0, z_me).reshape(512, 8 * tokens)


def trade_slopes(own, other):
    parts = []
    for part in (own, shift_x(other, 1), shift_x(other, -1), shift_x(own, 2)):
        parts += [part, swap_core(part)]
    return parts


def plus_nothing(index, v):
    return index + (v[(0,) * v.ndim].astype(F32) * 0.0).astype(jnp.int32)


def shards(master_old, first_old, second_old, layer_vectors, new_section, frozen, window_input, cotangent):
    y, xl, z_me, xh, core = (lax.axis_index(name) for name in AXES)
    section = y * 2 + xl
    x_me = xl + 2 * xh
    slot = (new_section[1] >= 0).astype(jnp.int32)
    goal = lax.dynamic_index_in_dim(new_section, slot, 0, keepdims=False)
    in_plane = goal // 2 == y
    label = jnp.where(in_plane, goal & 1, xl)

    held_of = lambda v: lax.dynamic_index_in_dim(v, slot, 0, keepdims=False)
    own_rows, own_vec = held_of(master_old).astype(BF16), held_of(layer_vectors)
    traded = swap_cross(jnp.concatenate([own_rows, jnp.pad(own_vec, ((0, 13), (0, 0)))], axis=0))
    near = gather_plane(jnp.where(in_plane, own_rows, traded[:64]), x_me, xh, z_me)
    far = [swap_core(m) for m in near]
    own_vec = jnp.where(in_plane, own_vec, traded[64:67])
    other_vec = swap_pair(own_vec)
    vec = jnp.where(label == 0, jnp.stack([own_vec, other_vec]), jnp.stack([other_vec, own_vec])).astype(F32)

    tokens = window_input.shape[0] // 2
    rows = tokens // MICRO
    stash = slope_stash = ()
    states = (master_old, first_old, second_old)
    slopes = []
    ahead = behind = jnp.zeros((rows, D), BF16)

    def control(batch):
        active = (batch >= 0) & (batch < MICRO)
        slot = jnp.clip(batch, 0, MICRO - 1)
        parts = [active, y, slot, x_me, core, label, xl]
        return jnp.stack([jnp.asarray(p, jnp.int32) for p in parts])

    for tick in range(MICRO + 2 * STAGES - 2):
        f_stages = [s for s in range(STAGES) if 0 <= tick - s < MICRO]
        b_stages = [s for s in range(STAGES) if 0 <= tick - 2 * (STAGES - 1) + s < MICRO]
        if f_stages:
            act, xs, ls = forward_call(control(tick - y), near, far, window_input, ahead, vec, stash)
            stash = (xs, ls)
            pairs = [(s, s + 1) for s in f_stages if s + 1 < STAGES]
            if pairs:
                ahead = lax.ppermute(act, "y", pairs)
                if tick == 0:
                    held = jnp.stack([lax.dynamic_index_in_dim(s, plus_nothing(slot, ahead), 0, keepdims=False) for s in states])
                    from_pair, from_cross = swap_pair(held), swap_cross(held)
        if b_stages:
            early = ()
            if tick == 5:
                early = (from_pair, from_cross)
            if tick == 7:
                early = (xt,)
            back, *slope_stash = backward_call(
                control(tick - 2 * (STAGES - 1) + y), near, far, cotangent, behind, vec, *stash, tuple(slope_stash), early
            )
            pairs = [(s, s - 1) for s in b_stages if s > 0]
            if pairs:
                behind = lax.ppermute(back, "y", pairs)
            if tick == 4:
                xt = trade_inputs(jnp.where(plus_nothing(0, behind) == 0, stash[0], 0), x_me, z_me, core)
            if tick >= 6:
                slopes.append(trade_slopes(slope_stash[tick - 6], slope_stash[2 + tick - 6]))

    kept = jnp.where(goal == section, held, jnp.where(in_plane, from_pair, from_cross))
    master, first_state, second_state = kept[0], kept[1], kept[2]

    parts = [slopes[m][i] for i in range(8) for m in range(MICRO)]
    grad_rows = ring_reduce(grad_call(xt, parts), shift_z, 4)
    learning = lax.dynamic_index_in_dim(frozen, section, 0, keepdims=False) == 0
    first_next = FIRST_DECAY * first_state + (1.0 - FIRST_DECAY) * grad_rows
    second_next = SECOND_DECAY * second_state + (1.0 - SECOND_DECAY) * grad_rows * grad_rows
    stepped = master - STEP_SIZE * (first_next / FIRST_CORRECTION) / (
        jnp.sqrt(second_next / SECOND_CORRECTION) + EPSILON
    )
    master_new = jnp.where(learning, stepped, master)
    first_new = jnp.where(learning, first_next, first_state)
    second_new = jnp.where(learning, second_next, second_state)
    return (master_new[None], first_new[None], second_new[None])


def solution(mesh):
    fine = jax.sharding.Mesh(mesh.devices.reshape(4, 2, 8, 2, 2), AXES)
    sec, rep = ("y", "xl"), ("z", "xh", "c")
    rows = P(sec, rep, None)
    in_specs = (rows, rows, rows, P(sec, None, None), P(sec), P(), P(rep, None), P(rep, None))
    return jax.shard_map(shards, mesh=fine, in_specs=in_specs, out_specs=(rows, rows, rows), check_vma=False)
```

```python
import functools
import jax
import jax.numpy as jnp
from jax import lax
from jax.experimental import pallas as pl
from jax.experimental.pallas import tpu as pltpu
from jax.sharding import PartitionSpec as P

BF16 = jnp.bfloat16
F32 = jnp.float32
D = 2048
NQ = 4
VMEM_LIMIT = 60 * 1024 * 1024
GELU_K = 0.7978845608028654


def weight_copies(near, far, w_scr, sems, x_me, core):
    copies = ([], [])
    for msgs, owner in ((near, core), (far, 1 - core)):
        for dx, ref, zs in ((0, 1, 0), (-1, 2, 0), (1, 3, 0), (2, 4, 0), (2, 5, 4)):
            xh = lax.rem(x_me + dx + 4, 4) // 2
            count = 8 if ref < 4 else 4
            dst = w_scr.at[dx % 2, pl.ds(zs, count), xh, owner, pl.ds(32, 32), :]
            copies[dx % 2].append(pltpu.make_async_copy(msgs[ref], dst, sems.at[dx % 2, NQ]))
    for slot in range(2):
        for q in range(NQ):
            for msgs, owner in ((near, core), (far, 1 - core)):
                src = msgs[0].at[pl.ds(2 * q, 2), slot]
                dst = w_scr.at[slot, pl.ds(2 * q, 2), :, owner, pl.ds(0, 32), :]
                copies[slot].append(pltpu.make_async_copy(src, dst, sems.at[slot, q]))
    return copies


def gelu_parts(u):
    square = u * u
    t = jnp.tanh(GELU_K * u * (1.0 + 0.044715 * square))
    return 0.5 * u * (1.0 + t), t, square


def gelu_slope(u, t, square):
    return 0.5 * (1.0 + t) + 0.5 * u * (1.0 - t * t) * (GELU_K * (1.0 + 3 * 0.044715 * square))


def norm_parts(z):
    center = z - jnp.mean(z, axis=-1, keepdims=True)
    spread = jnp.mean(center * center, axis=-1, keepdims=True)
    return center, lax.rsqrt(spread + 1e-5)


def issue(groups, first):
    def start(slot):
        for copy in groups[slot]:
            copy.start()

    @pl.when(first == 0)
    def _():
        start(0)
        start(1)

    @pl.when(first == 1)
    def _():
        start(1)
        start(0)


def wait_tails(w_scr, sems, slot):
    rows = w_scr.at[slot, :, :, :, pl.ds(32, 32), :]
    pltpu.make_async_copy(rows, rows, sems.at[slot, NQ]).wait()


def wait_heads(w_scr, sems, slot, q):
    rows = w_scr.at[slot, pl.ds(2 * q, 2), :, :, pl.ds(0, 32), :]
    pltpu.make_async_copy(rows, rows, sems.at[slot, q]).wait()


def forward_kernel(n_msgs, rows, ctl, *refs):
    near, far = refs[:n_msgs], refs[n_msgs:2 * n_msgs]
    window, recv, vec_in = refs[2 * n_msgs:2 * n_msgs + 3]
    act, xs, ls, w_scr, x_scr, lin_scr, vec, act_scr, sems, sem_x, sem_v, sem_o = refs[-12:]
    active, stage, batch, x_me, core, first, xl = (ctl[i] for i in range(7))

    @pl.when(active == 1)
    def _():
        groups = weight_copies(near, far, w_scr, sems, x_me, core)
        per_half = window.shape[0] // 2
        at = pl.multiple_of(batch * rows, rows)

        @pl.when(stage == 0)
        def _():
            src = window.at[pl.ds(pl.multiple_of(xl * per_half + batch * rows, rows), rows), :]
            pltpu.make_async_copy(src, x_scr.at[0], sem_x).start()

        @pl.when(stage != 0)
        def _():
            pltpu.make_async_copy(recv, x_scr.at[0], sem_x).start()

        vec_copy = pltpu.make_async_copy(vec_in, vec, sem_v)
        vec_copy.start()
        issue(groups, first)
        vec_copy.wait()
        pltpu.make_async_copy(recv, x_scr.at[0], sem_x).wait()
        outs = []
        for layer in range(2):
            slot = first ^ layer
            lin_scr[layer] = jnp.broadcast_to(vec[layer, 0:1, :], (rows, D))
            wait_tails(w_scr, sems, slot)

            @pl.loop(0, NQ)
            def _(q):
                wait_heads(w_scr, sems, slot, q)
                cols = pl.ds(pl.multiple_of(q * 512, 512), 512)
                lin_scr[layer] += jnp.dot(
                    x_scr[layer, :, cols], w_scr[slot, pl.ds(2 * q, 2)].reshape(512, D), preferred_element_type=F32
                )

            lin = lin_scr[layer]
            center, scale = norm_parts(x_scr[layer].astype(F32) + gelu_parts(lin)[0])
            y = (center * scale * vec[layer, 1:2, :] + vec[layer, 2:3, :]).astype(BF16)
            if layer == 0:
                x_scr[1] = y
            else:
                act_scr[...] = y
                outs.append(pltpu.make_async_copy(act_scr, act, sem_v))
                outs[-1].start()
            for src, dst, n in ((x_scr, xs, 0), (lin_scr, ls, 1)):
                copy = pltpu.make_async_copy(src.at[layer], dst.at[layer, pl.ds(at, rows), :], sem_o.at[layer, n])
                copy.start()
                outs.append(copy)
        for copy in outs:
            copy.wait()


def backward_kernel(n_msgs, rows, ctl, *refs):
    near, far = refs[:n_msgs], refs[n_msgs:2 * n_msgs]
    cot, recv, vec_in, xs, ls = refs[2 * n_msgs:2 * n_msgs + 5]
    back, own_0, own_1, other_0, other_1, zero = refs[-18:-12]
    zero[0] = 0
    w_scr, g_scr, x_scr, lin_scr, dz_scr, dl_scr, vec, back_scr, sems, sem_x, sem_v, sem_o = refs[-12:]
    active, stage, batch, x_me, core, first, xl = (ctl[i] for i in range(7))

    @pl.when(active == 1)
    def _():
        groups = weight_copies(near, far, w_scr, sems, x_me, core)
        per_half = cot.shape[0] // 2
        at = pl.multiple_of(batch * rows, rows)

        @pl.when(stage == 3)
        def _():
            src = cot.at[pl.ds(pl.multiple_of(xl * per_half + batch * rows, rows), rows), :]
            pltpu.make_async_copy(src, g_scr, sem_x.at[2, 0]).start()

        @pl.when(stage != 3)
        def _():
            pltpu.make_async_copy(recv, g_scr, sem_x.at[2, 0]).start()

        loads = {}
        for layer in (1, 0):
            loads[layer] = (
                pltpu.make_async_copy(xs.at[layer, pl.ds(at, rows), :], x_scr.at[layer], sem_x.at[layer, 0]),
                pltpu.make_async_copy(ls.at[layer, pl.ds(at, rows), :], lin_scr.at[layer], sem_x.at[layer, 1]),
            )
            for copy in loads[layer]:
                copy.start()
        vec_copy = pltpu.make_async_copy(vec_in, vec, sem_v)
        vec_copy.start()
        issue(groups, 1 - first)
        vec_copy.wait()
        pltpu.make_async_copy(recv, g_scr, sem_x.at[2, 0]).wait()
        outs = []
        for layer in (1, 0):
            slot = first ^ layer
            for copy in loads[layer]:
                copy.wait()
            lin = lin_scr[layer]
            gated, t, square = gelu_parts(lin)
            center, scale = norm_parts(x_scr[layer].astype(F32) + gated)
            unit = center * scale
            g = g_scr[...].astype(F32) * vec[layer, 1:2, :]
            dz = scale * (g - jnp.mean(g, axis=-1, keepdims=True) - unit * jnp.mean(g * unit, axis=-1, keepdims=True))
            dz_scr[...] = dz
            dl_scr[layer] = (dz * gelu_slope(lin, t, square)).astype(BF16)
            for is_own, pair in ((1, (own_0, own_1)), (0, (other_0, other_1))):
                for m, dst in enumerate(pair):

                    @pl.when((batch == m) & ((xl == layer) == (is_own == 1)))
                    def _():
                        pltpu.make_async_copy(dl_scr.at[layer], dst, sem_o.at[layer]).start()

            outs.append(pltpu.make_async_copy(dl_scr.at[layer], own_0, sem_o.at[layer]))
            wait_tails(w_scr, sems, slot)

            @pl.loop(0, NQ)
            def _(q):
                wait_heads(w_scr, sems, slot, q)
                cols = pl.ds(pl.multiple_of(q * 512, 512), 512)

                def step():
                    down = lax.dot_general(
                        dl_scr[layer], w_scr[slot, pl.ds(2 * q, 2)].reshape(512, D), (((1,), (1,)), ((), ())), preferred_element_type=F32
                    )
                    y = (dz_scr[:, cols] + down).astype(BF16)
                    if layer == 1:
                        g_scr[:, cols] = y
                    else:
                        back_scr[:, cols] = y

                if layer == 1:
                    step()
                else:
                    pl.when(stage != 0)(step)
        outs.append(pltpu.make_async_copy(back_scr, back, sem_v))
        outs[-1].start()
        for copy in outs:
            copy.wait()


def forward_call(ctl, near, far, window, recv, vec, stash):
    rows = recv.shape[0]
    tokens = window.shape[0] // 2
    n = len(near)
    any_spec = pl.BlockSpec(memory_space=pl.ANY)
    return pl.pallas_call(
        functools.partial(forward_kernel, n, rows),
        out_shape=(
            jax.ShapeDtypeStruct((rows, D), BF16),
            jax.ShapeDtypeStruct((2, tokens, D), BF16),
            jax.ShapeDtypeStruct((2, tokens, D), F32),
        ),
        in_specs=[pl.BlockSpec(memory_space=pltpu.SMEM)] + [any_spec] * (2 * n + 3 + len(stash)),
        out_specs=(any_spec, any_spec, any_spec),
        scratch_shapes=[
            pltpu.VMEM((2, 8, 2, 2, 64, D), BF16),
            pltpu.VMEM((2, rows, D), BF16),
            pltpu.VMEM((2, rows, D), F32),
            pltpu.VMEM(vec.shape, F32),
            pltpu.VMEM((rows, D), BF16),
            pltpu.SemaphoreType.DMA((2, NQ + 1)),
            pltpu.SemaphoreType.DMA,
            pltpu.SemaphoreType.DMA,
            pltpu.SemaphoreType.DMA((2, 2)),
        ],
        input_output_aliases={2 * n + 4 + i: 1 + i for i in range(len(stash))},
        compiler_params=pltpu.CompilerParams(vmem_limit_bytes=VMEM_LIMIT),
        cost_estimate=pl.CostEstimate(flops=4 * rows * D * D, bytes_accessed=4 * D * D, transcendentals=2 * rows * D),
        name="forward_tick",
    )(ctl, *near, *far, window, recv, vec, *stash)


def backward_call(ctl, near, far, cot, recv, vec, xs, ls, stash, early=()):
    rows = recv.shape[0]
    n = len(near)
    any_spec = pl.BlockSpec(memory_space=pl.ANY)
    return pl.pallas_call(
        functools.partial(backward_kernel, n, rows),
        out_shape=(jax.ShapeDtypeStruct((rows, D), BF16),) * 5 + (jax.ShapeDtypeStruct((1,), jnp.int32),),
        in_specs=[pl.BlockSpec(memory_space=pltpu.SMEM)] + [any_spec] * (2 * n + 5 + len(stash) + len(early)),
        out_specs=(any_spec,) * 5 + (pl.BlockSpec(memory_space=pltpu.SMEM),),
        scratch_shapes=[
            pltpu.VMEM((2, 8, 2, 2, 64, D), BF16),
            pltpu.VMEM((rows, D), BF16),
            pltpu.VMEM((2, rows, D), BF16),
            pltpu.VMEM((2, rows, D), F32),
            pltpu.VMEM((rows, D), F32),
            pltpu.VMEM((2, rows, D), BF16),
            pltpu.VMEM(vec.shape, F32),
            pltpu.VMEM((rows, D), BF16),
            pltpu.SemaphoreType.DMA((2, NQ + 1)),
            pltpu.SemaphoreType.DMA((3, 2)),
            pltpu.SemaphoreType.DMA,
            pltpu.SemaphoreType.DMA((2,)),
        ],
        input_output_aliases={2 * n + 6 + i: 1 + i for i in range(len(stash))},
        compiler_params=pltpu.CompilerParams(vmem_limit_bytes=VMEM_LIMIT),
        cost_estimate=pl.CostEstimate(flops=4 * rows * D * D, bytes_accessed=4 * D * D, transcendentals=2 * rows * D),
        name="backward_tick",
    )(ctl, *near, *far, cot, recv, vec, xs, ls, *stash, *early)

AXES = ("y", "xl", "z", "xh", "c")
MICRO = 2
STAGES = 4

FIRST_DECAY = 0.9
SECOND_DECAY = 0.999
STEP_SIZE = 0.01
EPSILON = 1e-08
FIRST_CORRECTION = 1.0 - 0.9**10
SECOND_CORRECTION = 1.0 - 0.999**10


def shift_x(v, by):
    place = lambda x: (x & 1) * 2 + (x >> 1)
    return lax.ppermute(v, ("xl", "xh"), [(place(x), place((x + by) % 4)) for x in range(4)])


def shift_z(v, by):
    return lax.ppermute(v, "z", [(z, (z + by) % 8) for z in range(8)])


def swap_core(v):
    return lax.ppermute(v, "c", [(0, 1), (1, 0)])


def swap_pair(v):
    return lax.ppermute(v, "xl", [(0, 1), (1, 0)])


def swap_cross(v):
    return lax.ppermute(v, ("y", "xl"), [(3, 4), (4, 3)])


def ring_gather(v, shift, steps):
    right = left = v
    out = []
    for _ in range(1, steps):
        right, left = shift(right, 1), shift(left, -1)
        out += [right, left]
    half = v.shape[0] // 2
    return out + [shift(right[:half], 1), shift(left[half:], -1)]


def after_kernel(*refs):
    del refs


def after(v, *others):
    return pl.pallas_call(
        after_kernel,
        out_shape=jax.ShapeDtypeStruct(v.shape, v.dtype),
        in_specs=[pl.BlockSpec(memory_space=pl.ANY)] * (1 + len(others)),
        out_specs=pl.BlockSpec(memory_space=pl.ANY),
        input_output_aliases={0: 0},
        compiler_params=pltpu.CompilerParams(vmem_limit_bytes=VMEM_LIMIT),
        name="after",
    )(v, *others)


def place_kernel(at, *refs):
    blocks, out, sem = refs[:9], refs[9], refs[10]
    for i, block in enumerate(blocks[:7]):
        pltpu.make_async_copy(block, out.at[at[i]], sem).start()
    for i, block in enumerate(blocks[7:]):
        pltpu.make_async_copy(block, out.at[at[7], pl.ds(16 * i, 16), :], sem).start()
    pltpu.make_async_copy(out, out, sem).wait()


def place(blocks, at):
    return pl.pallas_call(
        place_kernel,
        out_shape=jax.ShapeDtypeStruct((8, 32, D), BF16),
        in_specs=[pl.BlockSpec(memory_space=pltpu.SMEM)] + [pl.BlockSpec(memory_space=pl.ANY)] * 9,
        out_specs=pl.BlockSpec(memory_space=pltpu.VMEM),
        scratch_shapes=[pltpu.SemaphoreType.DMA],
        compiler_params=pltpu.CompilerParams(vmem_limit_bytes=VMEM_LIMIT),
        cost_estimate=pl.CostEstimate(flops=0, bytes_accessed=2 << 20, transcendentals=0),
        name="place_blocks",
    )(at, *blocks)


def gather_plane(rows, x_me, xh, z_me, moved, others):
    a, b = rows[:32], rows[32:]
    lower, upper, across = shift_x(a, 1), shift_x(a, -1), shift_x(a, 2)
    own_first, lower_first = xh == 0, lax.rem(x_me + 3, 4) < 2
    heads = jnp.stack(
        [
            jnp.stack([jnp.where(own_first, a, across), jnp.where(own_first, across, a)]),
            jnp.stack([jnp.where(lower_first, lower, upper), jnp.where(lower_first, upper, lower)]),
        ]
    )
    heads = lax.all_gather(heads, "z", axis=0)
    z_from = lax.rem(z_me + 8 + jnp.array((0, -1, 1, -2, 2, -3, 3, 4), jnp.int32), 8)
    tails = after(place([b] + ring_gather(b, shift_z, 4), z_from), *moved)
    right, left = shift_x(tails, 1), shift_x(tails, -1)
    ends = [shift_x(right[:4], 1), shift_x(left[4:], -1)]
    return [after(heads, right, left, *others), tails, right, left] + ends


def add_rounded(a, b):
    return (a.astype(F32) + b.astype(F32)).astype(BF16)


def ring_reduce(chunks, shift, steps):
    half = chunks.shape[1] // 2
    far = chunks[steps]
    right, left = shift(far[:half], 1), shift(far[half:], -1)
    for k in range(steps - 1, 0, -1):
        up, down = chunks[k], chunks[2 * steps - k]
        if k == steps - 1:
            right = jnp.concatenate([add_rounded(up[:half], right), up[half:]], axis=0)
            left = jnp.concatenate([down[:half], add_rounded(down[half:], left)], axis=0)
        else:
            right, left = add_rounded(up, right), add_rounded(down, left)
        right, left = shift(right, 1), shift(left, -1)
    return chunks[0].astype(F32) + right.astype(F32) + left.astype(F32)


def grad_kernel(n_parts, xt, *refs):
    parts, g, d_scr, sem = refs[:n_parts], refs[n_parts], refs[n_parts + 1], refs[n_parts + 2]
    size = parts[0].shape[0]
    for i, part in enumerate(parts):
        pltpu.make_async_copy(part, d_scr.at[pl.ds(i * size, size), :], sem).start()
    pltpu.make_async_copy(d_scr, d_scr, sem).wait()

    @pl.loop(0, D // 256)
    def _(n):
        cols = pl.ds(pl.multiple_of(n * 256, 256), 256)
        part = jnp.dot(xt[...], d_scr[:, cols], preferred_element_type=F32).astype(BF16)
        g[:, :, cols] = part.reshape(8, 64, 256)


def grad_call(xt, parts):
    tokens = xt.shape[1]
    return pl.pallas_call(
        functools.partial(grad_kernel, len(parts)),
        out_shape=jax.ShapeDtypeStruct((8, 64, D), BF16),
        in_specs=[pl.BlockSpec(memory_space=pltpu.VMEM)] + [pl.BlockSpec(memory_space=pl.ANY)] * len(parts),
        out_specs=pl.BlockSpec(memory_space=pltpu.VMEM),
        scratch_shapes=[pltpu.VMEM((tokens, D), BF16), pltpu.SemaphoreType.DMA],
        compiler_params=pltpu.CompilerParams(vmem_limit_bytes=VMEM_LIMIT),
        cost_estimate=pl.CostEstimate(flops=2 * tokens * D * 512, bytes_accessed=7 << 20, transcendentals=0),
        name="weight_grads",
    )(xt, *parts)


def rolled(v, axis, by):
    return lax.dynamic_slice_in_dim(jnp.concatenate([v, v], axis=axis), by, v.shape[axis], axis=axis)


def trade_inputs(xs, x_me, core):
    tokens = xs.shape[1]
    xt = jnp.swapaxes(xs, 1, 2).reshape(2, 8, 2, 2, 64, tokens)
    mine = lax.dynamic_index_in_dim(xt, core, 3, keepdims=False)
    theirs = lax.dynamic_index_in_dim(xt, 1 - core, 3, keepdims=False)
    both = jnp.concatenate([mine, swap_core(theirs)], axis=-1)

    def meant_for(step):
        x = lax.rem(x_me + step, 4)
        block = lax.dynamic_index_in_dim(both, x % 2, 0, keepdims=False)
        return lax.dynamic_index_in_dim(block, x // 2, 1, keepdims=False)

    return [meant_for(0), shift_x(meant_for(1), 1), shift_x(meant_for(3), -1), shift_x(meant_for(2), 2)]


def trade_slopes(own, other):
    parts = []
    for part in (own, shift_x(other, 1), shift_x(other, -1), shift_x(own, 2)):
        parts += [part, swap_core(part)]
    return parts


def shards(master_old, first_old, second_old, layer_vectors, new_section, frozen, window_input, cotangent):
    y, xl, z_me, xh, core = (lax.axis_index(name) for name in AXES)
    section = y * 2 + xl
    x_me = xl + 2 * xh
    slot = (new_section[1] >= 0).astype(jnp.int32)
    goal = lax.dynamic_index_in_dim(new_section, slot, 0, keepdims=False)
    in_plane = goal // 2 == y
    label = jnp.where(in_plane, goal & 1, xl)

    held_of = lambda v: lax.dynamic_index_in_dim(v, slot, 0, keepdims=False)
    own_rows, own_vec = held_of(master_old).astype(BF16), held_of(layer_vectors)
    own_vec = jnp.where(in_plane, own_vec, swap_cross(own_vec))
    other_vec = swap_pair(own_vec)
    vec = jnp.where(label == 0, jnp.stack([own_vec, other_vec]), jnp.stack([other_vec, own_vec])).astype(F32)
    held = jnp.stack([held_of(s) for s in (master_old, first_old, second_old)])
    moved = (swap_pair(held), swap_cross(held))
    near = gather_plane(jnp.where(in_plane, own_rows, swap_cross(own_rows)), x_me, xh, z_me, moved, (other_vec,))
    far = [swap_core(m) for m in near]

    tokens = window_input.shape[0] // 2
    rows = tokens // MICRO
    stash = slope_stash = ()
    slopes = []
    ahead = behind = jnp.zeros((rows, D), BF16)

    def control(batch):
        active = (batch >= 0) & (batch < MICRO)
        slot = jnp.clip(batch, 0, MICRO - 1)
        parts = [active, y, slot, x_me, core, label, xl]
        return jnp.stack([jnp.asarray(p, jnp.int32) for p in parts])

    for tick in range(MICRO + 2 * STAGES - 2):
        f_stages = [s for s in range(STAGES) if 0 <= tick - s < MICRO]
        b_stages = [s for s in range(STAGES) if 0 <= tick - 2 * (STAGES - 1) + s < MICRO]
        if f_stages:
            act, xs, ls = forward_call(control(tick - y), near, far, window_input, ahead, vec, stash)
            stash = (xs, ls)
            pairs = [(s, s + 1) for s in f_stages if s + 1 < STAGES]
            if pairs:
                ahead = lax.ppermute(act, "y", pairs)
        if b_stages:
            early = ()
            if tick == 6:
                early = tuple(inputs[1:3])
            if tick == 7:
                early = (inputs[3],)
            back, *slope_stash, zero = backward_call(
                control(tick - 2 * (STAGES - 1) + y), near, far, cotangent, behind, vec, *stash, tuple(slope_stash), early
            )
            pairs = [(s, s - 1) for s in b_stages if s > 0]
            if pairs:
                behind = lax.ppermute(back, "y", pairs)
            if tick == 4:
                inputs = trade_inputs(jnp.where(zero[0] == 0, stash[0], 0), x_me, core)
            if tick >= 6:
                slopes.append(trade_slopes(slope_stash[tick - 6], slope_stash[2 + tick - 6]))

    kept = jnp.where(goal == section, held, jnp.where(in_plane, *moved))
    master, first_state, second_state = kept[0], kept[1], kept[2]

    parts = [slopes[m][i] for i in range(8) for m in range(MICRO)]
    xt = rolled(jnp.concatenate(inputs, axis=-1), 0, z_me).reshape(512, -1)
    grad_rows = ring_reduce(grad_call(xt, parts), shift_z, 4)
    learning = lax.dynamic_index_in_dim(frozen, section, 0, keepdims=False) == 0
    first_next = FIRST_DECAY * first_state + (1.0 - FIRST_DECAY) * grad_rows
    second_next = SECOND_DECAY * second_state + (1.0 - SECOND_DECAY) * grad_rows * grad_rows
    stepped = master - STEP_SIZE * (first_next / FIRST_CORRECTION) / (
        jnp.sqrt(second_next / SECOND_CORRECTION) + EPSILON
    )
    master_new = jnp.where(learning, stepped, master)
    first_new = jnp.where(learning, first_next, first_state)
    second_new = jnp.where(learning, second_next, second_state)
    return (master_new[None], first_new[None], second_new[None])


def solution(mesh):
    fine = jax.sharding.Mesh(mesh.devices.reshape(4, 2, 8, 2, 2), AXES)
    sec, rep = ("y", "xl"), ("z", "xh", "c")
    rows = P(sec, rep, None)
    in_specs = (rows, rows, rows, P(sec, None, None), P(sec), P(), P(rep, None), P(rep, None))
    return jax.shard_map(shards, mesh=fine, in_specs=in_specs, out_specs=(rows, rows, rows), check_vma=False)
```

```python
import functools
import jax
import jax.numpy as jnp
from jax import lax
from jax.experimental import pallas as pl
from jax.experimental.pallas import tpu as pltpu
from jax.sharding import PartitionSpec as P

BF16 = jnp.bfloat16
F32 = jnp.float32
D = 2048
NQ = 4
VMEM_LIMIT = 64 * 1024 * 1024 - 65536
GELU_K = 0.7978845608028654


def weight_copies(near, far, w_scr, sems, x_me, core):
    copies = ([], [])
    for slot in range(2):
        for q in range(NQ):
            for msgs, owner in ((near, core), (far, 1 - core)):
                src = msgs[0].at[pl.ds(2 * q, 2), slot]
                dst = w_scr.at[slot, pl.ds(2 * q, 2), :, owner, pl.ds(0, 32), :]
                copies[slot].append(pltpu.make_async_copy(src, dst, sems.at[slot, q]))
                for dx in (0, 2) if slot == 0 else (-1, 1):
                    if dx == 2:
                        src = msgs[4 + q // 2].at[pl.ds(2 * (q % 2), 2)]
                    else:
                        src = msgs[(1, 3, 2)[dx]].at[pl.ds(2 * q, 2)]
                    xh = lax.rem(x_me + dx + 4, 4) // 2
                    dst = w_scr.at[slot, pl.ds(2 * q, 2), xh, owner, pl.ds(32, 32), :]
                    copies[slot].append(pltpu.make_async_copy(src, dst, sems.at[slot, q]))
    return copies


def gelu_parts(u):
    square = u * u
    t = jnp.tanh(GELU_K * u * (1.0 + 0.044715 * square))
    return 0.5 * u * (1.0 + t), t, square


def gelu_slope(u, t, square):
    return 0.5 * (1.0 + t) + 0.5 * u * (1.0 - t * t) * (GELU_K * (1.0 + 3 * 0.044715 * square))


def norm_parts(z):
    center = z - jnp.mean(z, axis=-1, keepdims=True)
    spread = jnp.mean(center * center, axis=-1, keepdims=True)
    return center, lax.rsqrt(spread + 1e-5)


def issue(groups, first):
    def start(slot):
        for copy in groups[slot]:
            copy.start()

    @pl.when(first == 0)
    def _():
        start(0)
        start(1)

    @pl.when(first == 1)
    def _():
        start(1)
        start(0)


def wait_pair(w_scr, sems, slot, q):
    blocks = w_scr.at[slot, pl.ds(2 * q, 2)]
    pltpu.make_async_copy(blocks, blocks, sems.at[slot, q]).wait()


def forward_kernel(n_msgs, rows, ctl, *refs):
    near, far = refs[:n_msgs], refs[n_msgs:2 * n_msgs]
    window, recv, vec_in = refs[2 * n_msgs:2 * n_msgs + 3]
    act, xs, ls, w_scr, x_scr, lin_scr, vec, act_scr, sems, sem_x, sem_v, sem_o = refs[-12:]
    active, stage, batch, x_me, core, first, xl = (ctl[i] for i in range(7))

    @pl.when(active == 1)
    def _():
        groups = weight_copies(near, far, w_scr, sems, x_me, core)
        per_half = window.shape[0] // 2
        at = pl.multiple_of(batch * rows, rows)

        @pl.when(stage == 0)
        def _():
            src = window.at[pl.ds(pl.multiple_of(xl * per_half + batch * rows, rows), rows), :]
            pltpu.make_async_copy(src, x_scr.at[0], sem_x).start()

        @pl.when(stage != 0)
        def _():
            pltpu.make_async_copy(recv, x_scr.at[0], sem_x).start()

        vec_copy = pltpu.make_async_copy(vec_in, vec, sem_v)
        vec_copy.start()
        issue(groups, first)
        vec_copy.wait()
        pltpu.make_async_copy(recv, x_scr.at[0], sem_x).wait()
        outs = []
        for layer in range(2):
            slot = first ^ layer
            lin_scr[layer] = jnp.broadcast_to(vec[layer, 0:1, :], (rows, D))

            @pl.loop(0, NQ)
            def _(q):
                wait_pair(w_scr, sems, slot, q)
                cols = pl.ds(pl.multiple_of(q * 512, 512), 512)
                lin_scr[layer] += jnp.dot(
                    x_scr[layer, :, cols], w_scr[slot, pl.ds(2 * q, 2)].reshape(512, D), preferred_element_type=F32
                )

            lin = lin_scr[layer]
            center, scale = norm_parts(x_scr[layer].astype(F32) + gelu_parts(lin)[0])
            y = (center * scale * vec[layer, 1:2, :] + vec[layer, 2:3, :]).astype(BF16)
            if layer == 0:
                x_scr[1] = y
            else:
                act_scr[...] = y
                outs.append(pltpu.make_async_copy(act_scr, act, sem_v))
                outs[-1].start()
            for src, dst, n in ((x_scr, xs, 0), (lin_scr, ls, 1)):
                copy = pltpu.make_async_copy(src.at[layer], dst.at[layer, pl.ds(at, rows), :], sem_o.at[layer, n])
                copy.start()
                outs.append(copy)
        for copy in outs:
            copy.wait()


def backward_kernel(n_msgs, rows, ctl, *refs):
    near, far = refs[:n_msgs], refs[n_msgs:2 * n_msgs]
    cot, recv, vec_in, xs, ls = refs[2 * n_msgs:2 * n_msgs + 5]
    back, own_0, own_1, other_0, other_1, zero = refs[-18:-12]
    zero[0] = 0
    w_scr, g_scr, x_scr, lin_scr, dz_scr, dl_scr, vec, back_scr, sems, sem_x, sem_v, sem_o = refs[-12:]
    active, stage, batch, x_me, core, first, xl = (ctl[i] for i in range(7))

    @pl.when(active == 1)
    def _():
        groups = weight_copies(near, far, w_scr, sems, x_me, core)
        per_half = cot.shape[0] // 2
        at = pl.multiple_of(batch * rows, rows)

        @pl.when(stage == 3)
        def _():
            src = cot.at[pl.ds(pl.multiple_of(xl * per_half + batch * rows, rows), rows), :]
            pltpu.make_async_copy(src, g_scr, sem_x.at[2, 0]).start()

        @pl.when(stage != 3)
        def _():
            pltpu.make_async_copy(recv, g_scr, sem_x.at[2, 0]).start()

        loads = {}
        for layer in (1, 0):
            loads[layer] = (
                pltpu.make_async_copy(xs.at[layer, pl.ds(at, rows), :], x_scr.at[layer], sem_x.at[layer, 0]),
                pltpu.make_async_copy(ls.at[layer, pl.ds(at, rows), :], lin_scr.at[layer], sem_x.at[layer, 1]),
            )
            for copy in loads[layer]:
                copy.start()
        vec_copy = pltpu.make_async_copy(vec_in, vec, sem_v)
        vec_copy.start()
        issue(groups, 1 - first)
        vec_copy.wait()
        pltpu.make_async_copy(recv, g_scr, sem_x.at[2, 0]).wait()
        outs = []
        for layer in (1, 0):
            slot = first ^ layer
            for copy in loads[layer]:
                copy.wait()
            lin = lin_scr[layer]
            gated, t, square = gelu_parts(lin)
            center, scale = norm_parts(x_scr[layer].astype(F32) + gated)
            unit = center * scale
            g = g_scr[...].astype(F32) * vec[layer, 1:2, :]
            dz = scale * (g - jnp.mean(g, axis=-1, keepdims=True) - unit * jnp.mean(g * unit, axis=-1, keepdims=True))
            dz_scr[...] = dz
            dl_scr[layer] = (dz * gelu_slope(lin, t, square)).astype(BF16)
            for is_own, pair in ((1, (own_0, own_1)), (0, (other_0, other_1))):
                for m, dst in enumerate(pair):

                    @pl.when((batch == m) & ((xl == layer) == (is_own == 1)))
                    def _():
                        pltpu.make_async_copy(dl_scr.at[layer], dst, sem_o.at[layer]).start()

            outs.append(pltpu.make_async_copy(dl_scr.at[layer], own_0, sem_o.at[layer]))

            @pl.loop(0, NQ)
            def _(q):
                wait_pair(w_scr, sems, slot, q)
                cols = pl.ds(pl.multiple_of(q * 512, 512), 512)

                def step():
                    down = lax.dot_general(
                        dl_scr[layer], w_scr[slot, pl.ds(2 * q, 2)].reshape(512, D), (((1,), (1,)), ((), ())), preferred_element_type=F32
                    )
                    y = (dz_scr[:, cols] + down).astype(BF16)
                    if layer == 1:
                        g_scr[:, cols] = y
                    else:
                        back_scr[:, cols] = y

                if layer == 1:
                    step()
                else:
                    pl.when(stage != 0)(step)
        outs.append(pltpu.make_async_copy(back_scr, back, sem_v))
        outs[-1].start()
        for copy in outs:
            copy.wait()


def forward_call(ctl, near, far, window, recv, vec, stash):
    rows = recv.shape[0]
    tokens = window.shape[0] // 2
    n = len(near)
    any_spec = pl.BlockSpec(memory_space=pl.ANY)
    return pl.pallas_call(
        functools.partial(forward_kernel, n, rows),
        out_shape=(
            jax.ShapeDtypeStruct((rows, D), BF16),
            jax.ShapeDtypeStruct((2, tokens, D), BF16),
            jax.ShapeDtypeStruct((2, tokens, D), F32),
        ),
        in_specs=[pl.BlockSpec(memory_space=pltpu.SMEM)] + [any_spec] * (2 * n + 3 + len(stash)),
        out_specs=(any_spec, any_spec, any_spec),
        scratch_shapes=[
            pltpu.VMEM((2, 8, 2, 2, 64, D), BF16),
            pltpu.VMEM((2, rows, D), BF16),
            pltpu.VMEM((2, rows, D), F32),
            pltpu.VMEM(vec.shape, F32),
            pltpu.VMEM((rows, D), BF16),
            pltpu.SemaphoreType.DMA((2, NQ)),
            pltpu.SemaphoreType.DMA,
            pltpu.SemaphoreType.DMA,
            pltpu.SemaphoreType.DMA((2, 2)),
        ],
        input_output_aliases={2 * n + 4 + i: 1 + i for i in range(len(stash))},
        compiler_params=pltpu.CompilerParams(vmem_limit_bytes=VMEM_LIMIT),
        cost_estimate=pl.CostEstimate(flops=4 * rows * D * D, bytes_accessed=4 * D * D, transcendentals=2 * rows * D),
        name="forward_tick",
    )(ctl, *near, *far, window, recv, vec, *stash)


def backward_call(ctl, near, far, cot, recv, vec, xs, ls, stash, early=()):
    rows = recv.shape[0]
    n = len(near)
    any_spec = pl.BlockSpec(memory_space=pl.ANY)
    return pl.pallas_call(
        functools.partial(backward_kernel, n, rows),
        out_shape=(jax.ShapeDtypeStruct((rows, D), BF16),) * 5 + (jax.ShapeDtypeStruct((1,), jnp.int32),),
        in_specs=[pl.BlockSpec(memory_space=pltpu.SMEM)] + [any_spec] * (2 * n + 5 + len(stash) + len(early)),
        out_specs=(any_spec,) * 5 + (pl.BlockSpec(memory_space=pltpu.SMEM),),
        scratch_shapes=[
            pltpu.VMEM((2, 8, 2, 2, 64, D), BF16),
            pltpu.VMEM((rows, D), BF16),
            pltpu.VMEM((2, rows, D), BF16),
            pltpu.VMEM((2, rows, D), F32),
            pltpu.VMEM((rows, D), F32),
            pltpu.VMEM((2, rows, D), BF16),
            pltpu.VMEM(vec.shape, F32),
            pltpu.VMEM((rows, D), BF16),
            pltpu.SemaphoreType.DMA((2, NQ)),
            pltpu.SemaphoreType.DMA((3, 2)),
            pltpu.SemaphoreType.DMA,
            pltpu.SemaphoreType.DMA((2,)),
        ],
        input_output_aliases={2 * n + 6 + i: 1 + i for i in range(len(stash))},
        compiler_params=pltpu.CompilerParams(vmem_limit_bytes=VMEM_LIMIT),
        cost_estimate=pl.CostEstimate(flops=4 * rows * D * D, bytes_accessed=4 * D * D, transcendentals=2 * rows * D),
        name="backward_tick",
    )(ctl, *near, *far, cot, recv, vec, xs, ls, *stash, *early)

AXES = ("y", "xl", "z", "xh", "c")
MICRO = 2
STAGES = 4

FIRST_DECAY = 0.9
SECOND_DECAY = 0.999
STEP_SIZE = 0.01
EPSILON = 1e-08
FIRST_CORRECTION = 1.0 - 0.9**10
SECOND_CORRECTION = 1.0 - 0.999**10


def shift_x(v, by):
    place = lambda x: (x & 1) * 2 + (x >> 1)
    return lax.ppermute(v, ("xl", "xh"), [(place(x), place((x + by) % 4)) for x in range(4)])


def shift_z(v, by):
    return lax.ppermute(v, "z", [(z, (z + by) % 8) for z in range(8)])


def swap_core(v):
    return lax.ppermute(v, "c", [(0, 1), (1, 0)])


def swap_pair(v):
    return lax.ppermute(v, "xl", [(0, 1), (1, 0)])


def swap_cross(v):
    return lax.ppermute(v, ("y", "xl"), [(3, 4), (4, 3)])


def ring_gather(v, shift, steps):
    right = left = v
    out = []
    for _ in range(1, steps):
        right, left = shift(right, 1), shift(left, -1)
        out += [right, left]
    half = v.shape[0] // 2
    return out + [shift(right[:half], 1), shift(left[half:], -1)]


def after_kernel(*refs):
    del refs


def after(v, *others):
    return pl.pallas_call(
        after_kernel,
        out_shape=jax.ShapeDtypeStruct(v.shape, v.dtype),
        in_specs=[pl.BlockSpec(memory_space=pl.ANY)] * (1 + len(others)),
        out_specs=pl.BlockSpec(memory_space=pl.ANY),
        input_output_aliases={0: 0},
        compiler_params=pltpu.CompilerParams(vmem_limit_bytes=VMEM_LIMIT),
        name="after",
    )(v, *others)


def place_kernel(at, *refs):
    blocks, out, sem = refs[:9], refs[9], refs[10]
    for i, block in enumerate(blocks[:7]):
        pltpu.make_async_copy(block, out.at[at[i]], sem).start()
    for i, block in enumerate(blocks[7:]):
        pltpu.make_async_copy(block, out.at[at[7], pl.ds(16 * i, 16), :], sem).start()
    pltpu.make_async_copy(out, out, sem).wait()


def place(blocks, at):
    return pl.pallas_call(
        place_kernel,
        out_shape=jax.ShapeDtypeStruct((8, 32, D), BF16),
        in_specs=[pl.BlockSpec(memory_space=pltpu.SMEM)] + [pl.BlockSpec(memory_space=pl.ANY)] * 9,
        out_specs=pl.BlockSpec(memory_space=pltpu.VMEM),
        scratch_shapes=[pltpu.SemaphoreType.DMA],
        compiler_params=pltpu.CompilerParams(vmem_limit_bytes=VMEM_LIMIT),
        cost_estimate=pl.CostEstimate(flops=0, bytes_accessed=2 << 20, transcendentals=0),
        name="place_blocks",
    )(at, *blocks)


def gather_plane(rows, x_me, xh, z_me, moved, other):
    a, b = rows[:32], rows[32:]
    lower, upper, across = shift_x(a, 1), shift_x(a, -1), shift_x(a, 2)
    own_first, lower_first = xh == 0, lax.rem(x_me + 3, 4) < 2
    heads = jnp.stack(
        [
            jnp.stack([jnp.where(own_first, a, across), jnp.where(own_first, across, a)]),
            jnp.stack([jnp.where(lower_first, lower, upper), jnp.where(lower_first, upper, lower)]),
        ]
    )
    heads = lax.all_gather(heads, "z", axis=0)
    z_from = lax.rem(z_me + 8 + jnp.array((0, -1, 1, -2, 2, -3, 3, 4), jnp.int32), 8)
    tails = after(place([b] + ring_gather(b, shift_z, 4), z_from), moved)
    right, left = shift_x(tails, 1), shift_x(tails, -1)
    ends = [shift_x(right[:4], 1), shift_x(left[4:], -1)]
    return [after(heads, *ends, other), tails, right, left] + ends


def add_rounded(a, b):
    return (a.astype(F32) + b.astype(F32)).astype(BF16)


def ring_reduce(chunks, far_low, far_high, shift, steps):
    half = chunks.shape[1] // 2
    right, left = shift(far_low, 1), shift(far_high, -1)
    for k in range(steps - 1, 0, -1):
        up, down = chunks[k], chunks[2 * steps - k]
        if k == steps - 1:
            right = jnp.concatenate([add_rounded(up[:half], right), up[half:]], axis=0)
            left = jnp.concatenate([down[:half], add_rounded(down[half:], left)], axis=0)
        else:
            right, left = add_rounded(up, right), add_rounded(down, left)
        right, left = shift(right, 1), shift(left, -1)
    return chunks[0].astype(F32) + right.astype(F32) + left.astype(F32)


def grad_kernel(n_inputs, z_ref, *refs):
    n_parts = len(refs) - n_inputs - 6
    inputs, parts = refs[:n_inputs], refs[n_inputs:n_inputs + n_parts]
    g, far_low, far_high, x_scr, d_scr, sem = refs[n_inputs + n_parts:]
    size, width = parts[0].shape[0], inputs[0].shape[-1]
    for i, part in enumerate(inputs):
        pltpu.make_async_copy(part, x_scr.at[:, :, pl.ds(i * width, width)], sem.at[0]).start()
    for i, part in enumerate(parts):
        pltpu.make_async_copy(part, d_scr.at[pl.ds(i * size, size), :], sem.at[1]).start()
    pltpu.make_async_copy(x_scr, x_scr, sem.at[0]).wait()
    pltpu.make_async_copy(d_scr, d_scr, sem.at[1]).wait()
    z_me = z_ref[0]

    @pl.loop(0, D // 256)
    def _(n):
        cols = pl.ds(pl.multiple_of(n * 256, 256), 256)
        part = jnp.dot(x_scr[...].reshape(512, -1), d_scr[:, cols], preferred_element_type=F32).astype(BF16)
        part = part.reshape(8, 64, 256)
        for z in range(8):
            g[lax.rem(z - z_me + 8, 8), :, cols] = part[z]
        far_low[:, cols] = g[4, :32, cols]
        far_high[:, cols] = g[4, 32:, cols]


def grad_call(z_me, inputs, parts):
    tokens = inputs[0].shape[-1] * len(inputs)
    vm = pl.BlockSpec(memory_space=pltpu.VMEM)
    half = jax.ShapeDtypeStruct((32, D), BF16)
    return pl.pallas_call(
        functools.partial(grad_kernel, len(inputs)),
        out_shape=(jax.ShapeDtypeStruct((8, 64, D), BF16), half, half),
        in_specs=[pl.BlockSpec(memory_space=pltpu.SMEM)]
        + [pl.BlockSpec(memory_space=pl.ANY)] * (len(inputs) + len(parts)),
        out_specs=(vm, vm, vm),
        scratch_shapes=[
            pltpu.VMEM((8, 64, tokens), BF16),
            pltpu.VMEM((tokens, D), BF16),
            pltpu.SemaphoreType.DMA((2,)),
        ],
        compiler_params=pltpu.CompilerParams(vmem_limit_bytes=VMEM_LIMIT),
        cost_estimate=pl.CostEstimate(flops=2 * tokens * D * 512, bytes_accessed=7 << 20, transcendentals=0),
        name="weight_grads",
    )(jnp.reshape(z_me, (1,)), *inputs, *parts)


def trade_inputs(xs, x_me, core):
    tokens = xs.shape[1]
    xt = jnp.swapaxes(xs, 1, 2).reshape(2, 8, 2, 2, 64, tokens)
    mine = lax.dynamic_index_in_dim(xt, core, 3, keepdims=False)
    theirs = lax.dynamic_index_in_dim(xt, 1 - core, 3, keepdims=False)
    both = jnp.concatenate([mine, swap_core(theirs)], axis=-1)

    def meant_for(step):
        x = lax.rem(x_me + step, 4)
        block = lax.dynamic_index_in_dim(both, x % 2, 0, keepdims=False)
        return lax.dynamic_index_in_dim(block, x // 2, 1, keepdims=False)

    return [meant_for(0), shift_x(meant_for(1), 1), shift_x(meant_for(3), -1), shift_x(meant_for(2), 2)]


def trade_slopes(own, other):
    parts = []
    for part in (own, shift_x(other, 1), shift_x(other, -1), shift_x(own, 2)):
        parts += [part, swap_core(part)]
    return parts


def shards(master_old, first_old, second_old, layer_vectors, new_section, frozen, window_input, cotangent):
    y, xl, z_me, xh, core = (lax.axis_index(name) for name in AXES)
    section = y * 2 + xl
    x_me = xl + 2 * xh
    slot = (new_section[1] >= 0).astype(jnp.int32)
    goal = lax.dynamic_index_in_dim(new_section, slot, 0, keepdims=False)
    in_plane = goal // 2 == y
    label = jnp.where(in_plane, goal & 1, xl)

    held_of = lambda v: lax.dynamic_index_in_dim(v, slot, 0, keepdims=False)
    own_rows, own_vec = held_of(master_old).astype(BF16), held_of(layer_vectors)
    own_vec = jnp.where(in_plane, own_vec, swap_cross(own_vec))
    other_vec = swap_pair(own_vec)
    vec = jnp.where(label == 0, jnp.stack([own_vec, other_vec]), jnp.stack([other_vec, own_vec])).astype(F32)
    states = (master_old, first_old, second_old)
    held = jnp.stack([held_of(s) for s in states])
    from_pair, from_cross = swap_pair(held), swap_cross(held)
    near = gather_plane(jnp.where(in_plane, own_rows, swap_cross(own_rows)), x_me, xh, z_me, from_pair, other_vec)
    far = [swap_core(m) for m in near]

    tokens = window_input.shape[0] // 2
    rows = tokens // MICRO
    stash = slope_stash = ()
    slopes = []
    ahead = behind = jnp.zeros((rows, D), BF16)

    def control(batch):
        active = (batch >= 0) & (batch < MICRO)
        slot = jnp.clip(batch, 0, MICRO - 1)
        parts = [active, y, slot, x_me, core, label, xl]
        return jnp.stack([jnp.asarray(p, jnp.int32) for p in parts])

    for tick in range(MICRO + 2 * STAGES - 2):
        f_stages = [s for s in range(STAGES) if 0 <= tick - s < MICRO]
        b_stages = [s for s in range(STAGES) if 0 <= tick - 2 * (STAGES - 1) + s < MICRO]
        if f_stages:
            act, xs, ls = forward_call(control(tick - y), near, far, window_input, ahead, vec, stash)
            stash = (xs, ls)
            pairs = [(s, s + 1) for s in f_stages if s + 1 < STAGES]
            if pairs:
                ahead = lax.ppermute(act, "y", pairs)
        if b_stages:
            early = ()
            if tick == 5:
                early = (from_cross,)
            if tick == 6:
                early = tuple(inputs[1:3])
            if tick == 7:
                early = (inputs[3],)
            back, *slope_stash, zero = backward_call(
                control(tick - 2 * (STAGES - 1) + y), near, far, cotangent, behind, vec, *stash, tuple(slope_stash), early
            )
            pairs = [(s, s - 1) for s in b_stages if s > 0]
            if pairs:
                behind = lax.ppermute(back, "y", pairs)
            if tick == 4:
                inputs = trade_inputs(jnp.where(zero[0] == 0, stash[0], 0), x_me, core)
            if tick >= 6:
                slopes.append(trade_slopes(slope_stash[tick - 6], slope_stash[2 + tick - 6]))

    kept = jnp.where(goal == section, held, jnp.where(in_plane, from_pair, from_cross))
    master, first_state, second_state = kept[0], kept[1], kept[2]

    parts = [slopes[m][i] for i in range(8) for m in range(MICRO)]
    grad_rows = ring_reduce(*grad_call(z_me, inputs, parts), shift_z, 4)
    learning = lax.dynamic_index_in_dim(frozen, section, 0, keepdims=False) == 0
    first_next = FIRST_DECAY * first_state + (1.0 - FIRST_DECAY) * grad_rows
    second_next = SECOND_DECAY * second_state + (1.0 - SECOND_DECAY) * grad_rows * grad_rows
    stepped = master - STEP_SIZE * (first_next / FIRST_CORRECTION) / (
        jnp.sqrt(second_next / SECOND_CORRECTION) + EPSILON
    )
    master_new = jnp.where(learning, stepped, master)
    first_new = jnp.where(learning, first_next, first_state)
    second_new = jnp.where(learning, second_next, second_state)
    return (master_new[None], first_new[None], second_new[None])


def solution(mesh):
    fine = jax.sharding.Mesh(mesh.devices.reshape(4, 2, 8, 2, 2), AXES)
    sec, rep = ("y", "xl"), ("z", "xh", "c")
    rows = P(sec, rep, None)
    in_specs = (rows, rows, rows, P(sec, None, None), P(sec), P(), P(rep, None), P(rep, None))
    return jax.shard_map(shards, mesh=fine, in_specs=in_specs, out_specs=(rows, rows, rows), check_vma=False)
```

```python
import functools
import jax
import jax.numpy as jnp
from jax import lax
from jax.experimental import pallas as pl
from jax.experimental.pallas import tpu as pltpu
from jax.sharding import PartitionSpec as P

BF16 = jnp.bfloat16
F32 = jnp.float32
D = 2048
NQ = 4
VMEM_LIMIT = 64 * 1024 * 1024 - 65536
GELU_K = 0.7978845608028654


def weight_copies(near, far, w_scr, sems, x_me, core):
    copies = ([], [])
    for slot in range(2):
        for q in range(NQ):
            for msgs, owner in ((near, core), (far, 1 - core)):
                src = msgs[0].at[pl.ds(2 * q, 2), slot]
                dst = w_scr.at[slot, pl.ds(2 * q, 2), :, owner, pl.ds(0, 32), :]
                copies[slot].append(pltpu.make_async_copy(src, dst, sems.at[slot, q]))
                for dx in (0, 2) if slot == 0 else (-1, 1):
                    if dx == 2:
                        src = msgs[4 + q // 2].at[pl.ds(2 * (q % 2), 2)]
                    else:
                        src = msgs[(1, 3, 2)[dx]].at[pl.ds(2 * q, 2)]
                    xh = lax.rem(x_me + dx + 4, 4) // 2
                    dst = w_scr.at[slot, pl.ds(2 * q, 2), xh, owner, pl.ds(32, 32), :]
                    copies[slot].append(pltpu.make_async_copy(src, dst, sems.at[slot, q]))
    return copies


def gelu_parts(u):
    square = u * u
    t = jnp.tanh(GELU_K * u * (1.0 + 0.044715 * square))
    return 0.5 * u * (1.0 + t), t, square


def gelu_slope(u, t, square):
    return 0.5 * (1.0 + t) + 0.5 * u * (1.0 - t * t) * (GELU_K * (1.0 + 3 * 0.044715 * square))


def norm_parts(z):
    center = z - jnp.mean(z, axis=-1, keepdims=True)
    spread = jnp.mean(center * center, axis=-1, keepdims=True)
    return center, lax.rsqrt(spread + 1e-5)


def issue(groups, first):
    def start(slot):
        for copy in groups[slot]:
            copy.start()

    @pl.when(first == 0)
    def _():
        start(0)
        start(1)

    @pl.when(first == 1)
    def _():
        start(1)
        start(0)


def wait_pair(w_scr, sems, slot, q):
    blocks = w_scr.at[slot, pl.ds(2 * q, 2)]
    pltpu.make_async_copy(blocks, blocks, sems.at[slot, q]).wait()


def forward_kernel(n_msgs, rows, ctl, *refs):
    near, far = refs[:n_msgs], refs[n_msgs:2 * n_msgs]
    window, recv, vec_in = refs[2 * n_msgs:2 * n_msgs + 3]
    act, xs, ls, w_scr, x_scr, lin_scr, vec, act_scr, sems, sem_x, sem_v, sem_o = refs[-12:]
    active, stage, batch, x_me, core, first, xl = (ctl[i] for i in range(7))

    @pl.when(active == 1)
    def _():
        groups = weight_copies(near, far, w_scr, sems, x_me, core)
        per_half = window.shape[0] // 2
        at = pl.multiple_of(batch * rows, rows)

        @pl.when(stage == 0)
        def _():
            src = window.at[pl.ds(pl.multiple_of(xl * per_half + batch * rows, rows), rows), :]
            pltpu.make_async_copy(src, x_scr.at[0], sem_x).start()

        @pl.when(stage != 0)
        def _():
            pltpu.make_async_copy(recv, x_scr.at[0], sem_x).start()

        vec_copy = pltpu.make_async_copy(vec_in, vec, sem_v)
        vec_copy.start()
        issue(groups, first)
        vec_copy.wait()
        pltpu.make_async_copy(recv, x_scr.at[0], sem_x).wait()
        outs = []
        for layer in range(2):
            slot = first ^ layer
            lin_scr[layer] = jnp.broadcast_to(vec[layer, 0:1, :], (rows, D))

            @pl.loop(0, NQ)
            def _(q):
                wait_pair(w_scr, sems, slot, q)
                cols = pl.ds(pl.multiple_of(q * 512, 512), 512)
                lin_scr[layer] += jnp.dot(
                    x_scr[layer, :, cols], w_scr[slot, pl.ds(2 * q, 2)].reshape(512, D), preferred_element_type=F32
                )

            lin = lin_scr[layer]
            center, scale = norm_parts(x_scr[layer].astype(F32) + gelu_parts(lin)[0])
            y = (center * scale * vec[layer, 1:2, :] + vec[layer, 2:3, :]).astype(BF16)
            if layer == 0:
                x_scr[1] = y
            else:
                act_scr[...] = y
                outs.append(pltpu.make_async_copy(act_scr, act, sem_v))
                outs[-1].start()
            for src, dst, n in ((x_scr, xs, 0), (lin_scr, ls, 1)):
                copy = pltpu.make_async_copy(src.at[layer], dst.at[layer, pl.ds(at, rows), :], sem_o.at[layer, n])
                copy.start()
                outs.append(copy)
        for copy in outs:
            copy.wait()


def backward_kernel(n_msgs, rows, ctl, *refs):
    near, far = refs[:n_msgs], refs[n_msgs:2 * n_msgs]
    cot, recv, vec_in, xs, ls = refs[2 * n_msgs:2 * n_msgs + 5]
    back, own_0, own_1, other_0, other_1, zero = refs[-18:-12]
    zero[0] = 0
    w_scr, g_scr, x_scr, lin_scr, dz_scr, dl_scr, vec, back_scr, sems, sem_x, sem_v, sem_o = refs[-12:]
    active, stage, batch, x_me, core, first, xl = (ctl[i] for i in range(7))

    @pl.when(active == 1)
    def _():
        groups = weight_copies(near, far, w_scr, sems, x_me, core)
        per_half = cot.shape[0] // 2
        at = pl.multiple_of(batch * rows, rows)

        @pl.when(stage == 3)
        def _():
            src = cot.at[pl.ds(pl.multiple_of(xl * per_half + batch * rows, rows), rows), :]
            pltpu.make_async_copy(src, g_scr, sem_x.at[2, 0]).start()

        @pl.when(stage != 3)
        def _():
            pltpu.make_async_copy(recv, g_scr, sem_x.at[2, 0]).start()

        loads = {}
        for layer in (1, 0):
            loads[layer] = (
                pltpu.make_async_copy(xs.at[layer, pl.ds(at, rows), :], x_scr.at[layer], sem_x.at[layer, 0]),
                pltpu.make_async_copy(ls.at[layer, pl.ds(at, rows), :], lin_scr.at[layer], sem_x.at[layer, 1]),
            )
            for copy in loads[layer]:
                copy.start()
        vec_copy = pltpu.make_async_copy(vec_in, vec, sem_v)
        vec_copy.start()
        issue(groups, 1 - first)
        vec_copy.wait()
        pltpu.make_async_copy(recv, g_scr, sem_x.at[2, 0]).wait()
        outs = []
        for layer in (1, 0):
            slot = first ^ layer
            for copy in loads[layer]:
                copy.wait()
            lin = lin_scr[layer]
            gated, t, square = gelu_parts(lin)
            center, scale = norm_parts(x_scr[layer].astype(F32) + gated)
            unit = center * scale
            g = g_scr[...].astype(F32) * vec[layer, 1:2, :]
            dz = scale * (g - jnp.mean(g, axis=-1, keepdims=True) - unit * jnp.mean(g * unit, axis=-1, keepdims=True))
            dz_scr[...] = dz
            dl_scr[layer] = (dz * gelu_slope(lin, t, square)).astype(BF16)
            for is_own, pair in ((1, (own_0, own_1)), (0, (other_0, other_1))):
                for m, dst in enumerate(pair):

                    @pl.when((batch == m) & ((xl == layer) == (is_own == 1)))
                    def _():
                        pltpu.make_async_copy(dl_scr.at[layer], dst, sem_o.at[layer]).start()

            outs.append(pltpu.make_async_copy(dl_scr.at[layer], own_0, sem_o.at[layer]))

            @pl.loop(0, NQ)
            def _(q):
                wait_pair(w_scr, sems, slot, q)
                cols = pl.ds(pl.multiple_of(q * 512, 512), 512)

                def step():
                    down = lax.dot_general(
                        dl_scr[layer], w_scr[slot, pl.ds(2 * q, 2)].reshape(512, D), (((1,), (1,)), ((), ())), preferred_element_type=F32
                    )
                    y = (dz_scr[:, cols] + down).astype(BF16)
                    if layer == 1:
                        g_scr[:, cols] = y
                    else:
                        back_scr[:, cols] = y

                if layer == 1:
                    step()
                else:
                    pl.when(stage != 0)(step)
        outs.append(pltpu.make_async_copy(back_scr, back, sem_v))
        outs[-1].start()
        for copy in outs:
            copy.wait()


def forward_call(ctl, near, far, window, recv, vec, stash, early):
    rows = recv.shape[0]
    tokens = window.shape[0] // 2
    n = len(near)
    any_spec = pl.BlockSpec(memory_space=pl.ANY)
    return pl.pallas_call(
        functools.partial(forward_kernel, n, rows),
        out_shape=(
            jax.ShapeDtypeStruct((rows, D), BF16),
            jax.ShapeDtypeStruct((2, tokens, D), BF16),
            jax.ShapeDtypeStruct((2, tokens, D), F32),
        ),
        in_specs=[pl.BlockSpec(memory_space=pltpu.SMEM)] + [any_spec] * (2 * n + 3 + len(stash) + len(early)),
        out_specs=(any_spec, any_spec, any_spec),
        scratch_shapes=[
            pltpu.VMEM((2, 8, 2, 2, 64, D), BF16),
            pltpu.VMEM((2, rows, D), BF16),
            pltpu.VMEM((2, rows, D), F32),
            pltpu.VMEM(vec.shape, F32),
            pltpu.VMEM((rows, D), BF16),
            pltpu.SemaphoreType.DMA((2, NQ)),
            pltpu.SemaphoreType.DMA,
            pltpu.SemaphoreType.DMA,
            pltpu.SemaphoreType.DMA((2, 2)),
        ],
        input_output_aliases={2 * n + 4 + i: 1 + i for i in range(len(stash))},
        compiler_params=pltpu.CompilerParams(vmem_limit_bytes=VMEM_LIMIT),
        cost_estimate=pl.CostEstimate(flops=4 * rows * D * D, bytes_accessed=4 * D * D, transcendentals=2 * rows * D),
        name="forward_tick",
    )(ctl, *near, *far, window, recv, vec, *stash, *early)


def backward_call(ctl, near, far, cot, recv, vec, xs, ls, stash, early=()):
    rows = recv.shape[0]
    n = len(near)
    any_spec = pl.BlockSpec(memory_space=pl.ANY)
    return pl.pallas_call(
        functools.partial(backward_kernel, n, rows),
        out_shape=(jax.ShapeDtypeStruct((rows, D), BF16),) * 5 + (jax.ShapeDtypeStruct((1,), jnp.int32),),
        in_specs=[pl.BlockSpec(memory_space=pltpu.SMEM)] + [any_spec] * (2 * n + 5 + len(stash) + len(early)),
        out_specs=(any_spec,) * 5 + (pl.BlockSpec(memory_space=pltpu.SMEM),),
        scratch_shapes=[
            pltpu.VMEM((2, 8, 2, 2, 64, D), BF16),
            pltpu.VMEM((rows, D), BF16),
            pltpu.VMEM((2, rows, D), BF16),
            pltpu.VMEM((2, rows, D), F32),
            pltpu.VMEM((rows, D), F32),
            pltpu.VMEM((2, rows, D), BF16),
            pltpu.VMEM(vec.shape, F32),
            pltpu.VMEM((rows, D), BF16),
            pltpu.SemaphoreType.DMA((2, NQ)),
            pltpu.SemaphoreType.DMA((3, 2)),
            pltpu.SemaphoreType.DMA,
            pltpu.SemaphoreType.DMA((2,)),
        ],
        input_output_aliases={2 * n + 6 + i: 1 + i for i in range(len(stash))},
        compiler_params=pltpu.CompilerParams(vmem_limit_bytes=VMEM_LIMIT),
        cost_estimate=pl.CostEstimate(flops=4 * rows * D * D, bytes_accessed=4 * D * D, transcendentals=2 * rows * D),
        name="backward_tick",
    )(ctl, *near, *far, cot, recv, vec, xs, ls, *stash, *early)

AXES = ("y", "xl", "z", "xh", "c")
MICRO = 2
STAGES = 4

FIRST_DECAY = 0.9
SECOND_DECAY = 0.999
STEP_SIZE = 0.01
EPSILON = 1e-08
FIRST_CORRECTION = 1.0 - 0.9**10
SECOND_CORRECTION = 1.0 - 0.999**10


def shift_x(v, by):
    place = lambda x: (x & 1) * 2 + (x >> 1)
    return lax.ppermute(v, ("xl", "xh"), [(place(x), place((x + by) % 4)) for x in range(4)])


def shift_z(v, by):
    return lax.ppermute(v, "z", [(z, (z + by) % 8) for z in range(8)])


def swap_core(v):
    return lax.ppermute(v, "c", [(0, 1), (1, 0)])


def swap_core_in(v, planes):
    return lax.ppermute(v, ("y", "c"), [(2 * y + c, 2 * y + 1 - c) for y in planes for c in range(2)])


def shift_x_in(v, by, planes):
    place = lambda y, x: y * 4 + (x & 1) * 2 + (x >> 1)
    return lax.ppermute(v, ("y", "xl", "xh"), [(place(y, x), place(y, (x + by) % 4)) for y in planes for x in range(4)])


def swap_pair(v):
    return lax.ppermute(v, "xl", [(0, 1), (1, 0)])


def swap_cross(v):
    return lax.ppermute(v, ("y", "xl"), [(3, 4), (4, 3)])


def ring_gather(v, shift, steps):
    right = left = v
    out = []
    for _ in range(1, steps):
        right, left = shift(right, 1), shift(left, -1)
        out += [right, left]
    half = v.shape[0] // 2
    return out + [shift(right[:half], 1), shift(left[half:], -1)]


def after_kernel(*refs):
    del refs


def after(v, *others):
    return pl.pallas_call(
        after_kernel,
        out_shape=jax.ShapeDtypeStruct(v.shape, v.dtype),
        in_specs=[pl.BlockSpec(memory_space=pl.ANY)] * (1 + len(others)),
        out_specs=pl.BlockSpec(memory_space=pl.ANY),
        input_output_aliases={0: 0},
        compiler_params=pltpu.CompilerParams(vmem_limit_bytes=VMEM_LIMIT),
        name="after",
    )(v, *others)


def place_kernel(at, *refs):
    blocks, out, sem = refs[:9], refs[9], refs[10]
    for i, block in enumerate(blocks[:7]):
        pltpu.make_async_copy(block, out.at[at[i]], sem).start()
    for i, block in enumerate(blocks[7:]):
        pltpu.make_async_copy(block, out.at[at[7], pl.ds(16 * i, 16), :], sem).start()
    pltpu.make_async_copy(out, out, sem).wait()


def place(blocks, at):
    return pl.pallas_call(
        place_kernel,
        out_shape=jax.ShapeDtypeStruct((8, 32, D), BF16),
        in_specs=[pl.BlockSpec(memory_space=pltpu.SMEM)] + [pl.BlockSpec(memory_space=pl.ANY)] * 9,
        out_specs=pl.BlockSpec(memory_space=pltpu.VMEM),
        scratch_shapes=[pltpu.SemaphoreType.DMA],
        compiler_params=pltpu.CompilerParams(vmem_limit_bytes=VMEM_LIMIT),
        cost_estimate=pl.CostEstimate(flops=0, bytes_accessed=2 << 20, transcendentals=0),
        name="place_blocks",
    )(at, *blocks)


def gather_plane(rows, x_me, xh, z_me, moved, other):
    a, b = rows[:32], rows[32:]
    lower, upper, across = shift_x(a, 1), shift_x(a, -1), shift_x(a, 2)
    own_first, lower_first = xh == 0, lax.rem(x_me + 3, 4) < 2
    heads = jnp.stack(
        [
            jnp.stack([jnp.where(own_first, a, across), jnp.where(own_first, across, a)]),
            jnp.stack([jnp.where(lower_first, lower, upper), jnp.where(lower_first, upper, lower)]),
        ]
    )
    heads = lax.all_gather(heads, "z", axis=0)
    z_from = lax.rem(z_me + 8 + jnp.array((0, -1, 1, -2, 2, -3, 3, 4), jnp.int32), 8)
    tails = after(place([b] + ring_gather(b, shift_z, 4), z_from), moved)
    right, left = shift_x(tails, 1), shift_x(tails, -1)
    ends = [shift_x(right[:4], 1), shift_x(left[4:], -1)]
    return [after(heads, *ends, other), tails, right, left] + ends


def add_rounded(a, b):
    return (a.astype(F32) + b.astype(F32)).astype(BF16)


def ring_reduce(chunks, far_low, far_high, shift, steps):
    half = chunks.shape[1] // 2
    right, left = shift(far_low, 1), shift(far_high, -1)
    for k in range(steps - 1, 0, -1):
        up, down = chunks[k], chunks[2 * steps - k]
        if k == steps - 1:
            right = jnp.concatenate([add_rounded(up[:half], right), up[half:]], axis=0)
            left = jnp.concatenate([down[:half], add_rounded(down[half:], left)], axis=0)
        else:
            right, left = add_rounded(up, right), add_rounded(down, left)
        right, left = shift(right, 1), shift(left, -1)
    return chunks[0].astype(F32) + right.astype(F32) + left.astype(F32)


def grad_kernel(n_inputs, z_ref, *refs):
    n_parts = len(refs) - 2 * n_inputs - 6
    inputs, parts = refs[:2 * n_inputs], refs[2 * n_inputs:2 * n_inputs + n_parts]
    g, far_low, far_high, x_scr, d_scr, sem = refs[2 * n_inputs + n_parts:]
    size, width = parts[0].shape[0], inputs[0].shape[-1]
    for which in range(2):

        @pl.when(z_ref[1] == which)
        def _():
            for i, part in enumerate(inputs[which * n_inputs:(which + 1) * n_inputs]):
                pltpu.make_async_copy(part, x_scr.at[:, :, pl.ds(i * width, width)], sem.at[0]).start()

    for i, part in enumerate(parts):
        pltpu.make_async_copy(part, d_scr.at[pl.ds(i * size, size), :], sem.at[1]).start()
    pltpu.make_async_copy(x_scr, x_scr, sem.at[0]).wait()
    pltpu.make_async_copy(d_scr, d_scr, sem.at[1]).wait()
    z_me = z_ref[0]

    @pl.loop(0, D // 256)
    def _(n):
        cols = pl.ds(pl.multiple_of(n * 256, 256), 256)
        part = jnp.dot(x_scr[...].reshape(512, -1), d_scr[:, cols], preferred_element_type=F32).astype(BF16)
        part = part.reshape(8, 64, 256)
        for z in range(8):
            g[lax.rem(z - z_me + 8, 8), :, cols] = part[z]
        far_low[:, cols] = g[4, :32, cols]
        far_high[:, cols] = g[4, 32:, cols]


def grad_call(z_me, which, inputs, parts):
    n = len(inputs[0])
    tokens = inputs[0][0].shape[-1] * n
    vm = pl.BlockSpec(memory_space=pltpu.VMEM)
    half = jax.ShapeDtypeStruct((32, D), BF16)
    return pl.pallas_call(
        functools.partial(grad_kernel, n),
        out_shape=(jax.ShapeDtypeStruct((8, 64, D), BF16), half, half),
        in_specs=[pl.BlockSpec(memory_space=pltpu.SMEM)]
        + [pl.BlockSpec(memory_space=pl.ANY)] * (2 * n + len(parts)),
        out_specs=(vm, vm, vm),
        scratch_shapes=[
            pltpu.VMEM((8, 64, tokens), BF16),
            pltpu.VMEM((tokens, D), BF16),
            pltpu.SemaphoreType.DMA((2,)),
        ],
        compiler_params=pltpu.CompilerParams(vmem_limit_bytes=VMEM_LIMIT),
        cost_estimate=pl.CostEstimate(flops=2 * tokens * D * 512, bytes_accessed=7 << 20, transcendentals=0),
        name="weight_grads",
    )(jnp.stack([z_me, which]), *inputs[0], *inputs[1], *parts)


def trade_inputs(xs, x_me, core, planes):
    tokens = xs.shape[1]
    xt = jnp.swapaxes(xs, 1, 2).reshape(2, 8, 2, 2, 64, tokens)
    mine = lax.dynamic_index_in_dim(xt, core, 3, keepdims=False)
    theirs = lax.dynamic_index_in_dim(xt, 1 - core, 3, keepdims=False)
    both = jnp.concatenate([mine, swap_core_in(theirs, planes)], axis=-1)

    def meant_for(step):
        x = lax.rem(x_me + step, 4)
        block = lax.dynamic_index_in_dim(both, x % 2, 0, keepdims=False)
        return lax.dynamic_index_in_dim(block, x // 2, 1, keepdims=False)

    return [meant_for(0)] + [shift_x_in(meant_for(by % 4), by, planes) for by in (1, -1, 2)]


def trade_slopes(own, other):
    parts = []
    for part in (own, shift_x(other, 1), shift_x(other, -1), shift_x(own, 2)):
        parts += [part, swap_core(part)]
    return parts


def shards(master_old, first_old, second_old, layer_vectors, new_section, frozen, window_input, cotangent):
    y, xl, z_me, xh, core = (lax.axis_index(name) for name in AXES)
    section = y * 2 + xl
    x_me = xl + 2 * xh
    goal = jnp.maximum(new_section[0], new_section[1])
    in_plane = goal // 2 == y
    label = jnp.where(in_plane, goal & 1, xl)

    held_of = lambda v: jnp.where(new_section[1] >= 0, v[1], v[0])
    own_rows, own_vec = held_of(master_old).astype(BF16), held_of(layer_vectors)
    own_vec = jnp.where(in_plane, own_vec, swap_cross(own_vec))
    other_vec = swap_pair(own_vec)
    vec = jnp.where(label == 0, jnp.stack([own_vec, other_vec]), jnp.stack([other_vec, own_vec])).astype(F32)
    states = (master_old, first_old, second_old)
    held = jnp.stack([held_of(s) for s in states])
    from_pair, from_cross = swap_pair(held), swap_cross(held)
    rows_here = jnp.where(in_plane, own_rows, swap_cross(own_rows))
    near = gather_plane(rows_here, x_me, xh, z_me, from_pair, vec)
    far = [swap_core(m) for m in near]

    tokens = window_input.shape[0] // 2
    rows = tokens // MICRO
    stash = slope_stash = ()
    slopes, inputs = [], []
    ahead = behind = rows_here

    def control(batch):
        active = (batch >= 0) & (batch < MICRO)
        slot = jnp.clip(batch, 0, MICRO - 1)
        parts = [active, y, slot, x_me, core, label, xl]
        return jnp.stack([jnp.asarray(p, jnp.int32) for p in parts])

    for tick in range(MICRO + 2 * STAGES - 2):
        f_stages = [s for s in range(STAGES) if 0 <= tick - s < MICRO]
        b_stages = [s for s in range(STAGES) if 0 <= tick - 2 * (STAGES - 1) + s < MICRO]
        if f_stages:
            early = tuple(inputs[0][1:]) if tick == 3 else ()
            act, xs, ls = forward_call(control(tick - y), near, far, window_input, ahead, vec, stash, early)
            stash = (xs, ls)
            if tick == 2:
                inputs.append(trade_inputs(xs, x_me, core, (0, 1)))
            pairs = [(s, s + 1) for s in f_stages if s + 1 < STAGES]
            if pairs:
                ahead = lax.ppermute(act, "y", pairs)
        if b_stages:
            early = ()
            if tick == 6:
                early = (from_cross,)
            if tick == 7:
                early = tuple(inputs[1][1:])
            back, *slope_stash, zero = backward_call(
                control(tick - 2 * (STAGES - 1) + y), near, far, cotangent, behind, vec, *stash, tuple(slope_stash), early
            )
            pairs = [(s, s - 1) for s in b_stages if s > 0]
            if pairs:
                behind = lax.ppermute(back, "y", pairs)
            if tick == 5:
                inputs.append(trade_inputs(jnp.where(zero[0] == 0, stash[0], 0), x_me, core, (2, 3)))
            if tick >= 6:
                slopes.append(trade_slopes(slope_stash[tick - 6], slope_stash[2 + tick - 6]))

    kept = jnp.where(goal == section, held, jnp.where(in_plane, from_pair, from_cross))
    master, first_state, second_state = kept[0], kept[1], kept[2]

    parts = [slopes[m][i] for i in range(8) for m in range(MICRO)]
    grad_rows = ring_reduce(*grad_call(z_me, y // 2, inputs, parts), shift_z, 4)
    learning = lax.dynamic_index_in_dim(frozen, section, 0, keepdims=False) == 0
    first_next = FIRST_DECAY * first_state + (1.0 - FIRST_DECAY) * grad_rows
    second_next = SECOND_DECAY * second_state + (1.0 - SECOND_DECAY) * grad_rows * grad_rows
    stepped = master - STEP_SIZE * (first_next / FIRST_CORRECTION) / (
        jnp.sqrt(second_next / SECOND_CORRECTION) + EPSILON
    )
    master_new = jnp.where(learning, stepped, master)
    first_new = jnp.where(learning, first_next, first_state)
    second_new = jnp.where(learning, second_next, second_state)
    return (master_new[None], first_new[None], second_new[None])


def solution(mesh):
    fine = jax.sharding.Mesh(mesh.devices.reshape(4, 2, 8, 2, 2), AXES)
    sec, rep = ("y", "xl"), ("z", "xh", "c")
    rows = P(sec, rep, None)
    in_specs = (rows, rows, rows, P(sec, None, None), P(sec), P(), P(rep, None), P(rep, None))
    return jax.shard_map(shards, mesh=fine, in_specs=in_specs, out_specs=(rows, rows, rows), check_vma=False)
```

```python
import functools
import jax
import jax.numpy as jnp
from jax import lax
from jax.experimental import pallas as pl
from jax.experimental.pallas import tpu as pltpu
from jax.sharding import PartitionSpec as P

BF16 = jnp.bfloat16
F32 = jnp.float32
D = 2048
NQ = 4
VMEM_LIMIT = 64 * 1024 * 1024 - 65536
GELU_K = 0.7978845608028654


def weight_copies(near, far, w_scr, sems, x_me, core):
    copies = ([], [])
    for slot in range(2):
        for q in range(NQ):
            for msgs, owner in ((near, core), (far, 1 - core)):
                src = msgs[0].at[pl.ds(2 * q, 2), slot]
                dst = w_scr.at[slot, pl.ds(2 * q, 2), :, owner, pl.ds(0, 32), :]
                copies[slot].append(pltpu.make_async_copy(src, dst, sems.at[slot, q]))
                for dx in (0, 2) if slot == 0 else (-1, 1):
                    if dx == 2:
                        src = msgs[4 + q // 2].at[pl.ds(2 * (q % 2), 2)]
                    else:
                        src = msgs[(1, 3, 2)[dx]].at[pl.ds(2 * q, 2)]
                    xh = lax.rem(x_me + dx + 4, 4) // 2
                    dst = w_scr.at[slot, pl.ds(2 * q, 2), xh, owner, pl.ds(32, 32), :]
                    copies[slot].append(pltpu.make_async_copy(src, dst, sems.at[slot, q]))
    return copies


def gelu_parts(u):
    square = u * u
    t = jnp.tanh(GELU_K * u * (1.0 + 0.044715 * square))
    return 0.5 * u * (1.0 + t), t, square


def gelu_slope(u, t, square):
    return 0.5 * (1.0 + t) + 0.5 * u * (1.0 - t * t) * (GELU_K * (1.0 + 3 * 0.044715 * square))


def norm_parts(z):
    center = z - jnp.mean(z, axis=-1, keepdims=True)
    spread = jnp.mean(center * center, axis=-1, keepdims=True)
    return center, lax.rsqrt(spread + 1e-5)


def issue(groups, first):
    def start(slot):
        for copy in groups[slot]:
            copy.start()

    @pl.when(first == 0)
    def _():
        start(0)
        start(1)

    @pl.when(first == 1)
    def _():
        start(1)
        start(0)


def wait_pair(w_scr, sems, slot, q):
    blocks = w_scr.at[slot, pl.ds(2 * q, 2)]
    pltpu.make_async_copy(blocks, blocks, sems.at[slot, q]).wait()


def forward_kernel(n_msgs, rows, ctl, *refs):
    near, far = refs[:n_msgs], refs[n_msgs:2 * n_msgs]
    window, recv, vec_in = refs[2 * n_msgs:2 * n_msgs + 3]
    act, xs, ls, w_scr, x_scr, lin_scr, vec, act_scr, sems, sem_x, sem_v, sem_o = refs[-12:]
    active, stage, batch, x_me, core, first, xl = (ctl[i] for i in range(7))

    @pl.when(active == 1)
    def _():
        groups = weight_copies(near, far, w_scr, sems, x_me, core)
        per_half = window.shape[0] // 2
        at = pl.multiple_of(batch * rows, rows)

        @pl.when(stage == 0)
        def _():
            src = window.at[pl.ds(pl.multiple_of(xl * per_half + batch * rows, rows), rows), :]
            pltpu.make_async_copy(src, x_scr.at[0], sem_x).start()

        @pl.when(stage != 0)
        def _():
            pltpu.make_async_copy(recv, x_scr.at[0], sem_x).start()

        vec_copy = pltpu.make_async_copy(vec_in, vec, sem_v)
        vec_copy.start()
        issue(groups, first)
        vec_copy.wait()
        pltpu.make_async_copy(recv, x_scr.at[0], sem_x).wait()
        outs = []
        for layer in range(2):
            slot = first ^ layer
            lin_scr[layer] = jnp.broadcast_to(vec[layer, 0:1, :], (rows, D))

            @pl.loop(0, NQ)
            def _(q):
                wait_pair(w_scr, sems, slot, q)
                cols = pl.ds(pl.multiple_of(q * 512, 512), 512)
                lin_scr[layer] += jnp.dot(
                    x_scr[layer, :, cols], w_scr[slot, pl.ds(2 * q, 2)].reshape(512, D), preferred_element_type=F32
                )

            lin = lin_scr[layer]
            center, scale = norm_parts(x_scr[layer].astype(F32) + gelu_parts(lin)[0])
            y = (center * scale * vec[layer, 1:2, :] + vec[layer, 2:3, :]).astype(BF16)
            if layer == 0:
                x_scr[1] = y
            else:
                act_scr[...] = y
                outs.append(pltpu.make_async_copy(act_scr, act, sem_v))
                outs[-1].start()
            for src, dst, n in ((x_scr, xs, 0), (lin_scr, ls, 1)):
                copy = pltpu.make_async_copy(src.at[layer], dst.at[layer, pl.ds(at, rows), :], sem_o.at[layer, n])
                copy.start()
                outs.append(copy)
        for copy in outs:
            copy.wait()


def backward_kernel(n_msgs, rows, ctl, *refs):
    near, far = refs[:n_msgs], refs[n_msgs:2 * n_msgs]
    cot, recv, vec_in, xs, ls = refs[2 * n_msgs:2 * n_msgs + 5]
    back, own_0, own_1, other_0, other_1, zero = refs[-18:-12]
    zero[0] = 0
    w_scr, g_scr, x_scr, lin_scr, dz_scr, dl_scr, vec, back_scr, sems, sem_x, sem_v, sem_o = refs[-12:]
    active, stage, batch, x_me, core, first, xl = (ctl[i] for i in range(7))

    @pl.when(active == 1)
    def _():
        groups = weight_copies(near, far, w_scr, sems, x_me, core)
        per_half = cot.shape[0] // 2
        at = pl.multiple_of(batch * rows, rows)

        @pl.when(stage == 3)
        def _():
            src = cot.at[pl.ds(pl.multiple_of(xl * per_half + batch * rows, rows), rows), :]
            pltpu.make_async_copy(src, g_scr, sem_x.at[2, 0]).start()

        @pl.when(stage != 3)
        def _():
            pltpu.make_async_copy(recv, g_scr, sem_x.at[2, 0]).start()

        loads = {}
        for layer in (1, 0):
            loads[layer] = (
                pltpu.make_async_copy(xs.at[layer, pl.ds(at, rows), :], x_scr.at[layer], sem_x.at[layer, 0]),
                pltpu.make_async_copy(ls.at[layer, pl.ds(at, rows), :], lin_scr.at[layer], sem_x.at[layer, 1]),
            )
            for copy in loads[layer]:
                copy.start()
        vec_copy = pltpu.make_async_copy(vec_in, vec, sem_v)
        vec_copy.start()
        issue(groups, 1 - first)
        vec_copy.wait()
        pltpu.make_async_copy(recv, g_scr, sem_x.at[2, 0]).wait()
        outs = []
        for layer in (1, 0):
            slot = first ^ layer
            for copy in loads[layer]:
                copy.wait()
            lin = lin_scr[layer]
            gated, t, square = gelu_parts(lin)
            center, scale = norm_parts(x_scr[layer].astype(F32) + gated)
            unit = center * scale
            g = g_scr[...].astype(F32) * vec[layer, 1:2, :]
            dz = scale * (g - jnp.mean(g, axis=-1, keepdims=True) - unit * jnp.mean(g * unit, axis=-1, keepdims=True))
            dz_scr[...] = dz
            dl_scr[layer] = (dz * gelu_slope(lin, t, square)).astype(BF16)
            for is_own, pair in ((1, (own_0, own_1)), (0, (other_0, other_1))):
                for m, dst in enumerate(pair):

                    @pl.when((batch == m) & ((xl == layer) == (is_own == 1)))
                    def _():
                        pltpu.make_async_copy(dl_scr.at[layer], dst, sem_o.at[layer]).start()

            outs.append(pltpu.make_async_copy(dl_scr.at[layer], own_0, sem_o.at[layer]))

            @pl.loop(0, NQ)
            def _(q):
                wait_pair(w_scr, sems, slot, q)
                cols = pl.ds(pl.multiple_of(q * 512, 512), 512)

                def step():
                    down = lax.dot_general(
                        dl_scr[layer], w_scr[slot, pl.ds(2 * q, 2)].reshape(512, D), (((1,), (1,)), ((), ())), preferred_element_type=F32
                    )
                    y = (dz_scr[:, cols] + down).astype(BF16)
                    if layer == 1:
                        g_scr[:, cols] = y
                    else:
                        back_scr[:, cols] = y

                if layer == 1:
                    step()
                else:
                    pl.when(stage != 0)(step)
        outs.append(pltpu.make_async_copy(back_scr, back, sem_v))
        outs[-1].start()
        for copy in outs:
            copy.wait()


def forward_call(ctl, near, far, window, recv, vec, stash, early):
    rows = recv.shape[0]
    tokens = window.shape[0] // 2
    n = len(near)
    any_spec = pl.BlockSpec(memory_space=pl.ANY)
    return pl.pallas_call(
        functools.partial(forward_kernel, n, rows),
        out_shape=(
            jax.ShapeDtypeStruct((rows, D), BF16),
            jax.ShapeDtypeStruct((2, tokens, D), BF16),
            jax.ShapeDtypeStruct((2, tokens, D), F32),
        ),
        in_specs=[pl.BlockSpec(memory_space=pltpu.SMEM)] + [any_spec] * (2 * n + 3 + len(stash) + len(early)),
        out_specs=(any_spec, any_spec, any_spec),
        scratch_shapes=[
            pltpu.VMEM((2, 8, 2, 2, 64, D), BF16),
            pltpu.VMEM((2, rows, D), BF16),
            pltpu.VMEM((2, rows, D), F32),
            pltpu.VMEM(vec.shape, F32),
            pltpu.VMEM((rows, D), BF16),
            pltpu.SemaphoreType.DMA((2, NQ)),
            pltpu.SemaphoreType.DMA,
            pltpu.SemaphoreType.DMA,
            pltpu.SemaphoreType.DMA((2, 2)),
        ],
        input_output_aliases={2 * n + 4 + i: 1 + i for i in range(len(stash))},
        compiler_params=pltpu.CompilerParams(vmem_limit_bytes=VMEM_LIMIT),
        cost_estimate=pl.CostEstimate(flops=4 * rows * D * D, bytes_accessed=4 * D * D, transcendentals=2 * rows * D),
        name="forward_tick",
    )(ctl, *near, *far, window, recv, vec, *stash, *early)


def backward_call(ctl, near, far, cot, recv, vec, xs, ls, stash, early=()):
    rows = recv.shape[0]
    n = len(near)
    any_spec = pl.BlockSpec(memory_space=pl.ANY)
    return pl.pallas_call(
        functools.partial(backward_kernel, n, rows),
        out_shape=(jax.ShapeDtypeStruct((rows, D), BF16),) * 5 + (jax.ShapeDtypeStruct((1,), jnp.int32),),
        in_specs=[pl.BlockSpec(memory_space=pltpu.SMEM)] + [any_spec] * (2 * n + 5 + len(stash) + len(early)),
        out_specs=(any_spec,) * 5 + (pl.BlockSpec(memory_space=pltpu.SMEM),),
        scratch_shapes=[
            pltpu.VMEM((2, 8, 2, 2, 64, D), BF16),
            pltpu.VMEM((rows, D), BF16),
            pltpu.VMEM((2, rows, D), BF16),
            pltpu.VMEM((2, rows, D), F32),
            pltpu.VMEM((rows, D), F32),
            pltpu.VMEM((2, rows, D), BF16),
            pltpu.VMEM(vec.shape, F32),
            pltpu.VMEM((rows, D), BF16),
            pltpu.SemaphoreType.DMA((2, NQ)),
            pltpu.SemaphoreType.DMA((3, 2)),
            pltpu.SemaphoreType.DMA,
            pltpu.SemaphoreType.DMA((2,)),
        ],
        input_output_aliases={2 * n + 6 + i: 1 + i for i in range(len(stash))},
        compiler_params=pltpu.CompilerParams(vmem_limit_bytes=VMEM_LIMIT),
        cost_estimate=pl.CostEstimate(flops=4 * rows * D * D, bytes_accessed=4 * D * D, transcendentals=2 * rows * D),
        name="backward_tick",
    )(ctl, *near, *far, cot, recv, vec, xs, ls, *stash, *early)

AXES = ("y", "xl", "z", "xh", "c")
MICRO = 2
STAGES = 4

FIRST_DECAY = 0.9
SECOND_DECAY = 0.999
STEP_SIZE = 0.01
EPSILON = 1e-08
FIRST_CORRECTION = 1.0 - 0.9**10
SECOND_CORRECTION = 1.0 - 0.999**10


def shift_x(v, by):
    place = lambda x: (x & 1) * 2 + (x >> 1)
    return lax.ppermute(v, ("xl", "xh"), [(place(x), place((x + by) % 4)) for x in range(4)])


def shift_z(v, by):
    return lax.ppermute(v, "z", [(z, (z + by) % 8) for z in range(8)])


def swap_core(v):
    return lax.ppermute(v, "c", [(0, 1), (1, 0)])


def shift_x_in(v, by, planes):
    place = lambda y, x, c: (y * 4 + (x & 1) * 2 + (x >> 1)) * 2 + c
    pairs = []
    for y in range(STAGES):
        for x in range(4):
            for c in range(2):
                to = (y, (x + by) % 4, c) if y in planes else (y, x, 1 - c)
                pairs.append((place(y, x, c), place(*to)))
    return lax.ppermute(v, ("y", "xl", "xh", "c"), pairs)


def swap_pair(v):
    return lax.ppermute(v, "xl", [(0, 1), (1, 0)])


def swap_cross(v):
    to = {3: 4, 4: 3}
    pairs = [(s * 2 + c, to[s] * 2 + c if s in to else s * 2 + 1 - c) for s in range(8) for c in range(2)]
    return lax.ppermute(v, ("y", "xl", "c"), pairs)


def ring_gather(v, shift, steps):
    right = left = v
    out = []
    for _ in range(1, steps):
        right, left = shift(right, 1), shift(left, -1)
        out += [right, left]
    half = v.shape[0] // 2
    return out + [shift(right[:half], 1), shift(left[half:], -1)]


def after_kernel(*refs):
    del refs


def after(v, *others):
    return pl.pallas_call(
        after_kernel,
        out_shape=jax.ShapeDtypeStruct(v.shape, v.dtype),
        in_specs=[pl.BlockSpec(memory_space=pl.ANY)] * (1 + len(others)),
        out_specs=pl.BlockSpec(memory_space=pl.ANY),
        input_output_aliases={0: 0},
        compiler_params=pltpu.CompilerParams(vmem_limit_bytes=VMEM_LIMIT),
        name="after",
    )(v, *others)


def place_kernel(at, *refs):
    blocks, out, sem = refs[:9], refs[9], refs[10]
    for i, block in enumerate(blocks[:7]):
        pltpu.make_async_copy(block, out.at[at[i]], sem).start()
    for i, block in enumerate(blocks[7:]):
        pltpu.make_async_copy(block, out.at[at[7], pl.ds(16 * i, 16), :], sem).start()
    pltpu.make_async_copy(out, out, sem).wait()


def place(blocks, at):
    return pl.pallas_call(
        place_kernel,
        out_shape=jax.ShapeDtypeStruct((8, 32, D), BF16),
        in_specs=[pl.BlockSpec(memory_space=pltpu.SMEM)] + [pl.BlockSpec(memory_space=pl.ANY)] * 9,
        out_specs=pl.BlockSpec(memory_space=pltpu.VMEM),
        scratch_shapes=[pltpu.SemaphoreType.DMA],
        compiler_params=pltpu.CompilerParams(vmem_limit_bytes=VMEM_LIMIT),
        cost_estimate=pl.CostEstimate(flops=0, bytes_accessed=2 << 20, transcendentals=0),
        name="place_blocks",
    )(at, *blocks)


def gather_plane(rows, x_me, xh, z_me, moved, other):
    a, b = rows[:32], rows[32:]
    lower, upper, across = shift_x(a, 1), shift_x(a, -1), shift_x(a, 2)
    own_first, lower_first = xh == 0, lax.rem(x_me + 3, 4) < 2
    heads = jnp.stack(
        [
            jnp.stack([jnp.where(own_first, a, across), jnp.where(own_first, across, a)]),
            jnp.stack([jnp.where(lower_first, lower, upper), jnp.where(lower_first, upper, lower)]),
        ]
    )
    heads = lax.all_gather(heads, "z", axis=0)
    z_from = lax.rem(z_me + 8 + jnp.array((0, -1, 1, -2, 2, -3, 3, 4), jnp.int32), 8)
    tails = after(place([b] + ring_gather(b, shift_z, 4), z_from), moved)
    right, left = shift_x(tails, 1), shift_x(tails, -1)
    ends = [shift_x(right[:4], 1), shift_x(left[4:], -1)]
    return [after(heads, *ends, other), tails, right, left] + ends


def add_rounded(a, b):
    return (a.astype(F32) + b.astype(F32)).astype(BF16)


def ring_reduce(chunks, far_low, far_high, shift, steps):
    half = chunks.shape[1] // 2
    right, left = shift(far_low, 1), shift(far_high, -1)
    for k in range(steps - 1, 0, -1):
        up, down = chunks[k], chunks[2 * steps - k]
        if k == steps - 1:
            right = jnp.concatenate([add_rounded(up[:half], right), up[half:]], axis=0)
            left = jnp.concatenate([down[:half], add_rounded(down[half:], left)], axis=0)
        else:
            right, left = add_rounded(up, right), add_rounded(down, left)
        right, left = shift(right, 1), shift(left, -1)
    return chunks[0].astype(F32) + right.astype(F32) + left.astype(F32)


def grad_kernel(n_inputs, z_ref, *refs):
    n_parts = len(refs) - 2 * n_inputs - 6
    inputs, parts = refs[:2 * n_inputs], refs[2 * n_inputs:2 * n_inputs + n_parts]
    g, far_low, far_high, x_scr, d_scr, sem = refs[2 * n_inputs + n_parts:]
    size, width = parts[0].shape[0], inputs[0].shape[-1]
    for which in range(2):

        @pl.when(z_ref[1] == which)
        def _():
            for i, part in enumerate(inputs[which * n_inputs:(which + 1) * n_inputs]):
                pltpu.make_async_copy(part, x_scr.at[:, :, pl.ds(i * width, width)], sem.at[0]).start()

    for i, part in enumerate(parts):
        pltpu.make_async_copy(part, d_scr.at[pl.ds(i * size, size), :], sem.at[1]).start()
    pltpu.make_async_copy(x_scr, x_scr, sem.at[0]).wait()
    pltpu.make_async_copy(d_scr, d_scr, sem.at[1]).wait()
    z_me = z_ref[0]

    @pl.loop(0, D // 256)
    def _(n):
        cols = pl.ds(pl.multiple_of(n * 256, 256), 256)
        part = jnp.dot(x_scr[...].reshape(512, -1), d_scr[:, cols], preferred_element_type=F32).astype(BF16)
        part = part.reshape(8, 64, 256)
        for z in range(8):
            g[lax.rem(z - z_me + 8, 8), :, cols] = part[z]
        far_low[:, cols] = g[4, :32, cols]
        far_high[:, cols] = g[4, 32:, cols]


def grad_call(z_me, which, inputs, parts):
    n = len(inputs[0])
    tokens = inputs[0][0].shape[-1] * n
    vm = pl.BlockSpec(memory_space=pltpu.VMEM)
    half = jax.ShapeDtypeStruct((32, D), BF16)
    return pl.pallas_call(
        functools.partial(grad_kernel, n),
        out_shape=(jax.ShapeDtypeStruct((8, 64, D), BF16), half, half),
        in_specs=[pl.BlockSpec(memory_space=pltpu.SMEM)]
        + [pl.BlockSpec(memory_space=pl.ANY)] * (2 * n + len(parts)),
        out_specs=(vm, vm, vm),
        scratch_shapes=[
            pltpu.VMEM((8, 64, tokens), BF16),
            pltpu.VMEM((tokens, D), BF16),
            pltpu.SemaphoreType.DMA((2,)),
        ],
        compiler_params=pltpu.CompilerParams(vmem_limit_bytes=VMEM_LIMIT),
        cost_estimate=pl.CostEstimate(flops=2 * tokens * D * 512, bytes_accessed=7 << 20, transcendentals=0),
        name="weight_grads",
    )(jnp.stack([z_me, which]), *inputs[0], *inputs[1], *parts)


def trade_inputs(xs, x_me, core, planes):
    tokens = xs.shape[1]
    xt = jnp.swapaxes(xs, 1, 2).reshape(2, 8, 2, 2, 64, tokens)
    mine = lax.dynamic_index_in_dim(xt, core, 3, keepdims=False)
    theirs = lax.dynamic_index_in_dim(xt, 1 - core, 3, keepdims=False)
    both = jnp.concatenate([mine, swap_core(theirs)], axis=-1)

    def meant_for(step):
        x = lax.rem(x_me + step, 4)
        block = lax.dynamic_index_in_dim(both, x % 2, 0, keepdims=False)
        return lax.dynamic_index_in_dim(block, x // 2, 1, keepdims=False)

    return [meant_for(0)] + [shift_x_in(meant_for(by % 4), by, planes) for by in (1, -1, 2)]


def trade_slopes(own, other):
    parts = []
    for part in (own, shift_x(other, 1), shift_x(other, -1), shift_x(own, 2)):
        parts += [part, swap_core(part)]
    return parts


def shards(master_old, first_old, second_old, layer_vectors, new_section, frozen, window_input, cotangent):
    y, xl, z_me, xh, core = (lax.axis_index(name) for name in AXES)
    section = y * 2 + xl
    x_me = xl + 2 * xh
    goal = jnp.maximum(new_section[0], new_section[1])
    in_plane = goal // 2 == y
    label = jnp.where(in_plane, goal & 1, xl)

    held_of = lambda v: jnp.where(new_section[1] >= 0, v[1], v[0])
    own_rows, own_vec = held_of(master_old).astype(BF16), held_of(layer_vectors)
    own_vec = jnp.where(in_plane, own_vec, swap_cross(own_vec))
    other_vec = swap_pair(own_vec)
    vec = jnp.where(label == 0, jnp.stack([own_vec, other_vec]), jnp.stack([other_vec, own_vec])).astype(F32)
    states = (master_old, first_old, second_old)
    held = jnp.stack([held_of(s) for s in states])
    from_pair, from_cross = swap_pair(held), swap_cross(held)
    rows_here = jnp.where(in_plane, own_rows, swap_cross(own_rows))
    near = gather_plane(rows_here, x_me, xh, z_me, from_pair, vec)
    far = [swap_core(m) for m in near]

    tokens = window_input.shape[0] // 2
    rows = tokens // MICRO
    stash = slope_stash = ()
    slopes, inputs = [], []
    ahead = behind = rows_here

    def control(batch):
        active = (batch >= 0) & (batch < MICRO)
        slot = jnp.clip(batch, 0, MICRO - 1)
        parts = [active, y, slot, x_me, core, label, xl]
        return jnp.stack([jnp.asarray(p, jnp.int32) for p in parts])

    for tick in range(MICRO + 2 * STAGES - 2):
        f_stages = [s for s in range(STAGES) if 0 <= tick - s < MICRO]
        b_stages = [s for s in range(STAGES) if 0 <= tick - 2 * (STAGES - 1) + s < MICRO]
        if f_stages:
            early = tuple(inputs[0][1:]) if tick == 3 else ()
            act, xs, ls = forward_call(control(tick - y), near, far, window_input, ahead, vec, stash, early)
            stash = (xs, ls)
            if tick == 2:
                inputs.append(trade_inputs(xs, x_me, core, (0, 1)))
            pairs = [(s, s + 1) for s in f_stages if s + 1 < STAGES]
            if pairs:
                ahead = lax.ppermute(act, "y", pairs)
        if b_stages:
            early = ()
            if tick == 6:
                early = (from_cross,)
            if tick == 7:
                early = tuple(inputs[1][1:])
            back, *slope_stash, zero = backward_call(
                control(tick - 2 * (STAGES - 1) + y), near, far, cotangent, behind, vec, *stash, tuple(slope_stash), early
            )
            pairs = [(s, s - 1) for s in b_stages if s > 0]
            if pairs:
                behind = lax.ppermute(back, "y", pairs)
            if tick == 5:
                inputs.append(trade_inputs(jnp.where(zero[0] == 0, stash[0], 0), x_me, core, (2, 3)))
            if tick >= 6:
                slopes.append(trade_slopes(slope_stash[tick - 6], slope_stash[2 + tick - 6]))

    kept = jnp.where(goal == section, held, jnp.where(in_plane, from_pair, from_cross))
    master, first_state, second_state = kept[0], kept[1], kept[2]

    parts = [slopes[m][i] for i in range(8) for m in range(MICRO)]
    grad_rows = ring_reduce(*grad_call(z_me, y // 2, inputs, parts), shift_z, 4)
    learning = lax.dynamic_index_in_dim(frozen, section, 0, keepdims=False) == 0
    first_next = FIRST_DECAY * first_state + (1.0 - FIRST_DECAY) * grad_rows
    second_next = SECOND_DECAY * second_state + (1.0 - SECOND_DECAY) * grad_rows * grad_rows
    stepped = master - STEP_SIZE * (first_next / FIRST_CORRECTION) / (
        jnp.sqrt(second_next / SECOND_CORRECTION) + EPSILON
    )
    master_new = jnp.where(learning, stepped, master)
    first_new = jnp.where(learning, first_next, first_state)
    second_new = jnp.where(learning, second_next, second_state)
    return (master_new[None], first_new[None], second_new[None])


def solution(mesh):
    fine = jax.sharding.Mesh(mesh.devices.reshape(4, 2, 8, 2, 2), AXES)
    sec, rep = ("y", "xl"), ("z", "xh", "c")
    rows = P(sec, rep, None)
    in_specs = (rows, rows, rows, P(sec, None, None), P(sec), P(), P(rep, None), P(rep, None))
    return jax.shard_map(shards, mesh=fine, in_specs=in_specs, out_specs=(rows, rows, rows), check_vma=False)
```

```python
import functools
import jax
import jax.numpy as jnp
from jax import lax
from jax.experimental import pallas as pl
from jax.experimental.pallas import tpu as pltpu
from jax.sharding import PartitionSpec as P

BF16 = jnp.bfloat16
F32 = jnp.float32
D = 2048
NQ = 4
VMEM_LIMIT = 64 * 1024 * 1024 - 65536
GELU_K = 0.7978845608028654


def weight_copies(near, far, w_scr, sems, x_me, core):
    copies = ([], [])
    for slot in range(2):
        for q in range(NQ):
            for msgs, owner in ((near, core), (far, 1 - core)):
                src = msgs[0].at[pl.ds(2 * q, 2), slot]
                dst = w_scr.at[slot, pl.ds(2 * q, 2), :, owner, pl.ds(0, 32), :]
                copies[slot].append(pltpu.make_async_copy(src, dst, sems.at[slot, q]))
                for dx in (0, 2) if slot == 0 else (-1, 1):
                    if dx == 2:
                        src = msgs[4 + q // 2].at[pl.ds(2 * (q % 2), 2)]
                    else:
                        src = msgs[(1, 3, 2)[dx]].at[pl.ds(2 * q, 2)]
                    xh = lax.rem(x_me + dx + 4, 4) // 2
                    dst = w_scr.at[slot, pl.ds(2 * q, 2), xh, owner, pl.ds(32, 32), :]
                    copies[slot].append(pltpu.make_async_copy(src, dst, sems.at[slot, q]))
    return copies


def gelu_parts(u):
    square = u * u
    t = jnp.tanh(GELU_K * u * (1.0 + 0.044715 * square))
    return 0.5 * u * (1.0 + t), t, square


def gelu_slope(u, t, square):
    return 0.5 * (1.0 + t) + 0.5 * u * (1.0 - t * t) * (GELU_K * (1.0 + 3 * 0.044715 * square))


def norm_parts(z):
    center = z - jnp.mean(z, axis=-1, keepdims=True)
    spread = jnp.mean(center * center, axis=-1, keepdims=True)
    return center, lax.rsqrt(spread + 1e-5)


def issue(groups, first):
    def start(slot):
        for copy in groups[slot]:
            copy.start()

    @pl.when(first == 0)
    def _():
        start(0)
        start(1)

    @pl.when(first == 1)
    def _():
        start(1)
        start(0)


def wait_pair(w_scr, sems, slot, q):
    blocks = w_scr.at[slot, pl.ds(2 * q, 2)]
    pltpu.make_async_copy(blocks, blocks, sems.at[slot, q]).wait()


def forward_kernel(n_msgs, rows, ctl, *refs):
    near, far = refs[:n_msgs], refs[n_msgs:2 * n_msgs]
    window, recv, vec_in = refs[2 * n_msgs:2 * n_msgs + 3]
    act, xs, ls, w_scr, x_scr, lin_scr, vec, act_scr, sems, sem_x, sem_v, sem_o = refs[-12:]
    active, stage, batch, x_me, core, first, xl = (ctl[i] for i in range(7))

    @pl.when(active == 1)
    def _():
        groups = weight_copies(near, far, w_scr, sems, x_me, core)
        per_half = window.shape[0] // 2
        at = pl.multiple_of(batch * rows, rows)

        @pl.when(stage == 0)
        def _():
            src = window.at[pl.ds(pl.multiple_of(xl * per_half + batch * rows, rows), rows), :]
            pltpu.make_async_copy(src, x_scr.at[0], sem_x).start()

        @pl.when(stage != 0)
        def _():
            pltpu.make_async_copy(recv, x_scr.at[0], sem_x).start()

        vec_copy = pltpu.make_async_copy(vec_in, vec, sem_v)
        vec_copy.start()
        issue(groups, first)
        vec_copy.wait()
        pltpu.make_async_copy(recv, x_scr.at[0], sem_x).wait()
        outs = []
        for layer in range(2):
            slot = first ^ layer
            lin_scr[layer] = jnp.broadcast_to(vec[layer, 0:1, :], (rows, D))

            @pl.loop(0, NQ)
            def _(q):
                wait_pair(w_scr, sems, slot, q)
                cols = pl.ds(pl.multiple_of(q * 512, 512), 512)
                lin_scr[layer] += jnp.dot(
                    x_scr[layer, :, cols], w_scr[slot, pl.ds(2 * q, 2)].reshape(512, D), preferred_element_type=F32
                )

            lin = lin_scr[layer]
            center, scale = norm_parts(x_scr[layer].astype(F32) + gelu_parts(lin)[0])
            y = (center * scale * vec[layer, 1:2, :] + vec[layer, 2:3, :]).astype(BF16)
            if layer == 0:
                x_scr[1] = y
            else:
                act_scr[...] = y
                outs.append(pltpu.make_async_copy(act_scr, act, sem_v))
                outs[-1].start()
            for src, dst, n in ((x_scr, xs, 0), (lin_scr, ls, 1)):
                copy = pltpu.make_async_copy(src.at[layer], dst.at[layer, pl.ds(at, rows), :], sem_o.at[layer, n])
                copy.start()
                outs.append(copy)
        for copy in outs:
            copy.wait()


def backward_kernel(n_msgs, rows, micros, ctl, *refs):
    near, far = refs[:n_msgs], refs[n_msgs:2 * n_msgs]
    cot, recv, vec_in, xs, ls = refs[2 * n_msgs:2 * n_msgs + 5]
    n_micro = len(micros)
    back, *slopes, zero = refs[-14 - 2 * n_micro:-12]
    zero[0] = 0
    w_scr, g_scr, x_scr, lin_scr, dz_scr, dl_scr, vec, back_scr, sems, sem_x, sem_v, sem_o = refs[-12:]
    active, stage, batch, x_me, core, first, xl = (ctl[i] for i in range(7))

    @pl.when(active == 1)
    def _():
        groups = weight_copies(near, far, w_scr, sems, x_me, core)
        per_half = cot.shape[0] // 2
        at = pl.multiple_of(batch * rows, rows)

        @pl.when(stage == 3)
        def _():
            src = cot.at[pl.ds(pl.multiple_of(xl * per_half + batch * rows, rows), rows), :]
            pltpu.make_async_copy(src, g_scr, sem_x.at[2, 0]).start()

        @pl.when(stage != 3)
        def _():
            pltpu.make_async_copy(recv, g_scr, sem_x.at[2, 0]).start()

        loads = {}
        for layer in (1, 0):
            loads[layer] = (
                pltpu.make_async_copy(xs.at[layer, pl.ds(at, rows), :], x_scr.at[layer], sem_x.at[layer, 0]),
                pltpu.make_async_copy(ls.at[layer, pl.ds(at, rows), :], lin_scr.at[layer], sem_x.at[layer, 1]),
            )
            for copy in loads[layer]:
                copy.start()
        vec_copy = pltpu.make_async_copy(vec_in, vec, sem_v)
        vec_copy.start()
        issue(groups, 1 - first)
        vec_copy.wait()
        pltpu.make_async_copy(recv, g_scr, sem_x.at[2, 0]).wait()
        outs = []
        for layer in (1, 0):
            slot = first ^ layer
            for copy in loads[layer]:
                copy.wait()
            lin = lin_scr[layer]
            gated, t, square = gelu_parts(lin)
            center, scale = norm_parts(x_scr[layer].astype(F32) + gated)
            unit = center * scale
            g = g_scr[...].astype(F32) * vec[layer, 1:2, :]
            dz = scale * (g - jnp.mean(g, axis=-1, keepdims=True) - unit * jnp.mean(g * unit, axis=-1, keepdims=True))
            dz_scr[...] = dz
            dl_scr[layer] = (dz * gelu_slope(lin, t, square)).astype(BF16)
            for is_own, dsts in ((1, slopes[:n_micro]), (0, slopes[n_micro:])):
                for m, dst in zip(micros, dsts):

                    @pl.when((batch == m) & ((xl == layer) == (is_own == 1)))
                    def _():
                        pltpu.make_async_copy(dl_scr.at[layer], dst, sem_o.at[layer]).start()

            outs.append(pltpu.make_async_copy(dl_scr.at[layer], slopes[0], sem_o.at[layer]))

            @pl.loop(0, NQ)
            def _(q):
                wait_pair(w_scr, sems, slot, q)
                cols = pl.ds(pl.multiple_of(q * 512, 512), 512)

                def step():
                    down = lax.dot_general(
                        dl_scr[layer], w_scr[slot, pl.ds(2 * q, 2)].reshape(512, D), (((1,), (1,)), ((), ())), preferred_element_type=F32
                    )
                    y = (dz_scr[:, cols] + down).astype(BF16)
                    if layer == 1:
                        g_scr[:, cols] = y
                    else:
                        back_scr[:, cols] = y

                if layer == 1:
                    step()
                else:
                    pl.when(stage != 0)(step)
        outs.append(pltpu.make_async_copy(back_scr, back, sem_v))
        outs[-1].start()
        for copy in outs:
            copy.wait()


def forward_call(ctl, near, far, window, recv, vec, stash, early):
    rows = recv.shape[0]
    tokens = window.shape[0] // 2
    n = len(near)
    any_spec = pl.BlockSpec(memory_space=pl.ANY)
    return pl.pallas_call(
        functools.partial(forward_kernel, n, rows),
        out_shape=(
            jax.ShapeDtypeStruct((rows, D), BF16),
            jax.ShapeDtypeStruct((2, tokens, D), BF16),
            jax.ShapeDtypeStruct((2, tokens, D), F32),
        ),
        in_specs=[pl.BlockSpec(memory_space=pltpu.SMEM)] + [any_spec] * (2 * n + 3 + len(stash) + len(early)),
        out_specs=(any_spec, any_spec, any_spec),
        scratch_shapes=[
            pltpu.VMEM((2, 8, 2, 2, 64, D), BF16),
            pltpu.VMEM((2, rows, D), BF16),
            pltpu.VMEM((2, rows, D), F32),
            pltpu.VMEM(vec.shape, F32),
            pltpu.VMEM((rows, D), BF16),
            pltpu.SemaphoreType.DMA((2, NQ)),
            pltpu.SemaphoreType.DMA,
            pltpu.SemaphoreType.DMA,
            pltpu.SemaphoreType.DMA((2, 2)),
        ],
        input_output_aliases={2 * n + 4 + i: 1 + i for i in range(len(stash))},
        compiler_params=pltpu.CompilerParams(vmem_limit_bytes=VMEM_LIMIT),
        cost_estimate=pl.CostEstimate(flops=4 * rows * D * D, bytes_accessed=4 * D * D, transcendentals=2 * rows * D),
        name="forward_tick",
    )(ctl, *near, *far, window, recv, vec, *stash, *early)


def backward_call(ctl, near, far, cot, recv, vec, xs, ls, micros, stash, early):
    rows = recv.shape[0]
    n = len(near)
    any_spec = pl.BlockSpec(memory_space=pl.ANY)
    return pl.pallas_call(
        functools.partial(backward_kernel, n, rows, micros),
        out_shape=(jax.ShapeDtypeStruct((rows, D), BF16),) * (1 + 2 * len(micros)) + (jax.ShapeDtypeStruct((1,), jnp.int32),),
        in_specs=[pl.BlockSpec(memory_space=pltpu.SMEM)] + [any_spec] * (2 * n + 5 + len(stash) + len(early)),
        out_specs=(any_spec,) * (1 + 2 * len(micros)) + (pl.BlockSpec(memory_space=pltpu.SMEM),),
        scratch_shapes=[
            pltpu.VMEM((2, 8, 2, 2, 64, D), BF16),
            pltpu.VMEM((rows, D), BF16),
            pltpu.VMEM((2, rows, D), BF16),
            pltpu.VMEM((2, rows, D), F32),
            pltpu.VMEM((rows, D), F32),
            pltpu.VMEM((2, rows, D), BF16),
            pltpu.VMEM(vec.shape, F32),
            pltpu.VMEM((rows, D), BF16),
            pltpu.SemaphoreType.DMA((2, NQ)),
            pltpu.SemaphoreType.DMA((3, 2)),
            pltpu.SemaphoreType.DMA,
            pltpu.SemaphoreType.DMA((2,)),
        ],
        input_output_aliases={2 * n + 6 + i: 1 + i for i in range(len(stash))},
        compiler_params=pltpu.CompilerParams(vmem_limit_bytes=VMEM_LIMIT),
        cost_estimate=pl.CostEstimate(flops=4 * rows * D * D, bytes_accessed=4 * D * D, transcendentals=2 * rows * D),
        name="backward_tick",
    )(ctl, *near, *far, cot, recv, vec, xs, ls, *stash, *early)

AXES = ("y", "xl", "z", "xh", "c")
MICRO = 2
STAGES = 4

FIRST_DECAY = 0.9
SECOND_DECAY = 0.999
STEP_SIZE = 0.01
EPSILON = 1e-08
FIRST_CORRECTION = 1.0 - 0.9**10
SECOND_CORRECTION = 1.0 - 0.999**10


def shift_x(v, by):
    place = lambda x: (x & 1) * 2 + (x >> 1)
    return lax.ppermute(v, ("xl", "xh"), [(place(x), place((x + by) % 4)) for x in range(4)])


def shift_z(v, by):
    return lax.ppermute(v, "z", [(z, (z + by) % 8) for z in range(8)])


def swap_core(v):
    return lax.ppermute(v, "c", [(0, 1), (1, 0)])


def shift_x_in(v, by, planes):
    place = lambda y, x, c: (y * 4 + (x & 1) * 2 + (x >> 1)) * 2 + c
    pairs = []
    for y in range(STAGES):
        for x in range(4):
            for c in range(2):
                to = (y, (x + by) % 4, c) if y in planes else (y, x, 1 - c)
                pairs.append((place(y, x, c), place(*to)))
    return lax.ppermute(v, ("y", "xl", "xh", "c"), pairs)


def swap_pair(v):
    return lax.ppermute(v, "xl", [(0, 1), (1, 0)])


def swap_cross(v):
    to = {3: 4, 4: 3}
    pairs = [(s * 2 + c, to[s] * 2 + c if s in to else s * 2 + 1 - c) for s in range(8) for c in range(2)]
    return lax.ppermute(v, ("y", "xl", "c"), pairs)


def ring_gather(v, shift, steps):
    right = left = v
    out = []
    for _ in range(1, steps):
        right, left = shift(right, 1), shift(left, -1)
        out += [right, left]
    half = v.shape[0] // 2
    return out + [shift(right[:half], 1), shift(left[half:], -1)]


def after_kernel(*refs):
    del refs


def after(v, *others):
    return pl.pallas_call(
        after_kernel,
        out_shape=jax.ShapeDtypeStruct(v.shape, v.dtype),
        in_specs=[pl.BlockSpec(memory_space=pl.ANY)] * (1 + len(others)),
        out_specs=pl.BlockSpec(memory_space=pl.ANY),
        input_output_aliases={0: 0},
        compiler_params=pltpu.CompilerParams(vmem_limit_bytes=VMEM_LIMIT),
        name="after",
    )(v, *others)


def place_kernel(at, *refs):
    blocks, out, sem = refs[:9], refs[9], refs[10]
    for i, block in enumerate(blocks[:7]):
        pltpu.make_async_copy(block, out.at[at[i]], sem).start()
    for i, block in enumerate(blocks[7:]):
        pltpu.make_async_copy(block, out.at[at[7], pl.ds(16 * i, 16), :], sem).start()
    pltpu.make_async_copy(out, out, sem).wait()


def place(blocks, at):
    return pl.pallas_call(
        place_kernel,
        out_shape=jax.ShapeDtypeStruct((8, 32, D), BF16),
        in_specs=[pl.BlockSpec(memory_space=pltpu.SMEM)] + [pl.BlockSpec(memory_space=pl.ANY)] * 9,
        out_specs=pl.BlockSpec(memory_space=pltpu.VMEM),
        scratch_shapes=[pltpu.SemaphoreType.DMA],
        compiler_params=pltpu.CompilerParams(vmem_limit_bytes=VMEM_LIMIT),
        cost_estimate=pl.CostEstimate(flops=0, bytes_accessed=2 << 20, transcendentals=0),
        name="place_blocks",
    )(at, *blocks)


def gather_plane(rows, x_me, xh, z_me, moved):
    a, b = rows[:32], rows[32:]
    lower, upper, across = shift_x(a, 1), shift_x(a, -1), shift_x(a, 2)
    own_first, lower_first = xh == 0, lax.rem(x_me + 3, 4) < 2
    heads = jnp.stack(
        [
            jnp.stack([jnp.where(own_first, a, across), jnp.where(own_first, across, a)]),
            jnp.stack([jnp.where(lower_first, lower, upper), jnp.where(lower_first, upper, lower)]),
        ]
    )
    heads = lax.all_gather(heads, "z", axis=0)
    z_from = lax.rem(z_me + 8 + jnp.array((0, -1, 1, -2, 2, -3, 3, 4), jnp.int32), 8)
    tails = after(place([b] + ring_gather(b, shift_z, 4), z_from), *moved)
    right, left = shift_x(tails, 1), shift_x(tails, -1)
    ends = [shift_x(right[:4], 1), shift_x(left[4:], -1)]
    return [after(heads, right, left), tails, right, left] + ends


def add_rounded(a, b):
    return (a.astype(F32) + b.astype(F32)).astype(BF16)


def ring_reduce(chunks, far_low, far_high, shift, steps):
    half = chunks.shape[1] // 2
    right, left = shift(far_low, 1), shift(far_high, -1)
    for k in range(steps - 1, 0, -1):
        up, down = chunks[k], chunks[2 * steps - k]
        if k == steps - 1:
            right = jnp.concatenate([add_rounded(up[:half], right), up[half:]], axis=0)
            left = jnp.concatenate([down[:half], add_rounded(down[half:], left)], axis=0)
        else:
            right, left = add_rounded(up, right), add_rounded(down, left)
        right, left = shift(right, 1), shift(left, -1)
    return chunks[0].astype(F32) + right.astype(F32) + left.astype(F32)


def grad_kernel(n_inputs, z_ref, *refs):
    n_parts = len(refs) - 2 * n_inputs - 6
    inputs, parts = refs[:2 * n_inputs], refs[2 * n_inputs:2 * n_inputs + n_parts]
    g, far_low, far_high, x_scr, d_scr, sem = refs[2 * n_inputs + n_parts:]
    size, width = parts[0].shape[0], inputs[0].shape[-1]
    for which in range(2):

        @pl.when(z_ref[1] == which)
        def _():
            for i, part in enumerate(inputs[which * n_inputs:(which + 1) * n_inputs]):
                pltpu.make_async_copy(part, x_scr.at[:, :, pl.ds(i * width, width)], sem.at[0]).start()

    for i, part in enumerate(parts):
        pltpu.make_async_copy(part, d_scr.at[pl.ds(i * size, size), :], sem.at[1]).start()
    pltpu.make_async_copy(x_scr, x_scr, sem.at[0]).wait()
    pltpu.make_async_copy(d_scr, d_scr, sem.at[1]).wait()
    z_me = z_ref[0]

    @pl.loop(0, D // 256)
    def _(n):
        cols = pl.ds(pl.multiple_of(n * 256, 256), 256)
        part = jnp.dot(x_scr[...].reshape(512, -1), d_scr[:, cols], preferred_element_type=F32).astype(BF16)
        part = part.reshape(8, 64, 256)
        for z in range(8):
            g[lax.rem(z - z_me + 8, 8), :, cols] = part[z]
        far_low[:, cols] = g[4, :32, cols]
        far_high[:, cols] = g[4, 32:, cols]


def grad_call(z_me, which, inputs, parts):
    n = len(inputs[0])
    tokens = inputs[0][0].shape[-1] * n
    vm = pl.BlockSpec(memory_space=pltpu.VMEM)
    half = jax.ShapeDtypeStruct((32, D), BF16)
    return pl.pallas_call(
        functools.partial(grad_kernel, n),
        out_shape=(jax.ShapeDtypeStruct((8, 64, D), BF16), half, half),
        in_specs=[pl.BlockSpec(memory_space=pltpu.SMEM)]
        + [pl.BlockSpec(memory_space=pl.ANY)] * (2 * n + len(parts)),
        out_specs=(vm, vm, vm),
        scratch_shapes=[
            pltpu.VMEM((8, 64, tokens), BF16),
            pltpu.VMEM((tokens, D), BF16),
            pltpu.SemaphoreType.DMA((2,)),
        ],
        compiler_params=pltpu.CompilerParams(vmem_limit_bytes=VMEM_LIMIT),
        cost_estimate=pl.CostEstimate(flops=2 * tokens * D * 512, bytes_accessed=7 << 20, transcendentals=0),
        name="weight_grads",
    )(jnp.stack([z_me, which]), *inputs[0], *inputs[1], *parts)


def trade_inputs(xs, x_me, core, planes):
    tokens = xs.shape[1]
    xt = jnp.swapaxes(xs, 1, 2).reshape(2, 8, 2, 2, 64, tokens)
    mine = lax.dynamic_index_in_dim(xt, core, 3, keepdims=False)
    theirs = lax.dynamic_index_in_dim(xt, 1 - core, 3, keepdims=False)
    both = jnp.concatenate([mine, swap_core(theirs)], axis=-1)

    def meant_for(step):
        x = lax.rem(x_me + step, 4)
        block = lax.dynamic_index_in_dim(both, x % 2, 0, keepdims=False)
        return lax.dynamic_index_in_dim(block, x // 2, 1, keepdims=False)

    return [meant_for(0)] + [shift_x_in(meant_for(by % 4), by, planes) for by in (1, -1, 2)]


def trade_slopes(own, other):
    parts = []
    for part in (own, shift_x(other, 1), shift_x(other, -1), shift_x(own, 2)):
        parts += [part, swap_core(part)]
    return parts


def shards(master_old, first_old, second_old, layer_vectors, new_section, frozen, window_input, cotangent):
    y, xl, z_me, xh, core = (lax.axis_index(name) for name in AXES)
    section = y * 2 + xl
    x_me = xl + 2 * xh
    goal = jnp.maximum(new_section[0], new_section[1])
    in_plane = goal // 2 == y
    label = jnp.where(in_plane, goal & 1, xl)

    held_of = lambda v: jnp.where(new_section[1] >= 0, v[1], v[0])
    own_rows, own_vec = held_of(master_old).astype(BF16), held_of(layer_vectors)
    own_vec = jnp.where(in_plane, own_vec, swap_cross(own_vec))
    other_vec = swap_pair(own_vec)
    vec = jnp.where(label == 0, jnp.stack([own_vec, other_vec]), jnp.stack([other_vec, own_vec])).astype(F32)
    states = (master_old, first_old, second_old)
    held = jnp.stack([held_of(s) for s in states])
    from_pair, from_cross = swap_pair(held), swap_cross(held)
    rows_here = jnp.where(in_plane, own_rows, swap_cross(own_rows))
    near = gather_plane(rows_here, x_me, xh, z_me, (from_pair, vec))
    far = [swap_core(m) for m in near]

    tokens = window_input.shape[0] // 2
    rows = tokens // MICRO
    stash = slope_stash = ()
    slopes, inputs = [], []
    ahead = behind = rows_here

    def control(batch):
        active = (batch >= 0) & (batch < MICRO)
        slot = jnp.clip(batch, 0, MICRO - 1)
        parts = [active, y, slot, x_me, core, label, xl]
        return jnp.stack([jnp.asarray(p, jnp.int32) for p in parts])

    for tick in range(MICRO + 2 * STAGES - 2):
        f_stages = [s for s in range(STAGES) if 0 <= tick - s < MICRO]
        b_stages = [s for s in range(STAGES) if 0 <= tick - 2 * (STAGES - 1) + s < MICRO]
        if f_stages:
            early = tuple(inputs[0][1:]) if tick == 3 else ()
            act, xs, ls = forward_call(control(tick - y), near, far, window_input, ahead, vec, stash, early)
            stash = (xs, ls)
            if tick == 2:
                inputs.append(trade_inputs(xs, x_me, core, (0, 1)))
            pairs = [(s, s + 1) for s in f_stages if s + 1 < STAGES]
            if pairs:
                ahead = lax.ppermute(act, "y", pairs)
        if b_stages:
            early = ()
            if tick == 6:
                early = (from_cross,)
            if tick == 7:
                early = tuple(inputs[1][1:])
            micros = tuple(range(MICRO))
            if tick == 7:
                micros, slope_stash = (1,), slope_stash[1::2]
            back, *slope_stash, zero = backward_call(
                control(tick - 2 * (STAGES - 1) + y),
                near,
                far,
                cotangent,
                behind,
                vec,
                *stash,
                micros,
                tuple(slope_stash),
                early,
            )
            pairs = [(s, s - 1) for s in b_stages if s > 0]
            if pairs:
                behind = lax.ppermute(back, "y", pairs)
            if tick == 5:
                inputs.append(trade_inputs(jnp.where(zero[0] == 0, stash[0], 0), x_me, core, (2, 3)))
            if tick >= 6:
                slopes.append(trade_slopes(slope_stash[0], slope_stash[len(micros)]))

    kept = jnp.where(goal == section, held, jnp.where(in_plane, from_pair, from_cross))
    master, first_state, second_state = kept[0], kept[1], kept[2]

    parts = [slopes[m][i] for i in range(8) for m in range(MICRO)]
    grad_rows = ring_reduce(*grad_call(z_me, y // 2, inputs, parts), shift_z, 4)
    learning = lax.dynamic_index_in_dim(frozen, section, 0, keepdims=False) == 0
    first_next = FIRST_DECAY * first_state + (1.0 - FIRST_DECAY) * grad_rows
    second_next = SECOND_DECAY * second_state + (1.0 - SECOND_DECAY) * grad_rows * grad_rows
    stepped = master - STEP_SIZE * (first_next / FIRST_CORRECTION) / (
        jnp.sqrt(second_next / SECOND_CORRECTION) + EPSILON
    )
    master_new = jnp.where(learning, stepped, master)
    first_new = jnp.where(learning, first_next, first_state)
    second_new = jnp.where(learning, second_next, second_state)
    return (master_new[None], first_new[None], second_new[None])


def solution(mesh):
    fine = jax.sharding.Mesh(mesh.devices.reshape(4, 2, 8, 2, 2), AXES)
    sec, rep = ("y", "xl"), ("z", "xh", "c")
    rows = P(sec, rep, None)
    in_specs = (rows, rows, rows, P(sec, None, None), P(sec), P(), P(rep, None), P(rep, None))
    return jax.shard_map(shards, mesh=fine, in_specs=in_specs, out_specs=(rows, rows, rows), check_vma=False)
```

```python
import functools
import jax
import jax.numpy as jnp
from jax import lax
from jax.experimental import pallas as pl
from jax.experimental.pallas import tpu as pltpu
from jax.sharding import PartitionSpec as P

BF16 = jnp.bfloat16
F32 = jnp.float32
D = 2048
NQ = 4
VMEM_LIMIT = 64 * 1024 * 1024 - 65536
GELU_K = 0.7978845608028654


def weight_copies(near, far, w_scr, sems, x_me, core):
    copies = ([], [])
    for slot in range(2):
        for q in range(NQ):
            for msgs, owner in ((near, core), (far, 1 - core)):
                src = msgs[0].at[pl.ds(2 * q, 2), slot]
                dst = w_scr.at[slot, pl.ds(2 * q, 2), :, owner, pl.ds(0, 32), :]
                copies[slot].append(pltpu.make_async_copy(src, dst, sems.at[slot, q]))
                for dx in (0, 2) if slot == 0 else (-1, 1):
                    if dx == 2:
                        src = msgs[4 + q // 2].at[pl.ds(2 * (q % 2), 2)]
                    else:
                        src = msgs[(1, 3, 2)[dx]].at[pl.ds(2 * q, 2)]
                    xh = lax.rem(x_me + dx + 4, 4) // 2
                    dst = w_scr.at[slot, pl.ds(2 * q, 2), xh, owner, pl.ds(32, 32), :]
                    copies[slot].append(pltpu.make_async_copy(src, dst, sems.at[slot, q]))
    return copies


def gelu_parts(u):
    square = u * u
    t = jnp.tanh(GELU_K * u * (1.0 + 0.044715 * square))
    return 0.5 * u * (1.0 + t), t, square


def gelu_slope(u, t, square):
    return 0.5 * (1.0 + t) + 0.5 * u * (1.0 - t * t) * (GELU_K * (1.0 + 3 * 0.044715 * square))


def norm_parts(z):
    center = z - jnp.mean(z, axis=-1, keepdims=True)
    spread = jnp.mean(center * center, axis=-1, keepdims=True)
    return center, lax.rsqrt(spread + 1e-5)


def issue(groups, first):
    def start(slot):
        for copy in groups[slot]:
            copy.start()

    @pl.when(first == 0)
    def _():
        start(0)
        start(1)

    @pl.when(first == 1)
    def _():
        start(1)
        start(0)


def wait_pair(w_scr, sems, slot, q):
    blocks = w_scr.at[slot, pl.ds(2 * q, 2)]
    pltpu.make_async_copy(blocks, blocks, sems.at[slot, q]).wait()


def forward_kernel(n_msgs, rows, ctl, *refs):
    near, far = refs[:n_msgs], refs[n_msgs:2 * n_msgs]
    window, recv, vec_in = refs[2 * n_msgs:2 * n_msgs + 3]
    act, xs, ls, w_scr, x_scr, lin_scr, vec, act_scr, sems, sem_x, sem_v, sem_o = refs[-12:]
    active, stage, batch, x_me, core, first, xl = (ctl[i] for i in range(7))

    @pl.when(active == 1)
    def _():
        groups = weight_copies(near, far, w_scr, sems, x_me, core)
        per_half = window.shape[0] // 2
        at = pl.multiple_of(batch * rows, rows)

        @pl.when(stage == 0)
        def _():
            src = window.at[pl.ds(pl.multiple_of(xl * per_half + batch * rows, rows), rows), :]
            pltpu.make_async_copy(src, x_scr.at[0], sem_x).start()

        @pl.when(stage != 0)
        def _():
            pltpu.make_async_copy(recv.at[pl.ds(0, rows), :], x_scr.at[0], sem_x).start()

        vec_copy = pltpu.make_async_copy(vec_in, vec, sem_v)
        vec_copy.start()
        issue(groups, first)
        vec_copy.wait()
        pltpu.make_async_copy(recv.at[pl.ds(0, rows), :], x_scr.at[0], sem_x).wait()
        outs = []
        for layer in range(2):
            slot = first ^ layer
            lin_scr[layer] = jnp.broadcast_to(vec[layer, 0:1, :], (rows, D))

            @pl.loop(0, NQ)
            def _(q):
                wait_pair(w_scr, sems, slot, q)
                cols = pl.ds(pl.multiple_of(q * 512, 512), 512)
                lin_scr[layer] += jnp.dot(
                    x_scr[layer, :, cols], w_scr[slot, pl.ds(2 * q, 2)].reshape(512, D), preferred_element_type=F32
                )

            lin = lin_scr[layer]
            center, scale = norm_parts(x_scr[layer].astype(F32) + gelu_parts(lin)[0])
            y = (center * scale * vec[layer, 1:2, :] + vec[layer, 2:3, :]).astype(BF16)
            if layer == 0:
                x_scr[1] = y
            else:
                act_scr[...] = y
                outs.append(pltpu.make_async_copy(act_scr, act, sem_v))
                outs[-1].start()
            for src, dst, n in ((x_scr, xs, 0), (lin_scr, ls, 1)):
                copy = pltpu.make_async_copy(src.at[layer], dst.at[layer, pl.ds(at, rows), :], sem_o.at[layer, n])
                copy.start()
                outs.append(copy)
        for copy in outs:
            copy.wait()


def backward_kernel(n_msgs, rows, micros, ctl, *refs):
    near, far = refs[:n_msgs], refs[n_msgs:2 * n_msgs]
    cot, recv, vec_in, xs, ls = refs[2 * n_msgs:2 * n_msgs + 5]
    n_micro = len(micros)
    back, *slopes, zero = refs[-14 - 2 * n_micro:-12]
    zero[0] = 0
    w_scr, g_scr, x_scr, lin_scr, dz_scr, dl_scr, vec, back_scr, sems, sem_x, sem_v, sem_o = refs[-12:]
    active, stage, batch, x_me, core, first, xl = (ctl[i] for i in range(7))

    @pl.when(active == 1)
    def _():
        groups = weight_copies(near, far, w_scr, sems, x_me, core)
        per_half = cot.shape[0] // 2
        at = pl.multiple_of(batch * rows, rows)

        @pl.when(stage == 3)
        def _():
            src = cot.at[pl.ds(pl.multiple_of(xl * per_half + batch * rows, rows), rows), :]
            pltpu.make_async_copy(src, g_scr, sem_x.at[2, 0]).start()

        @pl.when(stage != 3)
        def _():
            pltpu.make_async_copy(recv.at[pl.ds(0, rows), :], g_scr, sem_x.at[2, 0]).start()

        loads = {}
        for layer in (1, 0):
            loads[layer] = (
                pltpu.make_async_copy(xs.at[layer, pl.ds(at, rows), :], x_scr.at[layer], sem_x.at[layer, 0]),
                pltpu.make_async_copy(ls.at[layer, pl.ds(at, rows), :], lin_scr.at[layer], sem_x.at[layer, 1]),
            )
            for copy in loads[layer]:
                copy.start()
        vec_copy = pltpu.make_async_copy(vec_in, vec, sem_v)
        vec_copy.start()
        issue(groups, 1 - first)
        vec_copy.wait()
        pltpu.make_async_copy(recv.at[pl.ds(0, rows), :], g_scr, sem_x.at[2, 0]).wait()
        outs = []
        for layer in (1, 0):
            slot = first ^ layer
            for copy in loads[layer]:
                copy.wait()
            lin = lin_scr[layer]
            gated, t, square = gelu_parts(lin)
            center, scale = norm_parts(x_scr[layer].astype(F32) + gated)
            unit = center * scale
            g = g_scr[...].astype(F32) * vec[layer, 1:2, :]
            dz = scale * (g - jnp.mean(g, axis=-1, keepdims=True) - unit * jnp.mean(g * unit, axis=-1, keepdims=True))
            dz_scr[...] = dz
            dl_scr[layer] = (dz * gelu_slope(lin, t, square)).astype(BF16)
            for is_own, dsts in ((1, slopes[:n_micro]), (0, slopes[n_micro:])):
                for m, dst in zip(micros, dsts):

                    @pl.when((batch == m) & ((xl == layer) == (is_own == 1)))
                    def _():
                        pltpu.make_async_copy(dl_scr.at[layer], dst, sem_o.at[layer]).start()

            outs.append(pltpu.make_async_copy(dl_scr.at[layer], slopes[0], sem_o.at[layer]))

            @pl.loop(0, NQ)
            def _(q):
                wait_pair(w_scr, sems, slot, q)
                cols = pl.ds(pl.multiple_of(q * 512, 512), 512)

                def step():
                    down = lax.dot_general(
                        dl_scr[layer], w_scr[slot, pl.ds(2 * q, 2)].reshape(512, D), (((1,), (1,)), ((), ())), preferred_element_type=F32
                    )
                    y = (dz_scr[:, cols] + down).astype(BF16)
                    if layer == 1:
                        g_scr[:, cols] = y
                    else:
                        back_scr[:, cols] = y

                if layer == 1:
                    step()
                else:
                    pl.when(stage != 0)(step)
        outs.append(pltpu.make_async_copy(back_scr, back, sem_v))
        outs[-1].start()
        for copy in outs:
            copy.wait()


def forward_call(ctl, near, far, window, recv, vec, stash, early):
    tokens = window.shape[0] // 2
    rows = tokens // MICRO
    n = len(near)
    any_spec = pl.BlockSpec(memory_space=pl.ANY)
    return pl.pallas_call(
        functools.partial(forward_kernel, n, rows),
        out_shape=(
            jax.ShapeDtypeStruct((rows, D), BF16),
            jax.ShapeDtypeStruct((2, tokens, D), BF16),
            jax.ShapeDtypeStruct((2, tokens, D), F32),
        ),
        in_specs=[pl.BlockSpec(memory_space=pltpu.SMEM)] + [any_spec] * (2 * n + 3 + len(stash) + len(early)),
        out_specs=(any_spec, any_spec, any_spec),
        scratch_shapes=[
            pltpu.VMEM((2, 8, 2, 2, 64, D), BF16),
            pltpu.VMEM((2, rows, D), BF16),
            pltpu.VMEM((2, rows, D), F32),
            pltpu.VMEM(vec.shape, F32),
            pltpu.VMEM((rows, D), BF16),
            pltpu.SemaphoreType.DMA((2, NQ)),
            pltpu.SemaphoreType.DMA,
            pltpu.SemaphoreType.DMA,
            pltpu.SemaphoreType.DMA((2, 2)),
        ],
        input_output_aliases={2 * n + 4 + i: 1 + i for i in range(len(stash))},
        compiler_params=pltpu.CompilerParams(vmem_limit_bytes=VMEM_LIMIT),
        cost_estimate=pl.CostEstimate(flops=4 * rows * D * D, bytes_accessed=4 * D * D, transcendentals=2 * rows * D),
        name="forward_tick",
    )(ctl, *near, *far, window, recv, vec, *stash, *early)


def backward_call(ctl, near, far, cot, recv, vec, xs, ls, micros, stash, early):
    rows = cot.shape[0] // 2 // MICRO
    n = len(near)
    any_spec = pl.BlockSpec(memory_space=pl.ANY)
    return pl.pallas_call(
        functools.partial(backward_kernel, n, rows, micros),
        out_shape=(jax.ShapeDtypeStruct((rows, D), BF16),) * (1 + 2 * len(micros)) + (jax.ShapeDtypeStruct((1,), jnp.int32),),
        in_specs=[pl.BlockSpec(memory_space=pltpu.SMEM)] + [any_spec] * (2 * n + 5 + len(stash) + len(early)),
        out_specs=(any_spec,) * (1 + 2 * len(micros)) + (pl.BlockSpec(memory_space=pltpu.SMEM),),
        scratch_shapes=[
            pltpu.VMEM((2, 8, 2, 2, 64, D), BF16),
            pltpu.VMEM((rows, D), BF16),
            pltpu.VMEM((2, rows, D), BF16),
            pltpu.VMEM((2, rows, D), F32),
            pltpu.VMEM((rows, D), F32),
            pltpu.VMEM((2, rows, D), BF16),
            pltpu.VMEM(vec.shape, F32),
            pltpu.VMEM((rows, D), BF16),
            pltpu.SemaphoreType.DMA((2, NQ)),
            pltpu.SemaphoreType.DMA((3, 2)),
            pltpu.SemaphoreType.DMA,
            pltpu.SemaphoreType.DMA((2,)),
        ],
        input_output_aliases={2 * n + 6 + i: 1 + i for i in range(len(stash))},
        compiler_params=pltpu.CompilerParams(vmem_limit_bytes=VMEM_LIMIT),
        cost_estimate=pl.CostEstimate(flops=4 * rows * D * D, bytes_accessed=4 * D * D, transcendentals=2 * rows * D),
        name="backward_tick",
    )(ctl, *near, *far, cot, recv, vec, xs, ls, *stash, *early)

AXES = ("y", "xl", "z", "xh", "c")
MICRO = 2
STAGES = 4

FIRST_DECAY = 0.9
SECOND_DECAY = 0.999
STEP_SIZE = 0.01
EPSILON = 1e-08
FIRST_CORRECTION = 1.0 - 0.9**10
SECOND_CORRECTION = 1.0 - 0.999**10


def shift_x(v, by):
    place = lambda x: (x & 1) * 2 + (x >> 1)
    return lax.ppermute(v, ("xl", "xh"), [(place(x), place((x + by) % 4)) for x in range(4)])


def shift_z(v, by):
    return lax.ppermute(v, "z", [(z, (z + by) % 8) for z in range(8)])


def swap_core(v):
    return lax.ppermute(v, "c", [(0, 1), (1, 0)])


def shift_x_in(v, by, planes):
    place = lambda y, x, c: (y * 4 + (x & 1) * 2 + (x >> 1)) * 2 + c
    pairs = []
    for y in range(STAGES):
        for x in range(4):
            for c in range(2):
                to = (y, (x + by) % 4, c) if y in planes else (y, x, 1 - c)
                pairs.append((place(y, x, c), place(*to)))
    return lax.ppermute(v, ("y", "xl", "xh", "c"), pairs)


def swap_pair(v):
    return lax.ppermute(v, "xl", [(0, 1), (1, 0)])


def swap_cross(v):
    to = {3: 4, 4: 3}
    pairs = [(s * 2 + c, to[s] * 2 + c if s in to else s * 2 + 1 - c) for s in range(8) for c in range(2)]
    return lax.ppermute(v, ("y", "xl", "c"), pairs)


def ring_gather(v, shift, steps):
    right = left = v
    out = []
    for _ in range(1, steps):
        right, left = shift(right, 1), shift(left, -1)
        out += [right, left]
    half = v.shape[0] // 2
    return out + [shift(right[:half], 1), shift(left[half:], -1)]


def after_kernel(*refs):
    del refs


def after(v, *others):
    return pl.pallas_call(
        after_kernel,
        out_shape=jax.ShapeDtypeStruct(v.shape, v.dtype),
        in_specs=[pl.BlockSpec(memory_space=pl.ANY)] * (1 + len(others)),
        out_specs=pl.BlockSpec(memory_space=pl.ANY),
        input_output_aliases={0: 0},
        compiler_params=pltpu.CompilerParams(vmem_limit_bytes=VMEM_LIMIT),
        name="after",
    )(v, *others)


def place_kernel(at, *refs):
    blocks, out, sem = refs[:9], refs[9], refs[10]
    for i, block in enumerate(blocks[:7]):
        pltpu.make_async_copy(block, out.at[at[i]], sem).start()
    for i, block in enumerate(blocks[7:]):
        pltpu.make_async_copy(block, out.at[at[7], pl.ds(16 * i, 16), :], sem).start()
    pltpu.make_async_copy(out, out, sem).wait()


def place(blocks, at):
    return pl.pallas_call(
        place_kernel,
        out_shape=jax.ShapeDtypeStruct((8, 32, D), BF16),
        in_specs=[pl.BlockSpec(memory_space=pltpu.SMEM)] + [pl.BlockSpec(memory_space=pl.ANY)] * 9,
        out_specs=pl.BlockSpec(memory_space=pltpu.VMEM),
        scratch_shapes=[pltpu.SemaphoreType.DMA],
        compiler_params=pltpu.CompilerParams(vmem_limit_bytes=VMEM_LIMIT),
        cost_estimate=pl.CostEstimate(flops=0, bytes_accessed=2 << 20, transcendentals=0),
        name="place_blocks",
    )(at, *blocks)


def gather_plane(here, x_me, xh, z_me, from_pair, order):
    a, b = here[:32], here[48:]
    lower, upper, across = shift_x(here[:48], 1), shift_x(a, -1), shift_x(a, 2)
    vec = order(here[32:35], lower[32:35])
    lower = lower[:32]
    own_first, lower_first = xh == 0, lax.rem(x_me + 3, 4) < 2
    heads = jnp.stack(
        [
            jnp.stack([jnp.where(own_first, a, across), jnp.where(own_first, across, a)]),
            jnp.stack([jnp.where(lower_first, lower, upper), jnp.where(lower_first, upper, lower)]),
        ]
    )
    heads = lax.all_gather(heads, "z", axis=0)
    z_from = lax.rem(z_me + 8 + jnp.array((0, -1, 1, -2, 2, -3, 3, 4), jnp.int32), 8)
    tails = after(place([b] + ring_gather(b, shift_z, 4), z_from), from_pair, vec)
    right, left = shift_x(tails, 1), shift_x(tails, -1)
    ends = [shift_x(right[:4], 1), shift_x(left[4:], -1)]
    return [after(heads, right, left), tails, right, left] + ends, vec


def add_rounded(a, b):
    return (a.astype(F32) + b.astype(F32)).astype(BF16)


def ring_reduce(chunks, far_low, far_high, shift, steps):
    half = chunks.shape[1] // 2
    right, left = shift(far_low, 1), shift(far_high, -1)
    for k in range(steps - 1, 0, -1):
        up, down = chunks[k], chunks[2 * steps - k]
        if k == steps - 1:
            right = jnp.concatenate([add_rounded(up[:half], right), up[half:]], axis=0)
            left = jnp.concatenate([down[:half], add_rounded(down[half:], left)], axis=0)
        else:
            right, left = add_rounded(up, right), add_rounded(down, left)
        right, left = shift(right, 1), shift(left, -1)
    return chunks[0].astype(F32) + right.astype(F32) + left.astype(F32)


def grad_kernel(n_inputs, z_ref, *refs):
    n_parts = len(refs) - 2 * n_inputs - 6
    inputs, parts = refs[:2 * n_inputs], refs[2 * n_inputs:2 * n_inputs + n_parts]
    g, far_low, far_high, x_scr, d_scr, sem = refs[2 * n_inputs + n_parts:]
    size, width = parts[0].shape[0], inputs[0].shape[-1]
    for which in range(2):

        @pl.when(z_ref[1] == which)
        def _():
            for i, part in enumerate(inputs[which * n_inputs:(which + 1) * n_inputs]):
                pltpu.make_async_copy(part, x_scr.at[:, :, pl.ds(i * width, width)], sem.at[0]).start()

    for i, part in enumerate(parts):
        pltpu.make_async_copy(part, d_scr.at[pl.ds(i * size, size), :], sem.at[1]).start()
    pltpu.make_async_copy(x_scr, x_scr, sem.at[0]).wait()
    pltpu.make_async_copy(d_scr, d_scr, sem.at[1]).wait()
    z_me = z_ref[0]

    @pl.loop(0, D // 256)
    def _(n):
        cols = pl.ds(pl.multiple_of(n * 256, 256), 256)
        part = jnp.dot(x_scr[...].reshape(512, -1), d_scr[:, cols], preferred_element_type=F32).astype(BF16)
        part = part.reshape(8, 64, 256)
        for z in range(8):
            g[lax.rem(z - z_me + 8, 8), :, cols] = part[z]
        far_low[:, cols] = g[4, :32, cols]
        far_high[:, cols] = g[4, 32:, cols]


def grad_call(z_me, which, inputs, parts):
    n = len(inputs[0])
    tokens = inputs[0][0].shape[-1] * n
    vm = pl.BlockSpec(memory_space=pltpu.VMEM)
    half = jax.ShapeDtypeStruct((32, D), BF16)
    return pl.pallas_call(
        functools.partial(grad_kernel, n),
        out_shape=(jax.ShapeDtypeStruct((8, 64, D), BF16), half, half),
        in_specs=[pl.BlockSpec(memory_space=pltpu.SMEM)]
        + [pl.BlockSpec(memory_space=pl.ANY)] * (2 * n + len(parts)),
        out_specs=(vm, vm, vm),
        scratch_shapes=[
            pltpu.VMEM((8, 64, tokens), BF16),
            pltpu.VMEM((tokens, D), BF16),
            pltpu.SemaphoreType.DMA((2,)),
        ],
        compiler_params=pltpu.CompilerParams(vmem_limit_bytes=VMEM_LIMIT),
        cost_estimate=pl.CostEstimate(flops=2 * tokens * D * 512, bytes_accessed=7 << 20, transcendentals=0),
        name="weight_grads",
    )(jnp.stack([z_me, which]), *inputs[0], *inputs[1], *parts)


def trade_inputs(xs, x_me, core, planes):
    tokens = xs.shape[1]
    xt = jnp.swapaxes(xs, 1, 2).reshape(2, 8, 2, 2, 64, tokens)
    mine = lax.dynamic_index_in_dim(xt, core, 3, keepdims=False)
    theirs = lax.dynamic_index_in_dim(xt, 1 - core, 3, keepdims=False)
    both = jnp.concatenate([mine, swap_core(theirs)], axis=-1)

    def meant_for(step):
        x = lax.rem(x_me + step, 4)
        block = lax.dynamic_index_in_dim(both, x % 2, 0, keepdims=False)
        return lax.dynamic_index_in_dim(block, x // 2, 1, keepdims=False)

    return [meant_for(0)] + [shift_x_in(meant_for(by % 4), by, planes) for by in (1, -1, 2)]


def trade_slopes(own, other):
    parts = []
    for part in (own, shift_x(other, 1), shift_x(other, -1), shift_x(own, 2)):
        parts += [part, swap_core(part)]
    return parts


def shards(master_old, first_old, second_old, layer_vectors, new_section, frozen, window_input, cotangent):
    y, xl, z_me, xh, core = (lax.axis_index(name) for name in AXES)
    section = y * 2 + xl
    x_me = xl + 2 * xh
    goal = jnp.maximum(new_section[0], new_section[1])
    in_plane = goal // 2 == y
    label = jnp.where(in_plane, goal & 1, xl)

    held_of = lambda v: jnp.where(new_section[1] >= 0, v[1], v[0])
    own_rows = held_of(master_old).astype(BF16)
    own_vec = jnp.pad(held_of(layer_vectors), ((0, 13), (0, 0)))
    own = jnp.concatenate([own_rows[:32], own_vec, own_rows[32:]], axis=0)
    here = jnp.where(in_plane, own, swap_cross(own))
    states = (master_old, first_old, second_old)
    held = jnp.stack([held_of(s) for s in states])
    from_pair, from_cross = swap_pair(held), swap_cross(held)
    order = lambda own, other: jnp.where(label == 0, jnp.stack([own, other]), jnp.stack([other, own])).astype(F32)
    near, vec = gather_plane(here, x_me, xh, z_me, from_pair, order)
    far = [swap_core(m) for m in near]

    tokens = window_input.shape[0] // 2
    rows = tokens // MICRO
    stash = slope_stash = ()
    slopes, inputs = [], []
    ahead = behind = here

    def control(batch):
        active = (batch >= 0) & (batch < MICRO)
        slot = jnp.clip(batch, 0, MICRO - 1)
        parts = [active, y, slot, x_me, core, label, xl]
        return jnp.stack([jnp.asarray(p, jnp.int32) for p in parts])

    for tick in range(MICRO + 2 * STAGES - 2):
        f_stages = [s for s in range(STAGES) if 0 <= tick - s < MICRO]
        b_stages = [s for s in range(STAGES) if 0 <= tick - 2 * (STAGES - 1) + s < MICRO]
        if f_stages:
            early = tuple(inputs[0][1:]) if tick == 3 else ()
            act, xs, ls = forward_call(control(tick - y), near, far, window_input, ahead, vec, stash, early)
            stash = (xs, ls)
            if tick == 2:
                inputs.append(trade_inputs(xs, x_me, core, (0, 1)))
            pairs = [(s, s + 1) for s in f_stages if s + 1 < STAGES]
            if pairs:
                ahead = lax.ppermute(act, "y", pairs)
        if b_stages:
            early = ()
            if tick == 6:
                early = (from_cross,)
            if tick == 7:
                early = tuple(inputs[1][1:])
            micros = tuple(range(MICRO))
            if tick == 7:
                micros, slope_stash = (1,), slope_stash[1::2]
            back, *slope_stash, zero = backward_call(
                control(tick - 2 * (STAGES - 1) + y),
                near,
                far,
                cotangent,
                behind,
                vec,
                *stash,
                micros,
                tuple(slope_stash),
                early,
            )
            pairs = [(s, s - 1) for s in b_stages if s > 0]
            if pairs:
                behind = lax.ppermute(back, "y", pairs)
            if tick == 5:
                inputs.append(trade_inputs(jnp.where(zero[0] == 0, stash[0], 0), x_me, core, (2, 3)))
            if tick >= 6:
                slopes.append(trade_slopes(slope_stash[0], slope_stash[len(micros)]))

    kept = jnp.where(goal == section, held, jnp.where(in_plane, from_pair, from_cross))
    master, first_state, second_state = kept[0], kept[1], kept[2]

    parts = [slopes[m][i] for i in range(8) for m in range(MICRO)]
    grad_rows = ring_reduce(*grad_call(z_me, y // 2, inputs, parts), shift_z, 4)
    learning = lax.dynamic_index_in_dim(frozen, section, 0, keepdims=False) == 0
    first_next = FIRST_DECAY * first_state + (1.0 - FIRST_DECAY) * grad_rows
    second_next = SECOND_DECAY * second_state + (1.0 - SECOND_DECAY) * grad_rows * grad_rows
    stepped = master - STEP_SIZE * (first_next / FIRST_CORRECTION) / (
        jnp.sqrt(second_next / SECOND_CORRECTION) + EPSILON
    )
    master_new = jnp.where(learning, stepped, master)
    first_new = jnp.where(learning, first_next, first_state)
    second_new = jnp.where(learning, second_next, second_state)
    return (master_new[None], first_new[None], second_new[None])


def solution(mesh):
    fine = jax.sharding.Mesh(mesh.devices.reshape(4, 2, 8, 2, 2), AXES)
    sec, rep = ("y", "xl"), ("z", "xh", "c")
    rows = P(sec, rep, None)
    in_specs = (rows, rows, rows, P(sec, None, None), P(sec), P(), P(rep, None), P(rep, None))
    return jax.shard_map(shards, mesh=fine, in_specs=in_specs, out_specs=(rows, rows, rows), check_vma=False)
```

```python
import functools
import jax
import jax.numpy as jnp
from jax import lax
from jax.experimental import pallas as pl
from jax.experimental.pallas import tpu as pltpu
from jax.sharding import PartitionSpec as P

BF16 = jnp.bfloat16
F32 = jnp.float32
D = 2048
NQ = 4
VMEM_LIMIT = 64 * 1024 * 1024 - 65536
GELU_K = 0.7978845608028654


def weight_copies(near, far, w_scr, sems, x_me, core):
    copies = ([], [])
    for slot in range(2):
        for q in range(NQ):
            for msgs, owner in ((near, core), (far, 1 - core)):
                src = msgs[0].at[pl.ds(2 * q, 2), slot]
                dst = w_scr.at[slot, pl.ds(2 * q, 2), :, owner, pl.ds(0, 32), :]
                copies[slot].append(pltpu.make_async_copy(src, dst, sems.at[slot, q]))
                for dx in (0, 2) if slot == 0 else (-1, 1):
                    if dx == 2:
                        src = msgs[4 + q // 2].at[pl.ds(2 * (q % 2), 2)]
                    else:
                        src = msgs[(1, 3, 2)[dx]].at[pl.ds(2 * q, 2)]
                    xh = lax.rem(x_me + dx + 4, 4) // 2
                    dst = w_scr.at[slot, pl.ds(2 * q, 2), xh, owner, pl.ds(32, 32), :]
                    copies[slot].append(pltpu.make_async_copy(src, dst, sems.at[slot, q]))
    return copies


def gelu_parts(u):
    square = u * u
    t = jnp.tanh(GELU_K * u * (1.0 + 0.044715 * square))
    return 0.5 * u * (1.0 + t), t, square


def gelu_slope(u, t, square):
    return 0.5 * (1.0 + t) + 0.5 * u * (1.0 - t * t) * (GELU_K * (1.0 + 3 * 0.044715 * square))


def norm_parts(z):
    center = z - jnp.mean(z, axis=-1, keepdims=True)
    spread = jnp.mean(center * center, axis=-1, keepdims=True)
    return center, lax.rsqrt(spread + 1e-5)


def issue(groups, first):
    def start(slot):
        for copy in groups[slot]:
            copy.start()

    @pl.when(first == 0)
    def _():
        start(0)
        start(1)

    @pl.when(first == 1)
    def _():
        start(1)
        start(0)


def wait_pair(w_scr, sems, slot, q):
    blocks = w_scr.at[slot, pl.ds(2 * q, 2)]
    pltpu.make_async_copy(blocks, blocks, sems.at[slot, q]).wait()


def forward_kernel(n_msgs, rows, ctl, *refs):
    near, far = refs[:n_msgs], refs[n_msgs:2 * n_msgs]
    window, recv, vec_in = refs[2 * n_msgs:2 * n_msgs + 3]
    act, xs, ls, w_scr, x_scr, lin_scr, vec, act_scr, sems, sem_x, sem_v, sem_o = refs[-12:]
    active, stage, batch, x_me, core, first, xl = (ctl[i] for i in range(7))

    @pl.when(active == 1)
    def _():
        groups = weight_copies(near, far, w_scr, sems, x_me, core)
        per_half = window.shape[0] // 2
        at = pl.multiple_of(batch * rows, rows)

        @pl.when(stage == 0)
        def _():
            src = window.at[pl.ds(pl.multiple_of(xl * per_half + batch * rows, rows), rows), :]
            pltpu.make_async_copy(src, x_scr.at[0], sem_x).start()

        @pl.when(stage != 0)
        def _():
            pltpu.make_async_copy(recv.at[pl.ds(0, rows), :], x_scr.at[0], sem_x).start()

        vec_copy = pltpu.make_async_copy(vec_in, vec, sem_v)
        vec_copy.start()
        issue(groups, first)
        vec_copy.wait()
        pltpu.make_async_copy(recv.at[pl.ds(0, rows), :], x_scr.at[0], sem_x).wait()
        outs = []
        for layer in range(2):
            slot = first ^ layer
            lin_scr[layer] = jnp.broadcast_to(vec[layer, 0:1, :], (rows, D))

            @pl.loop(0, NQ)
            def _(q):
                wait_pair(w_scr, sems, slot, q)
                cols = pl.ds(pl.multiple_of(q * 512, 512), 512)
                lin_scr[layer] += jnp.dot(
                    x_scr[layer, :, cols], w_scr[slot, pl.ds(2 * q, 2)].reshape(512, D), preferred_element_type=F32
                )

            lin = lin_scr[layer]
            center, scale = norm_parts(x_scr[layer].astype(F32) + gelu_parts(lin)[0])
            y = (center * scale * vec[layer, 1:2, :] + vec[layer, 2:3, :]).astype(BF16)
            if layer == 0:
                x_scr[1] = y
            else:
                act_scr[...] = y
                outs.append(pltpu.make_async_copy(act_scr, act, sem_v))
                outs[-1].start()
            for src, dst, n in ((x_scr, xs, 0), (lin_scr, ls, 1)):
                copy = pltpu.make_async_copy(src.at[layer], dst.at[layer, pl.ds(at, rows), :], sem_o.at[layer, n])
                copy.start()
                outs.append(copy)
        for copy in outs:
            copy.wait()


def backward_kernel(n_msgs, rows, micros, ctl, *refs):
    near, far = refs[:n_msgs], refs[n_msgs:2 * n_msgs]
    cot, recv, vec_in, xs, ls = refs[2 * n_msgs:2 * n_msgs + 5]
    n_micro = len(micros)
    back, *slopes, zero = refs[-14 - 2 * n_micro:-12]
    zero[0] = 0
    w_scr, g_scr, x_scr, lin_scr, dz_scr, dl_scr, vec, back_scr, sems, sem_x, sem_v, sem_o = refs[-12:]
    active, stage, batch, x_me, core, first, xl = (ctl[i] for i in range(7))

    @pl.when(active == 1)
    def _():
        groups = weight_copies(near, far, w_scr, sems, x_me, core)
        per_half = cot.shape[0] // 2
        at = pl.multiple_of(batch * rows, rows)

        @pl.when(stage == 3)
        def _():
            src = cot.at[pl.ds(pl.multiple_of(xl * per_half + batch * rows, rows), rows), :]
            pltpu.make_async_copy(src, g_scr, sem_x.at[2, 0]).start()

        @pl.when(stage != 3)
        def _():
            pltpu.make_async_copy(recv.at[pl.ds(0, rows), :], g_scr, sem_x.at[2, 0]).start()

        loads = {}
        for layer in (1, 0):
            loads[layer] = (
                pltpu.make_async_copy(xs.at[layer, pl.ds(at, rows), :], x_scr.at[layer], sem_x.at[layer, 0]),
                pltpu.make_async_copy(ls.at[layer, pl.ds(at, rows), :], lin_scr.at[layer], sem_x.at[layer, 1]),
            )
            for copy in loads[layer]:
                copy.start()
        vec_copy = pltpu.make_async_copy(vec_in, vec, sem_v)
        vec_copy.start()
        issue(groups, 1 - first)
        vec_copy.wait()
        pltpu.make_async_copy(recv.at[pl.ds(0, rows), :], g_scr, sem_x.at[2, 0]).wait()
        outs = []
        for layer in (1, 0):
            slot = first ^ layer
            for copy in loads[layer]:
                copy.wait()
            lin = lin_scr[layer]
            gated, t, square = gelu_parts(lin)
            center, scale = norm_parts(x_scr[layer].astype(F32) + gated)
            unit = center * scale
            g = g_scr[...].astype(F32) * vec[layer, 1:2, :]
            dz = scale * (g - jnp.mean(g, axis=-1, keepdims=True) - unit * jnp.mean(g * unit, axis=-1, keepdims=True))
            dz_scr[...] = dz
            dl_scr[layer] = (dz * gelu_slope(lin, t, square)).astype(BF16)
            for is_own, dsts in ((1, slopes[:n_micro]), (0, slopes[n_micro:])):
                for m, dst in zip(micros, dsts):

                    @pl.when((batch == m) & ((xl == layer) == (is_own == 1)))
                    def _():
                        pltpu.make_async_copy(dl_scr.at[layer], dst, sem_o.at[layer]).start()

            outs.append(pltpu.make_async_copy(dl_scr.at[layer], slopes[0], sem_o.at[layer]))

            @pl.loop(0, NQ)
            def _(q):
                wait_pair(w_scr, sems, slot, q)
                cols = pl.ds(pl.multiple_of(q * 512, 512), 512)

                def step():
                    down = lax.dot_general(
                        dl_scr[layer], w_scr[slot, pl.ds(2 * q, 2)].reshape(512, D), (((1,), (1,)), ((), ())), preferred_element_type=F32
                    )
                    y = (dz_scr[:, cols] + down).astype(BF16)
                    if layer == 1:
                        g_scr[:, cols] = y
                    else:
                        back_scr[:, cols] = y

                if layer == 1:
                    step()
                else:
                    pl.when(stage != 0)(step)
        outs.append(pltpu.make_async_copy(back_scr, back, sem_v))
        outs[-1].start()
        for copy in outs:
            copy.wait()


def forward_call(ctl, near, far, window, recv, vec, stash, early):
    tokens = window.shape[0] // 2
    rows = tokens // MICRO
    n = len(near)
    any_spec = pl.BlockSpec(memory_space=pl.ANY)
    return pl.pallas_call(
        functools.partial(forward_kernel, n, rows),
        out_shape=(
            jax.ShapeDtypeStruct((rows, D), BF16),
            jax.ShapeDtypeStruct((2, tokens, D), BF16),
            jax.ShapeDtypeStruct((2, tokens, D), F32),
        ),
        in_specs=[pl.BlockSpec(memory_space=pltpu.SMEM)] + [any_spec] * (2 * n + 3 + len(stash) + len(early)),
        out_specs=(any_spec, any_spec, any_spec),
        scratch_shapes=[
            pltpu.VMEM((2, 8, 2, 2, 64, D), BF16),
            pltpu.VMEM((2, rows, D), BF16),
            pltpu.VMEM((2, rows, D), F32),
            pltpu.VMEM(vec.shape, F32),
            pltpu.VMEM((rows, D), BF16),
            pltpu.SemaphoreType.DMA((2, NQ)),
            pltpu.SemaphoreType.DMA,
            pltpu.SemaphoreType.DMA,
            pltpu.SemaphoreType.DMA((2, 2)),
        ],
        input_output_aliases={2 * n + 4 + i: 1 + i for i in range(len(stash))},
        compiler_params=pltpu.CompilerParams(vmem_limit_bytes=VMEM_LIMIT),
        cost_estimate=pl.CostEstimate(flops=4 * rows * D * D, bytes_accessed=4 * D * D, transcendentals=2 * rows * D),
        name="forward_tick",
    )(ctl, *near, *far, window, recv, vec, *stash, *early)


def backward_call(ctl, near, far, cot, recv, vec, xs, ls, micros, stash, early):
    rows = cot.shape[0] // 2 // MICRO
    n = len(near)
    any_spec = pl.BlockSpec(memory_space=pl.ANY)
    return pl.pallas_call(
        functools.partial(backward_kernel, n, rows, micros),
        out_shape=(jax.ShapeDtypeStruct((rows, D), BF16),) * (1 + 2 * len(micros)) + (jax.ShapeDtypeStruct((1,), jnp.int32),),
        in_specs=[pl.BlockSpec(memory_space=pltpu.SMEM)] + [any_spec] * (2 * n + 5 + len(stash) + len(early)),
        out_specs=(any_spec,) * (1 + 2 * len(micros)) + (pl.BlockSpec(memory_space=pltpu.SMEM),),
        scratch_shapes=[
            pltpu.VMEM((2, 8, 2, 2, 64, D), BF16),
            pltpu.VMEM((rows, D), BF16),
            pltpu.VMEM((2, rows, D), BF16),
            pltpu.VMEM((2, rows, D), F32),
            pltpu.VMEM((rows, D), F32),
            pltpu.VMEM((2, rows, D), BF16),
            pltpu.VMEM(vec.shape, F32),
            pltpu.VMEM((rows, D), BF16),
            pltpu.SemaphoreType.DMA((2, NQ)),
            pltpu.SemaphoreType.DMA((3, 2)),
            pltpu.SemaphoreType.DMA,
            pltpu.SemaphoreType.DMA((2,)),
        ],
        input_output_aliases={2 * n + 6 + i: 1 + i for i in range(len(stash))},
        compiler_params=pltpu.CompilerParams(vmem_limit_bytes=VMEM_LIMIT),
        cost_estimate=pl.CostEstimate(flops=4 * rows * D * D, bytes_accessed=4 * D * D, transcendentals=2 * rows * D),
        name="backward_tick",
    )(ctl, *near, *far, cot, recv, vec, xs, ls, *stash, *early)

AXES = ("y", "xl", "z", "xh", "c")
MICRO = 2
STAGES = 4

FIRST_DECAY = 0.9
SECOND_DECAY = 0.999
STEP_SIZE = 0.01
EPSILON = 1e-08
FIRST_CORRECTION = 1.0 - 0.9**10
SECOND_CORRECTION = 1.0 - 0.999**10


def shift_x(v, by):
    place = lambda x: (x & 1) * 2 + (x >> 1)
    return lax.ppermute(v, ("xl", "xh"), [(place(x), place((x + by) % 4)) for x in range(4)])


def shift_z(v, by):
    return lax.ppermute(v, "z", [(z, (z + by) % 8) for z in range(8)])


def swap_core(v):
    return lax.ppermute(v, "c", [(0, 1), (1, 0)])


def shift_x_in(v, by, planes):
    place = lambda y, x, c: (y * 4 + (x & 1) * 2 + (x >> 1)) * 2 + c
    pairs = []
    for y in range(STAGES):
        for x in range(4):
            for c in range(2):
                to = (y, (x + by) % 4, c) if y in planes else (y, x, 1 - c)
                pairs.append((place(y, x, c), place(*to)))
    return lax.ppermute(v, ("y", "xl", "xh", "c"), pairs)


def swap_pair(v):
    return lax.ppermute(v, "xl", [(0, 1), (1, 0)])


def swap_cross(v):
    to = {3: 4, 4: 3}
    pairs = [(s * 2 + c, to[s] * 2 + c if s in to else s * 2 + 1 - c) for s in range(8) for c in range(2)]
    return lax.ppermute(v, ("y", "xl", "c"), pairs)


def ring_gather(v, shift, steps):
    right = left = v
    out = []
    for _ in range(1, steps):
        right, left = shift(right, 1), shift(left, -1)
        out += [right, left]
    half = v.shape[0] // 2
    return out + [shift(right[:half], 1), shift(left[half:], -1)]


def after_kernel(*refs):
    del refs


def after(v, *others):
    return pl.pallas_call(
        after_kernel,
        out_shape=jax.ShapeDtypeStruct(v.shape, v.dtype),
        in_specs=[pl.BlockSpec(memory_space=pl.ANY)] * (1 + len(others)),
        out_specs=pl.BlockSpec(memory_space=pl.ANY),
        input_output_aliases={0: 0},
        compiler_params=pltpu.CompilerParams(vmem_limit_bytes=VMEM_LIMIT),
        name="after",
    )(v, *others)


def place_kernel(at, *refs):
    blocks, out, sem = refs[:9], refs[9], refs[10]
    for i, block in enumerate(blocks[:7]):
        pltpu.make_async_copy(block, out.at[at[i]], sem).start()
    for i, block in enumerate(blocks[7:]):
        pltpu.make_async_copy(block, out.at[at[7], pl.ds(16 * i, 16), :], sem).start()
    pltpu.make_async_copy(out, out, sem).wait()


def place(blocks, at):
    return pl.pallas_call(
        place_kernel,
        out_shape=jax.ShapeDtypeStruct((8, 32, D), BF16),
        in_specs=[pl.BlockSpec(memory_space=pltpu.SMEM)] + [pl.BlockSpec(memory_space=pl.ANY)] * 9,
        out_specs=pl.BlockSpec(memory_space=pltpu.VMEM),
        scratch_shapes=[pltpu.SemaphoreType.DMA],
        compiler_params=pltpu.CompilerParams(vmem_limit_bytes=VMEM_LIMIT),
        cost_estimate=pl.CostEstimate(flops=0, bytes_accessed=2 << 20, transcendentals=0),
        name="place_blocks",
    )(at, *blocks)


def gather_plane(here, x_me, xh, z_me, from_pair, order):
    a, b = here[:32], here[48:]
    lower, upper, across = shift_x(here[:48], 1), shift_x(a, -1), shift_x(a, 2)
    vec = order(here[32:35], lower[32:35])
    lower = lower[:32]
    own_first, lower_first = xh == 0, lax.rem(x_me + 3, 4) < 2
    heads = jnp.stack(
        [
            jnp.stack([jnp.where(own_first, a, across), jnp.where(own_first, across, a)]),
            jnp.stack([jnp.where(lower_first, lower, upper), jnp.where(lower_first, upper, lower)]),
        ]
    )
    heads = lax.all_gather(heads, "z", axis=0)
    z_from = lax.rem(z_me + 8 + jnp.array((0, -1, 1, -2, 2, -3, 3, 4), jnp.int32), 8)
    tails = after(place([b] + ring_gather(b, shift_z, 4), z_from), from_pair, vec)
    right, left = shift_x(tails, 1), shift_x(tails, -1)
    ends = [shift_x(right[:4], 1), shift_x(left[4:], -1)]
    return [after(heads, right, left), tails, right, left] + ends, vec


def add_rounded(a, b):
    return (a.astype(F32) + b.astype(F32)).astype(BF16)


def ring_reduce(chunks, far_low, far_high, shift, steps):
    half = chunks.shape[1] // 2
    right, left = shift(far_low, 1), shift(far_high, -1)
    for k in range(steps - 1, 0, -1):
        up, down = chunks[k], chunks[2 * steps - k]
        if k == steps - 1:
            right = jnp.concatenate([add_rounded(up[:half], right), up[half:]], axis=0)
            left = jnp.concatenate([down[:half], add_rounded(down[half:], left)], axis=0)
        else:
            right, left = add_rounded(up, right), add_rounded(down, left)
        right, left = shift(right, 1), shift(left, -1)
    return chunks[0].astype(F32) + right.astype(F32) + left.astype(F32)


def grad_kernel(n_inputs, z_ref, *refs):
    n_parts = len(refs) - 2 * n_inputs - 6
    inputs, parts = refs[:2 * n_inputs], refs[2 * n_inputs:2 * n_inputs + n_parts]
    g, far_low, far_high, x_scr, d_scr, sem = refs[2 * n_inputs + n_parts:]
    size, width = parts[0].shape[0], inputs[0].shape[-1]
    for which in range(2):

        @pl.when(z_ref[1] == which)
        def _():
            for i, part in enumerate(inputs[which * n_inputs:(which + 1) * n_inputs]):
                pltpu.make_async_copy(part, x_scr.at[:, :, pl.ds(i * width, width)], sem.at[0]).start()

    for i, part in enumerate(parts):
        pltpu.make_async_copy(part, d_scr.at[pl.ds(i * size, size), :], sem.at[1]).start()
    pltpu.make_async_copy(x_scr, x_scr, sem.at[0]).wait()
    pltpu.make_async_copy(d_scr, d_scr, sem.at[1]).wait()
    z_me = z_ref[0]

    @pl.loop(0, D // 256)
    def _(n):
        cols = pl.ds(pl.multiple_of(n * 256, 256), 256)
        part = jnp.dot(x_scr[...].reshape(512, -1), d_scr[:, cols], preferred_element_type=F32).astype(BF16)
        part = part.reshape(8, 64, 256)
        for z in range(8):
            g[lax.rem(z - z_me + 8, 8), :, cols] = part[z]
        far_low[:, cols] = g[4, :32, cols]
        far_high[:, cols] = g[4, 32:, cols]


def grad_call(z_me, which, inputs, parts):
    n = len(inputs[0])
    tokens = inputs[0][0].shape[-1] * n
    vm = pl.BlockSpec(memory_space=pltpu.VMEM)
    half = jax.ShapeDtypeStruct((32, D), BF16)
    return pl.pallas_call(
        functools.partial(grad_kernel, n),
        out_shape=(jax.ShapeDtypeStruct((8, 64, D), BF16), half, half),
        in_specs=[pl.BlockSpec(memory_space=pltpu.SMEM)]
        + [pl.BlockSpec(memory_space=pl.ANY)] * (2 * n + len(parts)),
        out_specs=(vm, vm, vm),
        scratch_shapes=[
            pltpu.VMEM((8, 64, tokens), BF16),
            pltpu.VMEM((tokens, D), BF16),
            pltpu.SemaphoreType.DMA((2,)),
        ],
        compiler_params=pltpu.CompilerParams(vmem_limit_bytes=VMEM_LIMIT),
        cost_estimate=pl.CostEstimate(flops=2 * tokens * D * 512, bytes_accessed=7 << 20, transcendentals=0),
        name="weight_grads",
    )(jnp.stack([z_me, which]), *inputs[0], *inputs[1], *parts)


def trade_inputs(xs, x_me, core, planes):
    tokens = xs.shape[1]
    xt = jnp.swapaxes(xs, 1, 2).reshape(2, 8, 2, 2, 64, tokens)
    mine = lax.dynamic_index_in_dim(xt, core, 3, keepdims=False)
    theirs = lax.dynamic_index_in_dim(xt, 1 - core, 3, keepdims=False)
    both = jnp.concatenate([mine, swap_core(theirs)], axis=-1)

    def meant_for(step):
        x = lax.rem(x_me + step, 4)
        block = lax.dynamic_index_in_dim(both, x % 2, 0, keepdims=False)
        return lax.dynamic_index_in_dim(block, x // 2, 1, keepdims=False)

    return [meant_for(0)] + [shift_x_in(meant_for(by % 4), by, planes) for by in (1, -1, 2)]


def trade_slopes(own, other):
    parts = []
    for part in (own, shift_x(other, 1), shift_x(other, -1), shift_x(own, 2)):
        parts += [part, swap_core(part)]
    return parts


def shards(master_old, first_old, second_old, layer_vectors, new_section, frozen, window_input, cotangent):
    y, xl, z_me, xh, core = (lax.axis_index(name) for name in AXES)
    section = y * 2 + xl
    x_me = xl + 2 * xh
    goal = jnp.maximum(new_section[0], new_section[1])
    in_plane = goal // 2 == y
    label = jnp.where(in_plane, goal & 1, xl)

    held_of = lambda v: jnp.where(new_section[1] >= 0, v[1], v[0])
    own_rows = held_of(master_old).astype(BF16)
    own_vec = jnp.pad(held_of(layer_vectors), ((0, 13), (0, 0)))
    own = jnp.concatenate([own_rows[:32], own_vec, own_rows[32:]], axis=0)
    here = jnp.where(in_plane, own, swap_cross(own))
    states = (master_old, first_old, second_old)
    held = jnp.stack([held_of(s) for s in states])
    from_pair, from_cross = swap_pair(held), swap_cross(held)
    order = lambda own, other: jnp.where(label == 0, jnp.stack([own, other]), jnp.stack([other, own])).astype(F32)
    near, vec = gather_plane(here, x_me, xh, z_me, from_pair, order)
    far = [swap_core(m) for m in near]

    tokens = window_input.shape[0] // 2
    rows = tokens // MICRO
    stash = slope_stash = ()
    slopes, inputs = [], []
    ahead = behind = here

    def control(batch):
        active = (batch >= 0) & (batch < MICRO)
        slot = jnp.clip(batch, 0, MICRO - 1)
        parts = [active, y, slot, x_me, core, label, xl]
        return jnp.stack([jnp.asarray(p, jnp.int32) for p in parts])

    for tick in range(MICRO + 2 * STAGES - 2):
        f_stages = [s for s in range(STAGES) if 0 <= tick - s < MICRO]
        b_stages = [s for s in range(STAGES) if 0 <= tick - 2 * (STAGES - 1) + s < MICRO]
        if f_stages:
            early = tuple(inputs[0][1:]) if tick == 3 else ()
            act, xs, ls = forward_call(control(tick - y), near, far, window_input, ahead, vec, stash, early)
            stash = (xs, ls)
            if tick == 2:
                inputs.append(trade_inputs(xs, x_me, core, (0, 1)))
            pairs = [(s, s + 1) for s in f_stages if s + 1 < STAGES]
            if pairs:
                ahead = lax.ppermute(act, "y", pairs)
        if b_stages:
            early = ()
            if tick == 6:
                early = (from_cross,)
            if tick == 7:
                early = tuple(inputs[1][1:])
            micros = tuple(range(MICRO))
            back, *slope_stash, zero = backward_call(
                control(tick - 2 * (STAGES - 1) + y),
                near,
                far,
                cotangent,
                behind,
                vec,
                *stash,
                micros,
                tuple(slope_stash),
                early,
            )
            pairs = [(s, s - 1) for s in b_stages if s > 0]
            if pairs:
                behind = lax.ppermute(back, "y", pairs)
            if tick == 5:
                inputs.append(trade_inputs(jnp.where(zero[0] == 0, stash[0], 0), x_me, core, (2, 3)))
            if tick >= 6:
                slopes.append(trade_slopes(slope_stash[tick - 6], slope_stash[MICRO + tick - 6]))

    kept = jnp.where(goal == section, held, jnp.where(in_plane, from_pair, from_cross))
    master, first_state, second_state = kept[0], kept[1], kept[2]

    parts = [slopes[m][i] for i in range(8) for m in range(MICRO)]
    grad_rows = ring_reduce(*grad_call(z_me, y // 2, inputs, parts), shift_z, 4)
    learning = lax.dynamic_index_in_dim(frozen, section, 0, keepdims=False) == 0
    first_next = FIRST_DECAY * first_state + (1.0 - FIRST_DECAY) * grad_rows
    second_next = SECOND_DECAY * second_state + (1.0 - SECOND_DECAY) * grad_rows * grad_rows
    stepped = master - STEP_SIZE * (first_next / FIRST_CORRECTION) / (
        jnp.sqrt(second_next / SECOND_CORRECTION) + EPSILON
    )
    master_new = jnp.where(learning, stepped, master)
    first_new = jnp.where(learning, first_next, first_state)
    second_new = jnp.where(learning, second_next, second_state)
    return (master_new[None], first_new[None], second_new[None])


def solution(mesh):
    fine = jax.sharding.Mesh(mesh.devices.reshape(4, 2, 8, 2, 2), AXES)
    sec, rep = ("y", "xl"), ("z", "xh", "c")
    rows = P(sec, rep, None)
    in_specs = (rows, rows, rows, P(sec, None, None), P(sec), P(), P(rep, None), P(rep, None))
    return jax.shard_map(shards, mesh=fine, in_specs=in_specs, out_specs=(rows, rows, rows), check_vma=False)
```
